256 devices in a mesh: chan: 8 (over x, y_hi), tm: 32 (over z, y_lo, core).
Axes of the slice: x: 4, y: 4 (y_hi: 2, y_lo: 2; y = y_hi * 2 + y_lo), z: 8, core: 2. Of those that a mesh axis runs over, the one named last changes fastest.
Arguments:
- strain_rate: bfloat16 [4096, 131072], P('chan', 'tm'), may hold values from -1500 to 1500
- whiten_taps: bfloat16 [64], replicated, may hold values from -0.75 to 0.75
- source_channels: int32 [2, 4], replicated, may hold values from 0 to 4095
- window_offsets: int32 [16], replicated, may hold values from 0 to 511
Outputs:
- correlations: float32 [4096, 2, 4, 256], P(('chan', 'tm'))
The draws below stay inside these ranges and needn't reach their ends.
All inputs are finite; a program needn't handle non-finite values.
Results may differ from the reference program's by a relative error of at most 0.0027.
Values may be sent and summed in bfloat16 or wider, within the bound.
No kernel may reach another device: no remote copies, remote signals or barrier semaphores. Data moves between devices by JAX's collectives and lax.ppermute only.
A program may use at most 256 MiB of HBM per device.

```python
import math
import jax
import jax.numpy as jnp
from jax import lax

NC = 4096
TAPS = 64
MAXLAG = 128
LAGS = 256
NSRC = 2
SB = 4
RECORD_LENGTH = 131072
WIN = 8192
NWIN = 16
MAXOFF = 512


def draw_strain_rate(key, part):
    key = jax.random.fold_in(key, 7)
    background_seed, line_seed, transient_seed = jax.random.split(key, 3)
    background_magnitude = jax.random.normal(background_seed, (NC, RECORD_LENGTH), jnp.float32)
    background_magnitude = jnp.clip(background_magnitude, -5.0, 5.0)
    trace_multiplier = jnp.exp(jax.random.uniform(line_seed, (NC, 1), jnp.float32) * math.log(10.0))
    transient_height = jnp.exp(jax.random.uniform(transient_seed, (1, RECORD_LENGTH // 64), jnp.float32) * math.log(10.0))
    transient_height = jnp.repeat(transient_height, 64, axis=1)
    linear_trend_height = jnp.exp(jnp.arange(RECORD_LENGTH, dtype=jnp.float32)[None, :] / RECORD_LENGTH * math.log(3.0))
    return (background_magnitude * trace_multiplier * transient_height * linear_trend_height).astype(jnp.bfloat16)


def touch_ends(entries, own_key, least, top_value):
    spot = [jax.random.randint(jax.random.fold_in(own_key, axis), (), 0, length) for axis, length in enumerate(entries.shape)]
    widest = entries.shape.index(max(entries.shape))
    next_to = spot[:widest] + [(spot[widest] + 1) % entries.shape[widest]] + spot[widest + 1:]
    return entries.at[tuple(spot)].set(least).at[tuple(next_to)].set(top_value)


def gaussian(own_key, dims, deviation, bound, kind=jnp.bfloat16):
    return jnp.clip(deviation * jax.random.normal(own_key, dims, jnp.float32), -bound, bound).astype(kind)


def setup_inputs(seed: int = 0) -> dict:
    key_of = jax.random.split(jax.random.key(seed), 5)
    return {
        "strain_rate": draw_strain_rate(jax.random.fold_in(key_of[4], 71), 0),
        "whiten_taps": gaussian(key_of[1], (TAPS,), TAPS ** -0.5, 0.75),
        "source_channels": touch_ends(jax.random.randint(key_of[2], (NSRC, SB), 0, NC), jax.random.fold_in(key_of[2], 1), 0, NC - 1).astype(jnp.int32),
        "window_offsets": touch_ends(jax.random.randint(key_of[3], (NWIN,), 0, MAXOFF), jax.random.fold_in(key_of[3], 1), 0, MAXOFF - 1).astype(jnp.int32),
    }


epsilon = 1e-05

def whiten_rows(channel_rows, whiten_taps, keep_mask):
    as_float = channel_rows.astype(jnp.float32)[:, None, :]
    reversed_taps = whiten_taps.astype(jnp.float32)[::-1][None, None, :]
    filtered = lax.conv_general_dilated(as_float, reversed_taps, (1,), [(TAPS - 1, 0)], dimension_numbers=('NCH', 'OIH', 'NCH'), precision=lax.Precision.HIGHEST)[:, 0, :]
    energy = lax.optimization_barrier(jnp.sum(filtered * filtered, axis=1))
    inverse_rms = lax.rsqrt(energy / RECORD_LENGTH + epsilon)
    return (filtered * inverse_rms[:, None] * keep_mask[None, :]).astype(jnp.bfloat16)

def reference(strain_rate, whiten_taps, source_channels, window_offsets):
    sample_index = jnp.arange(RECORD_LENGTH, dtype=jnp.int32)
    first_kept = window_offsets[sample_index // WIN]
    keep_mask = jnp.where(sample_index % WIN >= first_kept, 1.0, 0.0).astype(jnp.float32)
    group_rows = min(NC, 256)
    grouped = strain_rate.reshape(NC // group_rows, group_rows, RECORD_LENGTH)
    whitened = lax.map(lambda rows: whiten_rows(rows, whiten_taps, keep_mask), grouped).reshape(NC, RECORD_LENGTH)
    source_traces = whitened[source_channels.reshape(-1)]
    padded = jnp.pad(source_traces, ((0, 0), (MAXLAG, MAXLAG)))
    block_span = min(RECORD_LENGTH, 4096)
    lag_index = jnp.arange(block_span, dtype=jnp.int32)[:, None] + jnp.arange(LAGS, dtype=jnp.int32)[None, :]

    def add_block(turn_index, running):
        first_col = (turn_index * block_span).astype(jnp.int32)
        segment = lax.dynamic_slice_in_dim(padded, first_col, block_span + LAGS, 1)
        table = jnp.concatenate([segment[member][lag_index] for member in range(NSRC * SB)], axis=1).astype(jnp.float32)
        receivers = lax.dynamic_slice_in_dim(whitened, first_col, block_span, 1).astype(jnp.float32)
        return running + jnp.dot(receivers, table, precision=lax.Precision.HIGHEST, preferred_element_type=jnp.float32)
    total = lax.fori_loop(0, RECORD_LENGTH // block_span, add_block, jnp.zeros((NC, NSRC * SB * LAGS), jnp.float32))
    return (total * (1.0 / math.sqrt(RECORD_LENGTH))).reshape(NC, NSRC, SB, LAGS)
```

```python
import math

import jax
import jax.numpy as jnp
from jax import lax
from jax.experimental import pallas as pl
from jax.experimental.pallas import tpu as pltpu
from jax.sharding import PartitionSpec as P

TAPS = 64
MAXLAG = 128
LAGS = 256
NSRC = 2
SB = 4
NS = NSRC * SB
WIN = 8192
LANE = 128
SHIFTS = 16
LEFT = 256
EPS = 1e-05
VMEM_LIMIT = 56 * 1024 * 1024


def params():
    return pltpu.CompilerParams(vmem_limit_bytes=VMEM_LIMIT)


def permute(block, axis, pairs):
    return lax.ppermute(block, axis, pairs)


def fir_tile(taps_ref):
    wide = jnp.broadcast_to(taps_ref[...], (2 * LANE, 2 * LANE))
    rolled = pltpu.roll(wide, LANE, 1, stride=1, stride_axis=0)
    return rolled[:, :LANE].astype(jnp.bfloat16)


def pick_kernel(row_ref, own_ref, x_ref, out_ref, buf, sems):
    copies = []
    for j in range(NS):
        first = pl.multiple_of((row_ref[j] // 16) * 16, 16)
        copy = pltpu.make_async_copy(x_ref.at[pl.ds(first, 16), :], buf.at[j], sems.at[j])
        copy.start()
        copies.append(copy)
    for j in range(NS):
        copies[j].wait()
        inside = jnp.where(own_ref[j] > 0, row_ref[j] % 16, -1)
        rows = lax.broadcasted_iota(jnp.int32, (16, 1), 0)
        picked = jnp.where(rows == inside, buf[j].astype(jnp.float32), 0.0)
        out_ref[pl.ds(j, 1), :] = jnp.sum(picked, axis=0, keepdims=True)


def pick_sources(x, rows, owned):
    samples = x.shape[1]
    return pl.pallas_call(
        pick_kernel,
        out_shape=jax.ShapeDtypeStruct((NS, samples), jnp.float32),
        in_specs=[
            pl.BlockSpec(memory_space=pltpu.SMEM),
            pl.BlockSpec(memory_space=pltpu.SMEM),
            pl.BlockSpec(memory_space=pl.ANY),
        ],
        out_specs=pl.BlockSpec(memory_space=pltpu.VMEM),
        scratch_shapes=[
            pltpu.VMEM((NS, 16, samples), jnp.bfloat16),
            pltpu.SemaphoreType.DMA((NS,)),
        ],
        compiler_params=params(),
        name="pick_sources",
    )(rows, owned, x)


def filter_kernel(core_ref, taps_ref, own_ref, other_ref, halo_ref, out_ref, power_ref, tile):
    @pl.when(pl.program_id(0) == 0)
    def _():
        tile[...] = fir_tile(taps_ref)

    groups, _, sub, half = own_ref.shape
    rows = groups * sub
    own = own_ref[...].reshape(rows, half)
    other = other_ref[...].reshape(rows, half)
    halo = halo_ref[...].reshape(rows, LANE)
    first = core_ref[0] == 0
    matrix = tile[...]

    def run(low, high):
        power = jnp.zeros((rows, LANE), jnp.float32)
        previous = halo
        for part, block in enumerate((low, high)):
            for j in range(half // LANE):
                current = block[:, j * LANE : (j + 1) * LANE]
                framed = jnp.concatenate([previous, current], axis=1)
                value = jnp.dot(framed, matrix, preferred_element_type=jnp.float32)
                start = part * half + j * LANE
                out_ref[:, start : start + LANE] = value
                power = power + value * value
                previous = current
        power_ref[...] = power

    @pl.when(first)
    def _():
        run(own, other)

    @pl.when(jnp.logical_not(first))
    def _():
        run(other, own)


def filter_rows(core, taps, x4, other, halo):
    groups, _, sub, half = x4.shape
    step = 4
    rows = step * sub
    return pl.pallas_call(
        filter_kernel,
        grid_spec=pltpu.PrefetchScalarGridSpec(
            num_scalar_prefetch=1,
            grid=(groups // step,),
            in_specs=[
                pl.BlockSpec((1, 2 * LANE), lambda i, core: (0, 0)),
                pl.BlockSpec((step, 1, sub, half), lambda i, core: (i, core[0], 0, 0)),
                pl.BlockSpec((step, sub, half), lambda i, core: (i, 0, 0)),
                pl.BlockSpec((step, sub, LANE), lambda i, core: (i, 0, 0)),
            ],
            out_specs=[
                pl.BlockSpec((rows, 2 * half), lambda i, core: (i, 0)),
                pl.BlockSpec((rows, LANE), lambda i, core: (i, 0)),
            ],
            scratch_shapes=[pltpu.VMEM((2 * LANE, LANE), jnp.bfloat16)],
        ),
        out_shape=[
            jax.ShapeDtypeStruct((groups * sub, 2 * half), jnp.float32),
            jax.ShapeDtypeStruct((groups * sub, LANE), jnp.float32),
        ],
        compiler_params=params(),
        cost_estimate=pl.CostEstimate(
            flops=2 * groups * sub * 2 * half * 512, bytes_accessed=12 << 20, transcendentals=0
        ),
        name="filter_rows",
    )(core, taps, x4, other, halo)


def source_kernel(core_ref, taps_ref, mine_ref, other_ref, power_ref, out_ref, energy_ref):
    first = core_ref[0] == 0
    mine = mine_ref[...].astype(jnp.float32)
    other = other_ref[...].astype(jnp.float32)
    low = jnp.where(first, mine, other)
    high = jnp.where(first, other, mine)
    count = out_ref.shape[1] // LANE
    width = low.shape[1]
    raw = jnp.concatenate([low, high[:, : (count + 1) * LANE - width]], axis=1)
    blocks = [raw[:, j * LANE : (j + 1) * LANE] for j in range(count + 1)]
    before = jnp.concatenate(blocks[:-1], axis=0)
    after = jnp.concatenate(blocks[1:], axis=0)
    framed = jnp.concatenate([before, after], axis=1).astype(jnp.bfloat16)
    value = jnp.dot(framed, fir_tile(taps_ref), preferred_element_type=jnp.float32)
    total = jnp.zeros((NS, LANE), jnp.float32)
    for j in range(count):
        piece = value[j * NS : (j + 1) * NS, :]
        out_ref[:, j * LANE : (j + 1) * LANE] = piece
        if 1 <= j < count - 1:
            total = total + piece * piece
    rows = power_ref.shape[0]
    lines = []
    for r in range(rows // LANE):
        turned = power_ref[r * LANE : (r + 1) * LANE, :].T
        lines.append(jnp.sum(turned, axis=0, keepdims=True))
    padded = jnp.concatenate([total, jnp.zeros((LANE - NS, LANE), jnp.float32)], axis=0)
    lines.append(jnp.sum(padded.T, axis=0, keepdims=True))
    lines.append(jnp.zeros((8 - len(lines), LANE), jnp.float32))
    energy_ref[...] = jnp.concatenate(lines, axis=0)


def filter_sources(core, taps, mine, other, power, length):
    vmem = pl.BlockSpec(memory_space=pltpu.VMEM)
    return pl.pallas_call(
        source_kernel,
        out_shape=[
            jax.ShapeDtypeStruct((NS, length), jnp.float32),
            jax.ShapeDtypeStruct((8, LANE), jnp.float32),
        ],
        in_specs=[pl.BlockSpec(memory_space=pltpu.SMEM), vmem, vmem, vmem, vmem],
        out_specs=[vmem, vmem],
        compiler_params=params(),
        name="filter_sources",
    )(core, taps, mine, other, power)


def make_correlate_kernel(loads, dots, total_samples, half_groups):
    def kernel(
        place_ref, energy_ref, traces_ref, rows_ref, keep_ref, send_ref, gain, white, table, shifted
    ):
        step = pl.program_id(0)
        chip, line = place_ref[0], place_ref[1]
        before, here, after = place_ref[2], place_ref[3], place_ref[4]
        rows, span = rows_ref.shape
        length = traces_ref.shape[1]

        @pl.when(step == 0)
        def _():
            energy = jnp.sum(energy_ref[...], axis=0)
            scale = lax.rsqrt(energy / total_samples + EPS)
            padded = jnp.concatenate([scale, jnp.zeros((LANE - 8, LANE), jnp.float32)], axis=0)
            turned = padded.T
            for r in range(rows // LANE):
                gain[r * LANE : (r + 1) * LANE, :] = jnp.broadcast_to(
                    turned[:, r : r + 1], (LANE, LANE)
                )
            count = rows // LANE
            source_gain = turned[:NS, count : count + 1]
            place = lax.broadcasted_iota(jnp.int32, (1, length), 1) - MAXLAG
            when = chip * WIN + place
            bound = jnp.where(
                place < 0, before - WIN, jnp.where(place < WIN, here, after + WIN)
            )
            keep = jnp.where(place >= bound, 1.0, 0.0)
            keep = keep * jnp.where(when >= 0, 1.0, 0.0)
            keep = keep * jnp.where(when < total_samples, 1.0, 0.0)
            trace = (traces_ref[...] * source_gain * keep).astype(jnp.bfloat16).astype(jnp.float32)
            for b in range(SHIFTS):
                moved = trace if b == 0 else pltpu.roll(trace, length - b, 1)
                shifted[b * NS : (b + 1) * NS, :] = moved
            for j in range(length // LANE):
                block = shifted[:, j * LANE : (j + 1) * LANE]
                table[j * LANE : (j + 1) * LANE, :] = block.T.astype(jnp.bfloat16)

        @pl.when(step < loads)
        def _():
            start = pl.multiple_of(step * span, span)
            place = lax.broadcasted_iota(jnp.int32, (1, span), 1) + step * span
            keep = jnp.where(place >= here, 1.0, 0.0).astype(jnp.float32)
            factor = gain[...]
            for j in range(span // LANE):
                cols = slice(j * LANE, (j + 1) * LANE)
                value = rows_ref[:, cols] * factor * keep[:, cols]
                white[:, pl.ds(start + j * LANE, LANE)] = value.astype(jnp.bfloat16)

        @pl.when(step >= loads)
        def _():
            pair = step - loads
            offset = pl.multiple_of(pair * (2 * SHIFTS), 2 * SHIFTS)
            depth = white.shape[1]
            left = table[pl.ds(offset, depth), :]
            right = table[pl.ds(offset + SHIFTS, depth), :]
            lags = jnp.concatenate([left, right], axis=1)
            value = jnp.dot(white[...], lags, preferred_element_type=jnp.float32)
            value = value.reshape(half_groups, 2, rows // half_groups // 2, 2 * LANE)
            low, high = value[:, 0], value[:, 1]
            is_low = line == 0
            keep_ref[...] = jnp.where(is_low, low, high)
            send_ref[...] = jnp.where(is_low, high, low).astype(jnp.bfloat16)

    return kernel


def correlate(place, energy, traces, rows, total_samples):
    channels, depth = rows.shape
    loads = 8
    span = depth // loads
    dots = LAGS // (2 * SHIFTS)
    length = traces.shape[1]
    half_groups = 8
    sub = channels // half_groups // 2
    cols = NS * LAGS
    return pl.pallas_call(
        make_correlate_kernel(loads, dots, total_samples, half_groups),
        grid_spec=pltpu.PrefetchScalarGridSpec(
            num_scalar_prefetch=1,
            grid=(loads + dots,),
            in_specs=[
                pl.BlockSpec(energy.shape, lambda i, p: (0, 0, 0)),
                pl.BlockSpec(traces.shape, lambda i, p: (0, 0)),
                pl.BlockSpec((channels, span), lambda i, p: (0, jnp.minimum(i, loads - 1))),
            ],
            out_specs=[
                pl.BlockSpec(
                    (half_groups, sub, 2 * LANE), lambda i, p: (0, 0, jnp.maximum(i - loads, 0))
                ),
                pl.BlockSpec(
                    (half_groups, sub, 2 * LANE), lambda i, p: (0, 0, jnp.maximum(i - loads, 0))
                ),
            ],
            scratch_shapes=[
                pltpu.VMEM((channels, LANE), jnp.float32),
                pltpu.VMEM((channels, depth), jnp.bfloat16),
                pltpu.VMEM((length, LANE), jnp.bfloat16),
                pltpu.VMEM((LANE, length), jnp.float32),
            ],
        ),
        out_shape=[
            jax.ShapeDtypeStruct((half_groups, sub, cols), jnp.float32),
            jax.ShapeDtypeStruct((half_groups, sub, cols), jnp.bfloat16),
        ],
        compiler_params=params(),
        cost_estimate=pl.CostEstimate(
            flops=2 * channels * depth * cols, bytes_accessed=16 << 20, transcendentals=0
        ),
        name="correlate",
    )(place, energy, traces, rows)


def shards(strain_rate, whiten_taps, source_channels, window_offsets):
    channels, samples = strain_rate.shape
    tiles = lax.axis_size("tm")
    groups_chan = lax.axis_size("chan")
    total_samples = samples * tiles
    tile = lax.axis_index("tm")
    core = tile % 2
    chip = tile // 2
    chips = tiles // 2
    line = chip % 2
    sub = channels // tiles

    taps = jnp.zeros((1, 2 * LANE), jnp.float32).at[0, :TAPS].set(whiten_taps.astype(jnp.float32))
    core_arr = core.astype(jnp.int32).reshape(1)

    group_index = lax.axis_index("chan")
    local = source_channels.reshape(-1) - group_index * channels
    owned = ((local >= 0) & (local < channels)).astype(jnp.int32)
    rows = jnp.clip(local, 0, channels - 1)
    picked = pick_sources(strain_rate, rows, owned).astype(jnp.bfloat16)

    x4 = strain_rate.reshape(chips, 2, sub, samples)
    away = lax.dynamic_index_in_dim(x4, 1 - core, axis=1, keepdims=False)
    swap = [(i, i ^ 1) for i in range(tiles)]
    other = permute(away, "tm", swap)
    tail = x4[:, :, :, samples - LANE :]
    to_low = [(2 * k - 1, 2 * k) for k in range(1, chips)]
    to_high = [(2 * k - 1, 2 * k + 1) for k in range(1, chips)]
    halo_low = permute(tail[:, 0], "tm", to_low)
    halo_high = permute(tail[:, 1], "tm", to_high)
    halo = jnp.where(core == 0, halo_low, halo_high)

    up = [(i, i + 1) for i in range(tiles - 1)]
    down = [(i + 1, i) for i in range(tiles - 1)]
    left = permute(picked[:, samples - LEFT :], "tm", up)
    right = permute(picked[:, :LANE], "tm", down)
    pad = jnp.zeros((NS, LEFT - LANE), jnp.bfloat16)
    piece = jnp.where(
        core == 0,
        jnp.concatenate([left, picked], axis=1),
        jnp.concatenate([picked, right, pad], axis=1),
    )
    parts = [
        permute(piece, "chan", [(i, (i + 2 * d) % groups_chan) for i in range(groups_chan)])
        for d in range(1, groups_chan // 2)
    ]
    piece = piece + sum(parts[1:], parts[0])
    piece = piece + permute(piece, "chan", [(i, i ^ 1) for i in range(groups_chan)])
    piece_other = permute(piece, "tm", swap)

    filtered, power = filter_rows(core_arr, taps, x4, other, halo)
    length = WIN + 2 * MAXLAG
    traces, energy = filter_sources(core_arr, taps, piece, piece_other, power, length)

    same = [[2 * k + c for k in range(chips)] for c in range(2)]
    spread = jnp.broadcast_to(energy[None], (chips,) + energy.shape)
    energies = lax.all_to_all(spread, "tm", 0, 0, tiled=True, axis_index_groups=same)

    padded_offsets = jnp.concatenate(
        [jnp.zeros((1,), jnp.int32), window_offsets, jnp.zeros((1,), jnp.int32)]
    )
    place = jnp.concatenate(
        [
            jnp.stack([chip, line]).astype(jnp.int32),
            lax.dynamic_slice_in_dim(padded_offsets, chip, 3),
        ]
    )
    keep, send = correlate(place, energies, traces, filtered, total_samples)

    across = permute(send, "tm", [(i, i ^ 2) for i in range(tiles)])
    summed = (keep + across.astype(jnp.float32)).astype(jnp.bfloat16)
    column = [[4 * z + r for z in range(tiles // 4)] for r in range(4)]
    gathered = lax.all_to_all(summed, "tm", 0, 0, tiled=True, axis_index_groups=column)
    total = jnp.sum(gathered.astype(jnp.float32), axis=0) * (1.0 / math.sqrt(total_samples))
    total = total.reshape(sub, LAGS, NS).transpose(0, 2, 1)
    return total.reshape(sub, NSRC, SB, LAGS)


def solution(mesh):
    return jax.shard_map(
        shards,
        mesh=mesh,
        in_specs=(P("chan", "tm"), P(), P(), P()),
        out_specs=P(("chan", "tm"), None, None, None),
        check_vma=False,
    )
```

```python
import math

import jax
import jax.numpy as jnp
from jax import lax
from jax.experimental import pallas as pl
from jax.experimental.pallas import tpu as pltpu
from jax.sharding import PartitionSpec as P

TAPS = 64
MAXLAG = 128
LAGS = 256
NSRC = 2
SB = 4
NS = NSRC * SB
WIN = 8192
LANE = 128
SHIFTS = 16
LEFT = 256
EPS = 1e-05
MIB = 1024 * 1024

VMEM = pl.BlockSpec(memory_space=pltpu.VMEM)
SMEM = pl.BlockSpec(memory_space=pltpu.SMEM)
ANY = pl.BlockSpec(memory_space=pl.ANY)


def call(kernel, name, out, in_specs, scratch=(), limit=16, flops=0, moved=0):
    return pl.pallas_call(
        kernel,
        out_shape=out,
        in_specs=in_specs,
        out_specs=[VMEM] * len(out),
        scratch_shapes=list(scratch),
        compiler_params=pltpu.CompilerParams(vmem_limit_bytes=limit * MIB),
        cost_estimate=pl.CostEstimate(flops=flops, bytes_accessed=moved, transcendentals=0),
        name=name,
    )


def shape(dims, dtype):
    return jax.ShapeDtypeStruct(dims, dtype)


def fir_tile(taps):
    wide = jnp.broadcast_to(taps.astype(jnp.float32), (2 * LANE, 2 * LANE))
    rolled = pltpu.roll(wide, LANE, 1, stride=1, stride_axis=0)
    return rolled[:, :LANE].astype(jnp.bfloat16)


def wide_taps(taps):
    return jnp.pad(taps, (0, 2 * LANE - TAPS)).reshape(1, 2 * LANE)


def pick_sources(source_channels, x4):
    groups, _, sub, samples = x4.shape
    channels = groups * 2 * sub

    def kernel(ids_ref, x_ref, own_ref, edge_ref, high_ref, buf, sems):
        base = lax.axis_index("chan") * channels
        core = lax.axis_index("tm") % 2
        copies = []
        inner = []
        for j in range(NS):
            local = ids_ref[j // SB, j % SB] - base
            owned = (local >= 0) & (local < channels)
            row = jnp.clip(local, 0, channels - 1)
            group, half = row // (2 * sub), (row // sub) % 2
            inner.append(jnp.where(owned, row % sub, -1))
            copies.append(pltpu.make_async_copy(x_ref.at[group, half], buf.at[j], sems.at[j]))
        for copy in copies:
            copy.start()
        last = pl.ds(samples - LANE, LANE)
        low = pltpu.make_async_copy(
            x_ref.at[:, 0, :, last], edge_ref.at[pl.ds(0, groups)], sems.at[NS]
        )
        high = pltpu.make_async_copy(x_ref.at[:, 1, :, last], high_ref, sems.at[NS + 1])
        low.start()
        high.start()
        rows = lax.broadcasted_iota(jnp.int32, (sub, 1), 0)
        lines = []
        for j in range(NS):
            copies[j].wait()
            hit = jnp.where(rows == inner[j], 1.0, 0.0)
            lines.append(jnp.sum(buf[j].astype(jnp.float32) * hit, axis=0, keepdims=True))
        own = jnp.concatenate(lines, axis=0)
        own_ref[...] = own.astype(jnp.bfloat16)
        tail = jnp.concatenate(
            [own[:, samples - LEFT : samples - LANE], own[:, samples - LANE :]], axis=0
        )
        head = jnp.concatenate([own[:, :LANE], own[:, LANE : 2 * LANE]], axis=0)
        low.wait()
        high.wait()
        edge_ref[groups] = jnp.where(core == 1, tail, head).astype(jnp.bfloat16)

    return call(
        kernel,
        "pick_sources",
        [
            shape((NS, samples), jnp.bfloat16),
            shape((groups + 1, sub, LANE), jnp.bfloat16),
            shape((groups, sub, LANE), jnp.bfloat16),
        ],
        [SMEM, ANY],
        [pltpu.VMEM((NS, sub, samples), jnp.bfloat16), pltpu.SemaphoreType.DMA((NS + 2,))],
        limit=61,
        moved=2 * MIB,
    )(source_channels, x4)


def filter_rows(offsets, taps, x4, other, edge, high):
    groups, _, sub, half = x4.shape
    rows = groups * sub

    def kernel(off_ref, taps_ref, x_ref, other_ref, edge_ref, high_ref, out_ref, power_ref, own, sem):
        tile = lax.axis_index("tm")
        core = tile % 2
        copy = pltpu.make_async_copy(x_ref.at[:, core], own, sem)
        copy.start()
        matrix = fir_tile(taps_ref[...])
        first_kept = off_ref[tile // 2]
        copy.wait()

        def run(low, high_half, halo):
            power = jnp.zeros((rows, LANE), jnp.float32)
            previous = halo
            for part, block in enumerate((low, high_half)):
                for j in range(half // LANE):
                    current = block[:, :, j * LANE : (j + 1) * LANE].reshape(rows, LANE)
                    framed = jnp.concatenate([previous, current], axis=1)
                    value = jnp.dot(framed, matrix, preferred_element_type=jnp.float32)
                    start = part * half + j * LANE
                    power = power + value * value
                    place = lax.broadcasted_iota(jnp.int32, (1, LANE), 1) + start
                    value = value * jnp.where(place >= first_kept, 1.0, 0.0)
                    out_ref[:, start : start + LANE] = value
                    previous = current
            power_ref[...] = power

        @pl.when(core == 0)
        def _():
            run(own, other_ref, edge_ref[:groups].reshape(rows, LANE))

        @pl.when(core == 1)
        def _():
            run(other_ref, own, high_ref[...].reshape(rows, LANE))

    return call(
        kernel,
        "filter_rows",
        [shape((rows, 2 * half), jnp.float32), shape((rows, LANE), jnp.float32)],
        [SMEM, VMEM, ANY, VMEM, VMEM, VMEM],
        [pltpu.VMEM((groups, sub, half), jnp.bfloat16), pltpu.SemaphoreType.DMA],
        flops=2 * rows * 2 * half * 512,
        moved=12 * MIB,
    )(offsets, taps, x4, other, edge, high)


def filter_sources(offsets, taps, mine, other, power, chips, total_samples):
    length = WIN + 2 * MAXLAG
    count = length // LANE
    half = mine.shape[1] - LEFT

    def kernel(off_ref, taps_ref, mine_ref, other_ref, power_ref, out_ref, energy_ref):
        tile = lax.axis_index("tm")
        core, chip = tile % 2, tile // 2
        mine_rows = mine_ref[...].astype(jnp.float32)
        other_rows = other_ref[...].astype(jnp.float32)
        low = jnp.where(core == 0, mine_rows, other_rows)
        high = jnp.where(core == 0, other_rows, mine_rows)
        raw = [low[:, half:], low[:, :half], high[:, :half], high[:, half : half + LANE]]
        raw = jnp.concatenate(raw, axis=1)
        blocks = [raw[:, j * LANE : (j + 1) * LANE] for j in range(count + 1)]
        before = jnp.concatenate(blocks[:-1], axis=0)
        after = jnp.concatenate(blocks[1:], axis=0)
        framed = jnp.concatenate([before, after], axis=1).astype(jnp.bfloat16)
        value = jnp.dot(framed, fir_tile(taps_ref[...]), preferred_element_type=jnp.float32)
        total = jnp.zeros((NS, LANE), jnp.float32)
        first_kept = [
            off_ref[jnp.maximum(chip - 1, 0)],
            off_ref[chip],
            off_ref[jnp.minimum(chip + 1, chips - 1)],
        ]
        for j in range(count):
            piece = value[j * NS : (j + 1) * NS, :]
            start = j * LANE - MAXLAG
            window = start // WIN
            if window == 0:
                total = total + piece * piece
            place = lax.broadcasted_iota(jnp.int32, (1, LANE), 1) + (start - window * WIN)
            keep = jnp.where(place >= first_kept[window + 1], 1.0, 0.0)
            if window < 0:
                keep = keep * jnp.where(chip > 0, 1.0, 0.0)
            if window > 0:
                keep = keep * jnp.where(chip < chips - 1, 1.0, 0.0)
            out_ref[:, j * LANE : (j + 1) * LANE] = piece * keep
        lines = []
        for r in range(power_ref.shape[0] // LANE):
            turned = power_ref[r * LANE : (r + 1) * LANE, :].T
            lines.append(jnp.sum(turned, axis=0, keepdims=True))
        repeated = jnp.concatenate([total] * SHIFTS, axis=0)
        lines.append(jnp.sum(repeated.T, axis=0, keepdims=True))
        lines.append(jnp.zeros((8 - len(lines), LANE), jnp.float32))
        energy = jnp.concatenate(lines, axis=0)
        energy_ref[...] = jnp.broadcast_to(energy[None], energy_ref.shape)

    return call(
        kernel,
        "filter_sources",
        [shape((NS, length), jnp.float32), shape((chips, 8, LANE), jnp.float32)],
        [SMEM, VMEM, VMEM, VMEM, VMEM],
        moved=MIB,
    )(offsets, taps, mine, other, power)


def shift_sources(traces):
    length = traces.shape[1]

    def kernel(traces_ref, table_ref, shifted):
        trace = traces_ref[...]
        for b in range(SHIFTS):
            moved = trace if b == 0 else pltpu.roll(trace, length - b, 1)
            shifted[b * NS : (b + 1) * NS, :] = moved
        for j in range(length // LANE):
            cols = slice(j * LANE, (j + 1) * LANE)
            table_ref[cols, :] = shifted[:, cols].T

    return call(
        kernel,
        "shift_sources",
        [shape((length, LANE), jnp.float32)],
        [VMEM],
        [pltpu.VMEM((LANE, length), jnp.float32)],
        moved=8 * MIB,
    )(traces)[0]


def lag_products(white, table_ref, pairs, keep_ref, send_ref, half_groups):
    rows, depth = white.shape
    sub = rows // half_groups // 2
    own_low = (lax.axis_index("tm") // 2) % 2 == 0
    for place, pair in enumerate(pairs):
        offset = pair * 2 * SHIFTS
        left = table_ref[offset : offset + depth, :]
        right = table_ref[offset + SHIFTS : offset + SHIFTS + depth, :]
        lags = jnp.concatenate([left, right], axis=1)
        value = jnp.dot(white[...], lags, preferred_element_type=jnp.float32)
        value = value.reshape(half_groups, 2, sub, 2 * LANE)
        low, high = value[:, 0], value[:, 1]
        cols = slice(place * 2 * LANE, (place + 1) * 2 * LANE)
        keep_ref[:, :, cols] = jnp.where(own_low, low, high)
        send_ref[:, :, cols] = jnp.where(own_low, high, low).astype(jnp.bfloat16)


def correlate_first(energies, traces, rows, pairs, half_groups, total_samples):
    channels, depth = rows.shape
    length = traces.shape[0]

    def kernel(energy_ref, traces_ref, rows_ref, keep_ref, send_ref, white, table):
        energy = jnp.sum(energy_ref[...], axis=0)
        scale = lax.rsqrt(energy / total_samples + EPS)
        padded = jnp.concatenate([scale, jnp.zeros((LANE - 8, LANE), jnp.float32)], axis=0)
        turned = padded.T
        parts = channels // LANE
        columns = [turned[:, r : r + 1] for r in range(parts)]
        gain = jnp.concatenate(columns, axis=0)
        table[...] = (traces_ref[...] * scale[parts : parts + 1, :]).astype(jnp.bfloat16)
        white[...] = (rows_ref[...] * gain).astype(jnp.bfloat16)
        lag_products(white, table, pairs, keep_ref, send_ref, half_groups)

    sub = channels // half_groups // 2
    cols = len(pairs) * 2 * LANE
    return call(
        kernel,
        "correlate_first",
        [
            shape((half_groups, sub, cols), jnp.float32),
            shape((half_groups, sub, cols), jnp.bfloat16),
            shape((channels, depth), jnp.bfloat16),
            shape((length, LANE), jnp.bfloat16),
        ],
        [VMEM, VMEM, VMEM],
        flops=2 * channels * depth * cols,
        moved=16 * MIB,
    )(energies, traces, rows)


def correlate_next(white, table, pairs, half_groups):
    channels, depth = white.shape

    def kernel(white_ref, table_ref, keep_ref, send_ref):
        lag_products(white_ref, table_ref, pairs, keep_ref, send_ref, half_groups)

    sub = channels // half_groups // 2
    cols = len(pairs) * 2 * LANE
    return call(
        kernel,
        "correlate_next",
        [
            shape((half_groups, sub, cols), jnp.float32),
            shape((half_groups, sub, cols), jnp.bfloat16),
        ],
        [VMEM, VMEM],
        flops=2 * channels * depth * cols,
        moved=8 * MIB,
    )(white, table)


def shards(strain_rate, whiten_taps, source_channels, window_offsets):
    channels, samples = strain_rate.shape
    tiles = lax.axis_size("tm")
    groups_chan = lax.axis_size("chan")
    total_samples = samples * tiles
    chips = tiles // 2
    sub = channels // tiles
    core = lax.axis_index("tm") % 2
    taps = wide_taps(whiten_taps)

    x4 = strain_rate.reshape(chips, 2, sub, samples)
    own, edge, high = pick_sources(source_channels, x4)
    core, own = lax.optimization_barrier((core, own))

    swap = [(i, i ^ 1) for i in range(tiles)]
    across_edge = [(2 * k - 1, 2 * k) for k in range(1, chips)]
    across_edge = across_edge + [(b, a) for a, b in across_edge]
    edge = lax.ppermute(edge, "tm", across_edge)
    away = lax.dynamic_index_in_dim(x4, 1 - core, axis=1, keepdims=False)
    other = lax.ppermute(away, "tm", swap)
    high = lax.ppermute(high, "tm", [(2 * k - 1, 2 * k + 1) for k in range(1, chips)])

    piece = jnp.concatenate([own, edge[chips, :NS], edge[chips, NS:]], axis=1)
    parts = [
        lax.ppermute(piece, "chan", [(i, (i + 2 * d) % groups_chan) for i in range(groups_chan)])
        for d in range(1, groups_chan // 2)
    ]
    filtered, power = filter_rows(window_offsets, taps, x4, other, edge, high)
    *parts, power = lax.optimization_barrier((*parts, power))
    piece = piece + sum(parts[1:], parts[0])
    piece = piece + lax.ppermute(piece, "chan", [(i, i ^ 1) for i in range(groups_chan)])
    piece_other = lax.ppermute(piece, "tm", swap)

    traces, energy = filter_sources(
        window_offsets, taps, piece, piece_other, power, chips, total_samples
    )
    same = [[2 * k + c for k in range(chips)] for c in range(2)]
    energies = lax.all_to_all(energy, "tm", 0, 0, tiled=True, axis_index_groups=same)
    shifted = shift_sources(traces)

    column_size = tiles // 4
    column = [[4 * z + r for z in range(column_size)] for r in range(4)]
    dots = LAGS // (2 * SHIFTS)
    first, second = range(dots // 2), range(dots // 2, dots)
    keep_a, send_a, white, table = correlate_first(
        energies, shifted, filtered, first, column_size, total_samples
    )
    line = [(i, i ^ 2) for i in range(tiles)]

    def over_column(keep, across):
        summed = (keep + across.astype(jnp.float32)).astype(jnp.bfloat16)
        return lax.all_to_all(summed, "tm", 0, 0, tiled=True, axis_index_groups=column)

    across_a = lax.ppermute(send_a, "tm", line)
    keep_b, send_b = correlate_next(white, table, second, column_size)
    across_b = lax.ppermute(send_b, "tm", line)
    parts_a = over_column(keep_a, across_a)
    parts_b = over_column(keep_b, across_b)
    total = jnp.concatenate(
        [jnp.sum(p.astype(jnp.float32), axis=0) for p in (parts_a, parts_b)], axis=1
    )
    total = total * (1.0 / math.sqrt(total_samples))
    total = total.reshape(sub, LAGS, NS).transpose(0, 2, 1)
    return total.reshape(sub, NSRC, SB, LAGS)


def solution(mesh):
    return jax.shard_map(
        shards,
        mesh=mesh,
        in_specs=(P("chan", "tm"), P(), P(), P()),
        out_specs=P(("chan", "tm"), None, None, None),
        check_vma=False,
    )
```

```python
import math

import jax
import jax.numpy as jnp
from jax import lax
from jax.experimental import pallas as pl
from jax.experimental.pallas import tpu as pltpu
from jax.sharding import PartitionSpec as P

TAPS = 64
MAXLAG = 128
LAGS = 256
NSRC = 2
SB = 4
NS = NSRC * SB
WIN = 8192
LANE = 128
SHIFTS = 16
LEFT = 256
EPS = 1e-05
MIB = 1024 * 1024

VMEM = pl.BlockSpec(memory_space=pltpu.VMEM)
SMEM = pl.BlockSpec(memory_space=pltpu.SMEM)
ANY = pl.BlockSpec(memory_space=pl.ANY)


def call(kernel, name, out, in_specs, scratch=(), out_specs=None, limit=16, flops=0, moved=0):
    return pl.pallas_call(
        kernel,
        out_shape=out,
        in_specs=in_specs,
        out_specs=out_specs or [VMEM] * len(out),
        scratch_shapes=list(scratch),
        compiler_params=pltpu.CompilerParams(vmem_limit_bytes=limit * MIB),
        cost_estimate=pl.CostEstimate(flops=flops, bytes_accessed=moved, transcendentals=0),
        name=name,
    )


def shape(dims, dtype):
    return jax.ShapeDtypeStruct(dims, dtype)


def fir_tile(taps):
    wide = jnp.broadcast_to(taps.astype(jnp.float32), (2 * LANE, 2 * LANE))
    rolled = pltpu.roll(wide, LANE, 1, stride=1, stride_axis=0)
    return rolled[:, :LANE].astype(jnp.bfloat16)


def wide_taps(taps):
    return jnp.pad(taps, (0, 2 * LANE - TAPS)).reshape(1, 2 * LANE)


def pick_sources(source_channels, x4):
    groups, _, sub, samples = x4.shape
    channels = groups * 2 * sub

    def kernel(ids_ref, x_ref, own_ref, low_ref, high_ref, away_ref, buf, sems):
        base = lax.axis_index("chan") * channels
        core = lax.axis_index("tm") % 2
        copies = []
        inner = []
        for j in range(NS):
            local = ids_ref[j // SB, j % SB] - base
            owned = (local >= 0) & (local < channels)
            row = jnp.clip(local, 0, channels - 1)
            group, half = row // (2 * sub), (row // sub) % 2
            inner.append(jnp.where(owned, row % sub, -1))
            copies.append(pltpu.make_async_copy(x_ref.at[group, half], buf.at[j], sems.at[j]))
        last = pl.ds(samples - LANE, LANE)
        rest = [
            pltpu.make_async_copy(x_ref.at[:, 0, :, last], low_ref, sems.at[NS]),
            pltpu.make_async_copy(x_ref.at[:, 1, :, last], high_ref, sems.at[NS + 1]),
            pltpu.make_async_copy(x_ref.at[:, 1 - core], away_ref, sems.at[NS + 2]),
        ]
        for copy in copies + rest:
            copy.start()
        rows = lax.broadcasted_iota(jnp.int32, (sub, 1), 0)
        own = jnp.zeros((NS, samples), jnp.float32)
        for j in range(NS):
            copies[j].wait()
            picked = buf[j].astype(jnp.float32) * jnp.where(rows == inner[j], 1.0, 0.0)
            picked = picked[:NS] + picked[NS:]
            own = own + pltpu.roll(picked, (j + NS - inner[j] % NS) % NS, 0)
        own_ref[...] = own.astype(jnp.bfloat16)
        for copy in rest:
            copy.wait()

    edge = shape((groups, sub, LANE), jnp.bfloat16)
    return call(
        kernel,
        "pick_sources",
        [
            shape((NS, samples), jnp.bfloat16),
            edge,
            edge,
            shape((groups, sub, samples), jnp.bfloat16),
        ],
        [SMEM, ANY],
        [pltpu.VMEM((NS, sub, samples), jnp.bfloat16), pltpu.SemaphoreType.DMA((NS + 3,))],
        out_specs=[VMEM, VMEM, VMEM, ANY],
        limit=61,
        moved=4 * MIB,
    )(source_channels, x4)


def join_sources(piece, arrived):
    samples = piece.shape[1]

    def kernel(piece_ref, arrived_ref, out_ref, end_ref):
        core = lax.axis_index("tm") % 2
        total = piece_ref[...].astype(jnp.float32) + arrived_ref[...].astype(jnp.float32)
        out_ref[...] = total.astype(jnp.bfloat16)
        end = jnp.where(core == 1, total[:, samples - LEFT :], total[:, :LEFT])
        end_ref[...] = end.astype(jnp.bfloat16)

    return call(
        kernel,
        "join_sources",
        [shape(piece.shape, jnp.bfloat16), shape((NS, LEFT), jnp.bfloat16)],
        [VMEM, VMEM],
    )(piece, arrived)


def filter_rows(offsets, taps, x4, other, low_edge, high_edge):
    groups, _, sub, half = x4.shape
    rows = groups * sub
    chunk = 1024
    parts = half // chunk
    total = 2 * parts

    def kernel(
        off_ref, taps_ref, x_ref, other_ref, low_ref, high_ref, out_ref, power_ref,
        raw, value_buf, in_sems, out_sems
    ):
        tile = lax.axis_index("tm")
        core = tile % 2

        def fetch(part, source, index):
            cols = pl.ds(index * chunk, chunk)
            return pltpu.make_async_copy(source.at[:, :, cols], raw.at[part], in_sems.at[part])

        own = x_ref.at[:, core]

        @pl.when(core == 0)
        def _():
            for p in range(parts):
                fetch(p, own, p).start()
            for p in range(parts):
                fetch(parts + p, other_ref, p).start()

        @pl.when(core == 1)
        def _():
            for p in range(parts):
                fetch(p, other_ref, p).start()
            for p in range(parts):
                fetch(parts + p, own, p).start()

        matrix = fir_tile(taps_ref[...])
        first_kept = off_ref[tile // 2]
        previous = jnp.where(core == 0, low_ref[...], high_ref[...]).reshape(rows, LANE)
        power = jnp.zeros((rows, LANE), jnp.float32)
        stores = []
        for part in range(total):
            fetch(part, own, 0).wait()
            for j in range(chunk // LANE):
                current = raw[part, :, :, j * LANE : (j + 1) * LANE].reshape(rows, LANE)
                framed = jnp.concatenate([previous, current], axis=1)
                value = jnp.dot(framed, matrix, preferred_element_type=jnp.float32)
                power = power + value * value
                start = part * chunk + j * LANE
                if start < WIN:
                    place = lax.broadcasted_iota(jnp.int32, (1, LANE), 1) + start
                    value = value * jnp.where(place >= first_kept, 1.0, 0.0)
                value_buf[part, :, j * LANE : (j + 1) * LANE] = value
                previous = current
            store = pltpu.make_async_copy(
                value_buf.at[part],
                out_ref.at[:, pl.ds(part * chunk, chunk)],
                out_sems.at[part],
            )
            store.start()
            stores.append(store)
        power_ref[...] = power
        for store in stores:
            store.wait()

    return call(
        kernel,
        "filter_rows",
        [shape((rows, 2 * half), jnp.float32), shape((rows, LANE), jnp.float32)],
        [SMEM, VMEM, ANY, ANY, VMEM, VMEM],
        [
            pltpu.VMEM((total, groups, sub, chunk), jnp.bfloat16),
            pltpu.VMEM((total, rows, chunk), jnp.float32),
            pltpu.SemaphoreType.DMA((total,)),
            pltpu.SemaphoreType.DMA((total,)),
        ],
        out_specs=[ANY, VMEM],
        limit=40,
        flops=2 * rows * 2 * half * 512,
        moved=12 * MIB,
    )(offsets, taps, x4, other, low_edge, high_edge)


def filter_sources(offsets, taps, mine, other, edge, cross, power, chips):
    length = WIN + 2 * MAXLAG
    count = length // LANE

    def kernel(
        off_ref, taps_ref, mine_ref, other_ref, edge_ref, cross_ref, power_ref, out_ref, energy_ref
    ):
        tile = lax.axis_index("tm")
        core, chip = tile % 2, tile // 2
        mine_rows = mine_ref[...].astype(jnp.float32)
        other_rows = other_ref[...].astype(jnp.float32)
        low = jnp.where(core == 0, mine_rows, other_rows)
        high = jnp.where(core == 0, other_rows, mine_rows)
        edge_rows = edge_ref[...].astype(jnp.float32)
        cross_rows = cross_ref[...].astype(jnp.float32)
        left = jnp.where(core == 0, edge_rows, cross_rows)
        right = jnp.where(core == 0, cross_rows, edge_rows)
        raw = jnp.concatenate([left, low, high, right[:, :LANE]], axis=1)
        blocks = [raw[:, j * LANE : (j + 1) * LANE] for j in range(count + 1)]
        before = jnp.concatenate(blocks[:-1], axis=0)
        after = jnp.concatenate(blocks[1:], axis=0)
        framed = jnp.concatenate([before, after], axis=1).astype(jnp.bfloat16)
        value = jnp.dot(framed, fir_tile(taps_ref[...]), preferred_element_type=jnp.float32)
        total = jnp.zeros((NS, LANE), jnp.float32)
        first_kept = [
            off_ref[jnp.maximum(chip - 1, 0)],
            off_ref[chip],
            off_ref[jnp.minimum(chip + 1, chips - 1)],
        ]
        for j in range(count):
            piece = value[j * NS : (j + 1) * NS, :]
            start = j * LANE - MAXLAG
            window = start // WIN
            if window == 0:
                total = total + piece * piece
            place = lax.broadcasted_iota(jnp.int32, (1, LANE), 1) + (start - window * WIN)
            keep = jnp.where(place >= first_kept[window + 1], 1.0, 0.0)
            if window < 0:
                keep = keep * jnp.where(chip > 0, 1.0, 0.0)
            if window > 0:
                keep = keep * jnp.where(chip < chips - 1, 1.0, 0.0)
            out_ref[:, j * LANE : (j + 1) * LANE] = piece * keep
        lines = []
        for r in range(power_ref.shape[0] // LANE):
            turned = power_ref[r * LANE : (r + 1) * LANE, :].T
            lines.append(jnp.sum(turned, axis=0, keepdims=True))
        repeated = jnp.concatenate([total] * SHIFTS, axis=0)
        lines.append(jnp.sum(repeated.T, axis=0, keepdims=True))
        lines.append(jnp.zeros((8 - len(lines), LANE), jnp.float32))
        energy = jnp.concatenate(lines, axis=0)
        energy_ref[...] = jnp.broadcast_to(energy[None], energy_ref.shape)

    return call(
        kernel,
        "filter_sources",
        [shape((NS, length), jnp.float32), shape((chips, 8, LANE), jnp.float32)],
        [SMEM, VMEM, VMEM, VMEM, VMEM, VMEM, VMEM],
        moved=MIB,
    )(offsets, taps, mine, other, edge, cross, power)


def lag_products(white, table_ref, pairs, keep_ref, send_ref, half_groups):
    rows, depth = white.shape
    sub = rows // half_groups // 2
    own_low = (lax.axis_index("tm") // 2) % 2 == 0
    for place, pair in enumerate(pairs):
        offset = pair * 2 * SHIFTS
        left = table_ref[offset : offset + depth, :]
        right = table_ref[offset + SHIFTS : offset + SHIFTS + depth, :]
        lags = jnp.concatenate([left, right], axis=1)
        value = jnp.dot(white[...], lags, preferred_element_type=jnp.float32)
        value = value.reshape(half_groups, 2, sub, 2 * LANE)
        low, high = value[:, 0], value[:, 1]
        cols = slice(place * 2 * LANE, (place + 1) * 2 * LANE)
        keep_ref[:, :, cols] = jnp.where(own_low, low, high)
        send_ref[:, :, cols] = jnp.where(own_low, high, low).astype(jnp.bfloat16)


def correlate_first(energies, traces, rows, pairs, half_groups, total_samples):
    channels, depth = rows.shape
    length = traces.shape[1]
    chunk = 1024
    loads = depth // chunk

    def kernel(
        energy_ref, traces_ref, rows_ref, keep_ref, send_ref, white, table, buf, shifted, sems
    ):
        copies = []
        for i in range(loads):
            cols = pl.ds(i * chunk, chunk)
            copies.append(pltpu.make_async_copy(rows_ref.at[:, cols], buf.at[i], sems.at[i]))
        for copy in copies:
            copy.start()
        energy = jnp.sum(energy_ref[...], axis=0)
        scale = lax.rsqrt(energy / total_samples + EPS)
        padded = jnp.concatenate([scale, jnp.zeros((LANE - 8, LANE), jnp.float32)], axis=0)
        turned = padded.T
        parts = channels // LANE
        gain = jnp.concatenate([turned[:, r : r + 1] for r in range(parts)], axis=0)
        trace = traces_ref[...] * turned[:NS, parts : parts + 1]
        trace = trace.astype(jnp.bfloat16).astype(jnp.float32)
        for b in range(SHIFTS):
            moved = trace if b == 0 else pltpu.roll(trace, length - b, 1)
            shifted[b * NS : (b + 1) * NS, :] = moved
        for j in range(length // LANE):
            cols = slice(j * LANE, (j + 1) * LANE)
            table[cols, :] = shifted[:, cols].T.astype(jnp.bfloat16)
        for i in range(loads):
            copies[i].wait()
            white[:, i * chunk : (i + 1) * chunk] = (buf[i] * gain).astype(jnp.bfloat16)
        lag_products(white, table, pairs, keep_ref, send_ref, half_groups)

    sub = channels // half_groups // 2
    cols = len(pairs) * 2 * LANE
    return call(
        kernel,
        "correlate_first",
        [
            shape((half_groups, sub, cols), jnp.float32),
            shape((half_groups, sub, cols), jnp.bfloat16),
            shape((channels, depth), jnp.bfloat16),
            shape((length, LANE), jnp.bfloat16),
        ],
        [VMEM, VMEM, ANY],
        [
            pltpu.VMEM((loads, channels, chunk), jnp.float32),
            pltpu.VMEM((LANE, length), jnp.float32),
            pltpu.SemaphoreType.DMA((loads,)),
        ],
        limit=40,
        flops=2 * channels * depth * cols,
        moved=16 * MIB,
    )(energies, traces, rows)


def correlate_next(white, table, pairs, half_groups):
    channels, depth = white.shape

    def kernel(white_ref, table_ref, keep_ref, send_ref):
        lag_products(white_ref, table_ref, pairs, keep_ref, send_ref, half_groups)

    sub = channels // half_groups // 2
    cols = len(pairs) * 2 * LANE
    return call(
        kernel,
        "correlate_next",
        [
            shape((half_groups, sub, cols), jnp.float32),
            shape((half_groups, sub, cols), jnp.bfloat16),
        ],
        [VMEM, VMEM],
        flops=2 * channels * depth * cols,
        moved=8 * MIB,
    )(white, table)


def add_line(keep, across):
    groups, sub, cols = keep.shape

    def kernel(keep_ref, across_ref, own_ref, *out_refs):
        place = lax.axis_index("tm") // 4
        for d in range(groups):
            index = lax.rem(place + d, groups)
            value = keep_ref[index] + across_ref[index].astype(jnp.float32)
            if d == 0:
                own_ref[...] = value
            else:
                out_refs[d - 1][...] = value.astype(jnp.bfloat16)

    return call(
        kernel,
        "add_line",
        [shape((sub, cols), jnp.float32)]
        + [shape((sub, cols), jnp.bfloat16)] * (groups - 1),
        [VMEM, VMEM],
        moved=MIB,
    )(keep, across)


def finish(halves, factor):
    count = len(halves[0])
    sub, cols = halves[0][0].shape
    blocks = cols // LANE

    def kernel(*refs):
        out_ref, turned = refs[-2], refs[-1]
        blank = jnp.zeros((LANE - sub, LANE), jnp.float32)
        for h in range(len(halves)):
            part = refs[h * count : (h + 1) * count]
            value = part[0][...]
            for ref in part[1:]:
                value = value + ref[...].astype(jnp.float32)
            value = value * factor
            for j in range(blocks):
                block = jnp.concatenate([value[:, j * LANE : (j + 1) * LANE], blank], axis=0)
                start = (h * blocks + j) * LANE
                turned[start : start + LANE, :] = block.T
        for m in range(NS):
            for j in range(LAGS // LANE):
                block = turned[pl.ds(j * LANE * NS + m, LANE, stride=NS), :]
                out_ref[:, m, j * LANE : (j + 1) * LANE] = block.T[:sub]

    return call(
        kernel,
        "finish",
        [shape((sub, NS, LAGS), jnp.float32)],
        [VMEM] * (count * len(halves)),
        [pltpu.VMEM((NS * LAGS, LANE), jnp.float32)],
        moved=MIB,
    )(*[part for half in halves for part in half])[0]


def shards(strain_rate, whiten_taps, source_channels, window_offsets):
    channels, samples = strain_rate.shape
    tiles = lax.axis_size("tm")
    groups_chan = lax.axis_size("chan")
    total_samples = samples * tiles
    chips = tiles // 2
    sub = channels // tiles
    taps = wide_taps(whiten_taps)

    x4 = strain_rate.reshape(chips, 2, sub, samples)
    piece, low_edge, high_edge, away = pick_sources(source_channels, x4)

    swap = [(i, i ^ 1) for i in range(tiles)]
    to_next = [(2 * k - 1, 2 * k) for k in range(1, chips)]
    skip_next = [(2 * k - 1, 2 * k + 1) for k in range(1, chips)]
    both_next = to_next + [(b, a) for a, b in to_next]
    both_skip = skip_next + [(2 * k, 2 * k - 2) for k in range(1, chips)]

    parts = [
        lax.ppermute(piece, "chan", [(i, (i + 2 * d) % groups_chan) for i in range(groups_chan)])
        for d in range(1, groups_chan // 2)
    ]
    other = lax.ppermute(away, "tm", swap)
    piece = piece + sum(parts[1:], parts[0])
    arrived = lax.ppermute(piece, "chan", [(i, i ^ 1) for i in range(groups_chan)])
    low_edge = lax.ppermute(low_edge, "tm", to_next)
    high_edge = lax.ppermute(high_edge, "tm", skip_next)
    piece, end = join_sources(piece, arrived)
    piece_other = lax.ppermute(piece, "tm", swap)
    edge = lax.ppermute(end, "tm", both_next)
    cross = lax.ppermute(end, "tm", both_skip)
    filtered, power = filter_rows(window_offsets, taps, x4, other, low_edge, high_edge)
    piece_other, edge, cross, power = lax.optimization_barrier((piece_other, edge, cross, power))
    traces, energy = filter_sources(
        window_offsets, taps, piece, piece_other, edge, cross, power, chips
    )
    same = [[2 * k + c for k in range(chips)] for c in range(2)]
    energies = lax.all_to_all(energy, "tm", 0, 0, tiled=True, axis_index_groups=same)

    column = tiles // 4
    dots = LAGS // (2 * SHIFTS)
    first, second = range(dots // 2), range(dots // 2, dots)
    keep_a, send_a, white, table = correlate_first(
        energies, traces, filtered, first, column, total_samples
    )
    line = [(i, i ^ 2) for i in range(tiles)]

    def over_column(keep, across):
        own, *sends = add_line(keep, across)
        far_first = sorted(range(1, column), key=lambda d: -min(d, column - d))
        arrived = [
            lax.ppermute(sends[d - 1], "tm", [(i, (i + 4 * d) % tiles) for i in range(tiles)])
            for d in far_first
        ]
        return [own] + arrived

    across_a = lax.ppermute(send_a, "tm", line)
    keep_b, send_b = correlate_next(white, table, second, column)
    across_b = lax.ppermute(send_b, "tm", line)
    halves = [over_column(keep_a, across_a), over_column(keep_b, across_b)]
    total = finish(halves, 1.0 / math.sqrt(total_samples))
    return total.reshape(sub, NSRC, SB, LAGS)


def solution(mesh):
    return jax.shard_map(
        shards,
        mesh=mesh,
        in_specs=(P("chan", "tm"), P(), P(), P()),
        out_specs=P(("chan", "tm"), None, None, None),
        check_vma=False,
    )
```

```python
import math

import jax
import jax.numpy as jnp
from jax import lax
from jax.experimental import pallas as pl
from jax.experimental.pallas import tpu as pltpu
from jax.sharding import PartitionSpec as P

TAPS = 64
MAXLAG = 128
LAGS = 256
NSRC = 2
SB = 4
NS = NSRC * SB
WIN = 8192
LANE = 128
SHIFTS = 16
LEFT = 256
EPS = 1e-05
MIB = 1024 * 1024

VMEM = pl.BlockSpec(memory_space=pltpu.VMEM)
SMEM = pl.BlockSpec(memory_space=pltpu.SMEM)
ANY = pl.BlockSpec(memory_space=pl.ANY)


def call(kernel, name, out, in_specs, scratch=(), out_specs=None, limit=16, flops=0, moved=0):
    return pl.pallas_call(
        kernel,
        out_shape=out,
        in_specs=in_specs,
        out_specs=out_specs or [VMEM] * len(out),
        scratch_shapes=list(scratch),
        compiler_params=pltpu.CompilerParams(vmem_limit_bytes=limit * MIB),
        cost_estimate=pl.CostEstimate(flops=flops, bytes_accessed=moved, transcendentals=0),
        name=name,
    )


def shape(dims, dtype):
    return jax.ShapeDtypeStruct(dims, dtype)


def fir_tile(taps):
    wide = jnp.broadcast_to(taps.astype(jnp.float32), (2 * LANE, 2 * LANE))
    rolled = pltpu.roll(wide, LANE, 1, stride=1, stride_axis=0)
    return rolled[:, :LANE].astype(jnp.bfloat16)


def wide_taps(taps):
    return jnp.pad(taps, (0, 2 * LANE - TAPS)).reshape(1, 2 * LANE)


def pick_sources(source_channels, x4):
    groups, _, sub, samples = x4.shape
    channels = groups * 2 * sub

    def kernel(ids_ref, x_ref, own_ref, edge_ref, high_ref, buf, sems):
        base = lax.axis_index("chan") * channels
        core = lax.axis_index("tm") % 2
        copies = []
        inner = []
        for j in range(NS):
            local = ids_ref[j // SB, j % SB] - base
            owned = (local >= 0) & (local < channels)
            row = jnp.clip(local, 0, channels - 1)
            group, half = row // (2 * sub), (row // sub) % 2
            inner.append(jnp.where(owned, row % sub, -1))
            copies.append(pltpu.make_async_copy(x_ref.at[group, half], buf.at[j], sems.at[j]))
        last = pl.ds(samples - LANE, LANE)
        rest = [
            pltpu.make_async_copy(
                x_ref.at[:, 0, :, last], edge_ref.at[pl.ds(0, groups)], sems.at[NS]
            ),
            pltpu.make_async_copy(x_ref.at[:, 1, :, last], high_ref, sems.at[NS + 1]),
        ]
        for copy in copies + rest:
            copy.start()
        rows = lax.broadcasted_iota(jnp.int32, (sub, 1), 0)
        own = jnp.zeros((NS, samples), jnp.float32)
        for j in range(NS):
            copies[j].wait()
            picked = buf[j].astype(jnp.float32) * jnp.where(rows == inner[j], 1.0, 0.0)
            picked = picked[:NS] + picked[NS:]
            own = own + pltpu.roll(picked, (j + NS - inner[j] % NS) % NS, 0)
        own_ref[...] = own.astype(jnp.bfloat16)
        end = jnp.where(core == 1, own[:, samples - LEFT :], own[:, :LEFT])
        for copy in rest:
            copy.wait()
        edge_ref[groups] = jnp.concatenate(
            [end[:, :LANE], end[:, LANE:]], axis=0
        ).astype(jnp.bfloat16)

    return call(
        kernel,
        "pick_sources",
        [
            shape((NS, samples), jnp.bfloat16),
            shape((groups + 1, sub, LANE), jnp.bfloat16),
            shape((groups, sub, LANE), jnp.bfloat16),
        ],
        [SMEM, ANY],
        [pltpu.VMEM((NS, sub, samples), jnp.bfloat16), pltpu.SemaphoreType.DMA((NS + 2,))],
        limit=61,
        moved=2 * MIB,
    )(source_channels, x4)


def extend_sources(own, edge):
    samples = own.shape[1]
    groups = edge.shape[0] - 1

    def kernel(own_ref, edge_ref, out_ref):
        end = edge_ref[groups].astype(jnp.float32)
        joined = [own_ref[...].astype(jnp.float32), end[:NS], end[NS:]]
        out_ref[...] = jnp.concatenate(joined, axis=1).astype(jnp.bfloat16)

    return call(
        kernel,
        "extend_sources",
        [shape((NS, samples + LEFT), jnp.bfloat16)],
        [VMEM, VMEM],
    )(own, edge)[0]


def add_pieces(*pieces):
    def kernel(*refs):
        total = refs[0][...].astype(jnp.float32)
        for ref in refs[1:-1]:
            total = total + ref[...].astype(jnp.float32)
        refs[-1][...] = total.astype(jnp.bfloat16)

    return call(
        kernel,
        "add_pieces",
        [shape(pieces[0].shape, jnp.bfloat16)],
        [VMEM] * len(pieces),
    )(*pieces)[0]


def filter_rows(offsets, taps, x4, other, low_edge, high_edge):
    groups, _, sub, half = x4.shape
    rows = groups * sub
    chunk = 1024
    parts = half // chunk
    total = 2 * parts

    def kernel(
        off_ref, taps_ref, x_ref, other_ref, low_ref, high_ref, out_ref, power_ref,
        value_buf, sems
    ):
        tile = lax.axis_index("tm")
        core = tile % 2
        matrix = fir_tile(taps_ref[...])
        first_kept = off_ref[tile // 2]

        def store(part):
            cols = pl.ds(part * chunk, chunk)
            return pltpu.make_async_copy(value_buf.at[part], out_ref.at[:, cols], sems.at[part])

        def run(read_low, read_high, previous):
            power = jnp.zeros((rows, LANE), jnp.float32)
            for part in range(total):
                read = read_low if part < parts else read_high
                for j in range(chunk // LANE):
                    first = (part % parts) * chunk + j * LANE
                    current = read(slice(first, first + LANE)).reshape(rows, LANE)
                    framed = jnp.concatenate([previous, current], axis=1)
                    value = jnp.dot(framed, matrix, preferred_element_type=jnp.float32)
                    power = power + value * value
                    place = lax.broadcasted_iota(jnp.int32, (1, LANE), 1) + part * chunk + j * LANE
                    value = value * jnp.where(place >= first_kept, 1.0, 0.0)
                    value_buf[part, :, j * LANE : (j + 1) * LANE] = value
                    previous = current
                store(part).start()
            power_ref[...] = power

        def own(cols):
            return x_ref[:, core, :, cols]

        def swapped(cols):
            return other_ref[:, :, cols]

        @pl.when(core == 0)
        def _():
            run(own, swapped, low_ref[:groups].reshape(rows, LANE))

        @pl.when(core == 1)
        def _():
            run(swapped, own, high_ref[...].reshape(rows, LANE))

        for part in range(total):
            store(part).wait()

    return call(
        kernel,
        "filter_rows",
        [shape((rows, 2 * half), jnp.float32), shape((rows, LANE), jnp.float32)],
        [SMEM, VMEM, VMEM, VMEM, VMEM, VMEM],
        [pltpu.VMEM((total, rows, chunk), jnp.float32), pltpu.SemaphoreType.DMA((total,))],
        out_specs=[ANY, VMEM],
        limit=40,
        flops=2 * rows * 2 * half * 512,
        moved=12 * MIB,
    )(offsets, taps, x4, other, low_edge, high_edge)


def filter_sources(offsets, taps, mine, other, power, chips):
    length = WIN + 2 * MAXLAG
    count = length // LANE
    half = mine.shape[1] - LEFT

    def kernel(off_ref, taps_ref, mine_ref, other_ref, power_ref, out_ref, energy_ref):
        tile = lax.axis_index("tm")
        core, chip = tile % 2, tile // 2
        mine_rows = mine_ref[...].astype(jnp.float32)
        other_rows = other_ref[...].astype(jnp.float32)
        low = jnp.where(core == 0, mine_rows, other_rows)
        high = jnp.where(core == 0, other_rows, mine_rows)
        raw = [low[:, half:], low[:, :half], high[:, :half], high[:, half : half + LANE]]
        raw = jnp.concatenate(raw, axis=1)
        blocks = [raw[:, j * LANE : (j + 1) * LANE] for j in range(count + 1)]
        before = jnp.concatenate(blocks[:-1], axis=0)
        after = jnp.concatenate(blocks[1:], axis=0)
        framed = jnp.concatenate([before, after], axis=1).astype(jnp.bfloat16)
        value = jnp.dot(framed, fir_tile(taps_ref[...]), preferred_element_type=jnp.float32)
        total = jnp.zeros((NS, LANE), jnp.float32)
        first_kept = [
            off_ref[jnp.maximum(chip - 1, 0)],
            off_ref[chip],
            off_ref[jnp.minimum(chip + 1, chips - 1)],
        ]
        for j in range(count):
            piece = value[j * NS : (j + 1) * NS, :]
            start = j * LANE - MAXLAG
            window = start // WIN
            if window == 0:
                total = total + piece * piece
            place = lax.broadcasted_iota(jnp.int32, (1, LANE), 1) + (start - window * WIN)
            keep = jnp.where(place >= first_kept[window + 1], 1.0, 0.0)
            if window < 0:
                keep = keep * jnp.where(chip > 0, 1.0, 0.0)
            if window > 0:
                keep = keep * jnp.where(chip < chips - 1, 1.0, 0.0)
            out_ref[:, j * LANE : (j + 1) * LANE] = piece * keep
        lines = []
        for r in range(power_ref.shape[0] // LANE):
            turned = power_ref[r * LANE : (r + 1) * LANE, :].T
            lines.append(jnp.sum(turned, axis=0, keepdims=True))
        repeated = jnp.concatenate([total] * SHIFTS, axis=0)
        lines.append(jnp.sum(repeated.T, axis=0, keepdims=True))
        lines.append(jnp.zeros((8 - len(lines), LANE), jnp.float32))
        energy = jnp.concatenate(lines, axis=0)
        energy_ref[...] = jnp.broadcast_to(energy[None], energy_ref.shape)

    return call(
        kernel,
        "filter_sources",
        [shape((NS, length), jnp.float32), shape((chips, 8, LANE), jnp.float32)],
        [SMEM, VMEM, VMEM, VMEM, VMEM],
        moved=MIB,
    )(offsets, taps, mine, other, power)


def lag_products(white, table_ref, pairs, keep_ref, send_ref, half_groups):
    rows, depth = white.shape
    sub = rows // half_groups // 2
    own_low = (lax.axis_index("tm") // 2) % 2 == 0
    for place, pair in enumerate(pairs):
        offset = pair * 2 * SHIFTS
        left = table_ref[offset : offset + depth, :]
        right = table_ref[offset + SHIFTS : offset + SHIFTS + depth, :]
        lags = jnp.concatenate([left, right], axis=1)
        value = jnp.dot(white[...], lags, preferred_element_type=jnp.float32)
        value = value.reshape(half_groups, 2, sub, 2 * LANE)
        low, high = value[:, 0], value[:, 1]
        cols = slice(place * 2 * LANE, (place + 1) * 2 * LANE)
        keep_ref[:, :, cols] = jnp.where(own_low, low, high)
        send_ref[:, :, cols] = jnp.where(own_low, high, low).astype(jnp.bfloat16)


def correlate_first(energies, traces, rows, pairs, half_groups, total_samples):
    channels, depth = rows.shape
    length = traces.shape[1]
    chunk = 1024
    loads = depth // chunk

    def kernel(
        energy_ref, traces_ref, rows_ref, keep_ref, send_ref, white, table, buf, shifted, sems
    ):
        copies = []
        for i in range(loads):
            cols = pl.ds(i * chunk, chunk)
            copies.append(pltpu.make_async_copy(rows_ref.at[:, cols], buf.at[i], sems.at[i]))
        for copy in copies:
            copy.start()
        energy = jnp.sum(energy_ref[...], axis=0)
        scale = lax.rsqrt(energy / total_samples + EPS)
        padded = jnp.concatenate([scale, jnp.zeros((LANE - 8, LANE), jnp.float32)], axis=0)
        turned = padded.T
        parts = channels // LANE
        gain = jnp.concatenate([turned[:, r : r + 1] for r in range(parts)], axis=0)
        trace = traces_ref[...] * turned[:NS, parts : parts + 1]
        trace = trace.astype(jnp.bfloat16).astype(jnp.float32)
        for b in range(SHIFTS):
            moved = trace if b == 0 else pltpu.roll(trace, length - b, 1)
            shifted[b * NS : (b + 1) * NS, :] = moved
        for j in range(length // LANE):
            cols = slice(j * LANE, (j + 1) * LANE)
            table[cols, :] = shifted[:, cols].T.astype(jnp.bfloat16)
        for i in range(loads):
            copies[i].wait()
            white[:, i * chunk : (i + 1) * chunk] = (buf[i] * gain).astype(jnp.bfloat16)
        lag_products(white, table, pairs, keep_ref, send_ref, half_groups)

    sub = channels // half_groups // 2
    cols = len(pairs) * 2 * LANE
    return call(
        kernel,
        "correlate_first",
        [
            shape((half_groups, sub, cols), jnp.float32),
            shape((half_groups, sub, cols), jnp.bfloat16),
            shape((channels, depth), jnp.bfloat16),
            shape((length, LANE), jnp.bfloat16),
        ],
        [VMEM, VMEM, ANY],
        [
            pltpu.VMEM((loads, channels, chunk), jnp.float32),
            pltpu.VMEM((LANE, length), jnp.float32),
            pltpu.SemaphoreType.DMA((loads,)),
        ],
        limit=40,
        flops=2 * channels * depth * cols,
        moved=16 * MIB,
    )(energies, traces, rows)


def correlate_next(white, table, pairs, half_groups):
    channels, depth = white.shape

    def kernel(white_ref, table_ref, keep_ref, send_ref):
        lag_products(white_ref, table_ref, pairs, keep_ref, send_ref, half_groups)

    sub = channels // half_groups // 2
    cols = len(pairs) * 2 * LANE
    return call(
        kernel,
        "correlate_next",
        [
            shape((half_groups, sub, cols), jnp.float32),
            shape((half_groups, sub, cols), jnp.bfloat16),
        ],
        [VMEM, VMEM],
        flops=2 * channels * depth * cols,
        moved=8 * MIB,
    )(white, table)


def add_line(keeps, arrivals):
    groups, sub, _ = keeps[0].shape
    widths = [keep.shape[2] for keep in keeps]
    count = len(keeps)

    def kernel(*refs):
        start = 0
        for keep_ref, across_ref, width in zip(refs[:count], refs[count : 2 * count], widths):
            value = keep_ref[...] + across_ref[...].astype(jnp.float32)
            refs[-1][:, :, start : start + width] = value.astype(jnp.bfloat16)
            start += width

    return call(
        kernel,
        "add_line",
        [shape((groups, sub, sum(widths)), jnp.bfloat16)],
        [VMEM] * (2 * count),
        moved=MIB,
    )(*keeps, *arrivals)[0]


def finish(parts, factor):
    count, sub, cols = parts.shape

    def kernel(parts_ref, out_ref, turned):
        blank = jnp.zeros((LANE - sub, LANE), jnp.float32)
        value = parts_ref[0].astype(jnp.float32)
        for i in range(1, count):
            value = value + parts_ref[i].astype(jnp.float32)
        value = value * factor
        for j in range(cols // LANE):
            block = jnp.concatenate([value[:, j * LANE : (j + 1) * LANE], blank], axis=0)
            turned[j * LANE : (j + 1) * LANE, :] = block.T
        for m in range(NS):
            for j in range(LAGS // LANE):
                block = turned[pl.ds(j * LANE * NS + m, LANE, stride=NS), :]
                out_ref[:, m // SB, m % SB, j * LANE : (j + 1) * LANE] = block.T[:sub]

    return call(
        kernel,
        "finish",
        [shape((sub, NSRC, SB, LAGS), jnp.float32)],
        [VMEM],
        [pltpu.VMEM((NS * LAGS, LANE), jnp.float32)],
        moved=MIB,
    )(parts)[0]


def shards(strain_rate, whiten_taps, source_channels, window_offsets):
    channels, samples = strain_rate.shape
    tiles = lax.axis_size("tm")
    groups_chan = lax.axis_size("chan")
    total_samples = samples * tiles
    chips = tiles // 2
    sub = channels // tiles
    core = lax.axis_index("tm") % 2
    taps = wide_taps(whiten_taps)

    x4 = strain_rate.reshape(chips, 2, sub, samples)
    own, edge, high = pick_sources(source_channels, x4)
    core, own = lax.optimization_barrier((core, own))

    swap = [(i, i ^ 1) for i in range(tiles)]
    to_next = [(2 * k - 1, 2 * k) for k in range(1, chips)]
    both_next = to_next + [(b, a) for a, b in to_next]
    edge = lax.ppermute(edge, "tm", both_next)
    away = lax.dynamic_index_in_dim(x4, 1 - core, axis=1, keepdims=False)
    other = lax.ppermute(away, "tm", swap)
    high = lax.ppermute(high, "tm", [(2 * k - 1, 2 * k + 1) for k in range(1, chips)])

    piece = extend_sources(own, edge)
    parts = [
        lax.ppermute(piece, "chan", [(i, (i + 2 * d) % groups_chan) for i in range(groups_chan)])
        for d in range(1, groups_chan // 2)
    ]
    piece = add_pieces(piece, *parts)
    arrived = lax.ppermute(piece, "chan", [(i, i ^ 1) for i in range(groups_chan)])
    filtered, power = filter_rows(window_offsets, taps, x4, other, edge, high)
    arrived, power = lax.optimization_barrier((arrived, power))
    piece = add_pieces(piece, arrived)
    piece_other = lax.ppermute(piece, "tm", swap)
    traces, energy = filter_sources(window_offsets, taps, piece, piece_other, power, chips)
    same = [[2 * k + c for k in range(chips)] for c in range(2)]
    energies = lax.all_to_all(energy, "tm", 0, 0, tiled=True, axis_index_groups=same)

    column = tiles // 4
    dots = LAGS // (2 * SHIFTS)
    first, second = range(dots // 2), range(dots // 2, dots)
    keep_a, send_a, white, table = correlate_first(
        energies, traces, filtered, first, column, total_samples
    )
    line = [(i, i ^ 2) for i in range(tiles)]
    across_a = lax.ppermute(send_a, "tm", line)
    keep_b, send_b = correlate_next(white, table, second, column)
    across_b = lax.ppermute(send_b, "tm", line)
    summed = add_line([keep_a, keep_b], [across_a, across_b])
    columns = [[4 * z + r for z in range(column)] for r in range(4)]
    parts = lax.all_to_all(summed, "tm", 0, 0, tiled=True, axis_index_groups=columns)
    return finish(parts, 1.0 / math.sqrt(total_samples))


def solution(mesh):
    return jax.shard_map(
        shards,
        mesh=mesh,
        in_specs=(P("chan", "tm"), P(), P(), P()),
        out_specs=P(("chan", "tm"), None, None, None),
        check_vma=False,
    )
```

```python
import math

import jax
import jax.numpy as jnp
from jax import lax
from jax.experimental import pallas as pl
from jax.experimental.pallas import tpu as pltpu
from jax.sharding import PartitionSpec as P

TAPS = 64
MAXLAG = 128
LAGS = 256
NSRC = 2
SB = 4
NS = NSRC * SB
WIN = 8192
LANE = 128
SHIFTS = 16
LEFT = 256
EPS = 1e-05
MIB = 1024 * 1024

VMEM = pl.BlockSpec(memory_space=pltpu.VMEM)
SMEM = pl.BlockSpec(memory_space=pltpu.SMEM)
ANY = pl.BlockSpec(memory_space=pl.ANY)


def call(kernel, name, out, in_specs, scratch=(), out_specs=None, limit=16, flops=0, moved=0):
    return pl.pallas_call(
        kernel,
        out_shape=out,
        in_specs=in_specs,
        out_specs=out_specs or [VMEM] * len(out),
        scratch_shapes=list(scratch),
        compiler_params=pltpu.CompilerParams(vmem_limit_bytes=limit * MIB),
        cost_estimate=pl.CostEstimate(flops=flops, bytes_accessed=moved, transcendentals=0),
        name=name,
    )


def shape(dims, dtype):
    return jax.ShapeDtypeStruct(dims, dtype)


def fir_tile(taps):
    wide = jnp.broadcast_to(taps.astype(jnp.float32), (2 * LANE, 2 * LANE))
    rolled = pltpu.roll(wide, LANE, 1, stride=1, stride_axis=0)
    return rolled[:, :LANE].astype(jnp.bfloat16)


def wide_taps(taps):
    return jnp.pad(taps, (0, 2 * LANE - TAPS)).reshape(1, 2 * LANE)


def pick_sources(source_channels, x4):
    groups, _, sub, samples = x4.shape
    channels = groups * 2 * sub

    def kernel(ids_ref, x_ref, own_ref, low_ref, high_ref, buf, sems):
        base = lax.axis_index("chan") * channels
        copies = []
        inner = []
        for j in range(NS):
            local = ids_ref[j // SB, j % SB] - base
            owned = (local >= 0) & (local < channels)
            row = jnp.clip(local, 0, channels - 1)
            group, half = row // (2 * sub), (row // sub) % 2
            inner.append(jnp.where(owned, row % sub, -1))
            copies.append(pltpu.make_async_copy(x_ref.at[group, half], buf.at[j], sems.at[j]))
        last = pl.ds(samples - LANE, LANE)
        rest = [
            pltpu.make_async_copy(x_ref.at[:, 0, :, last], low_ref, sems.at[NS]),
            pltpu.make_async_copy(x_ref.at[:, 1, :, last], high_ref, sems.at[NS + 1]),
        ]
        for copy in copies + rest:
            copy.start()
        rows = lax.broadcasted_iota(jnp.int32, (sub, 1), 0)
        own = jnp.zeros((NS, samples), jnp.float32)
        for j in range(NS):
            copies[j].wait()
            picked = buf[j].astype(jnp.float32) * jnp.where(rows == inner[j], 1.0, 0.0)
            picked = picked[:NS] + picked[NS:]
            own = own + pltpu.roll(picked, (j + NS - inner[j] % NS) % NS, 0)
        own_ref[...] = own.astype(jnp.bfloat16)
        for copy in rest:
            copy.wait()

    edge = shape((groups, sub, LANE), jnp.bfloat16)
    return call(
        kernel,
        "pick_sources",
        [
            shape((NS, samples), jnp.bfloat16),
            edge,
            edge,
        ],
        [SMEM, ANY],
        [pltpu.VMEM((NS, sub, samples), jnp.bfloat16), pltpu.SemaphoreType.DMA((NS + 2,))],
        limit=52,
        moved=2 * MIB,
    )(source_channels, x4)


def join_sources(piece, arrived):
    samples = piece.shape[1]

    def kernel(piece_ref, arrived_ref, out_ref, end_ref):
        core = lax.axis_index("tm") % 2
        total = piece_ref[...].astype(jnp.float32) + arrived_ref[...].astype(jnp.float32)
        out_ref[...] = total.astype(jnp.bfloat16)
        end = jnp.where(core == 1, total[:, samples - LEFT :], total[:, :LEFT])
        end_ref[...] = end.astype(jnp.bfloat16)

    return call(
        kernel,
        "join_sources",
        [shape(piece.shape, jnp.bfloat16), shape((NS, LEFT), jnp.bfloat16)],
        [VMEM, VMEM],
    )(piece, arrived)


def extend_sources(piece, edge):
    samples = piece.shape[1]

    def kernel(piece_ref, edge_ref, out_ref):
        out_ref[:, :samples] = piece_ref[...]
        out_ref[:, samples:] = edge_ref[...]

    return call(
        kernel,
        "extend_sources",
        [shape((NS, samples + LEFT), jnp.bfloat16)],
        [VMEM, VMEM],
    )(piece, edge)[0]


def add_pieces(*pieces):
    def kernel(*refs):
        total = refs[0][...].astype(jnp.float32)
        for ref in refs[1:-1]:
            total = total + ref[...].astype(jnp.float32)
        refs[-1][...] = total.astype(jnp.bfloat16)

    return call(
        kernel,
        "add_pieces",
        [shape(pieces[0].shape, jnp.bfloat16)],
        [VMEM] * len(pieces),
    )(*pieces)[0]


def filter_rows(offsets, taps, x4, other, low_edge, high_edge):
    groups, _, sub, half = x4.shape
    rows = groups * sub
    chunk = 1024
    parts = half // chunk
    total = 2 * parts

    def kernel(
        off_ref, taps_ref, x_ref, other_ref, low_ref, high_ref, out_ref, power_ref,
        value_buf, sems
    ):
        tile = lax.axis_index("tm")
        core = tile % 2
        matrix = fir_tile(taps_ref[...])
        first_kept = off_ref[tile // 2]

        def store(part):
            cols = pl.ds(part * chunk, chunk)
            return pltpu.make_async_copy(value_buf.at[part], out_ref.at[:, cols], sems.at[part])

        def run(read_low, read_high, previous):
            power = jnp.zeros((rows, LANE), jnp.float32)
            for part in range(total):
                read = read_low if part < parts else read_high
                for j in range(chunk // LANE):
                    first = (part % parts) * chunk + j * LANE
                    current = read(slice(first, first + LANE)).reshape(rows, LANE)
                    framed = jnp.concatenate([previous, current], axis=1)
                    value = jnp.dot(framed, matrix, preferred_element_type=jnp.float32)
                    power = power + value * value
                    place = lax.broadcasted_iota(jnp.int32, (1, LANE), 1) + part * chunk + j * LANE
                    value = value * jnp.where(place >= first_kept, 1.0, 0.0)
                    value_buf[part, :, j * LANE : (j + 1) * LANE] = value
                    previous = current
                store(part).start()
            power_ref[...] = power

        def own(cols):
            return x_ref[:, core, :, cols]

        def swapped(cols):
            return other_ref[:, :, cols]

        @pl.when(core == 0)
        def _():
            run(own, swapped, low_ref[...].reshape(rows, LANE))

        @pl.when(core == 1)
        def _():
            run(swapped, own, high_ref[...].reshape(rows, LANE))

        for part in range(total):
            store(part).wait()

    return call(
        kernel,
        "filter_rows",
        [shape((rows, 2 * half), jnp.float32), shape((rows, LANE), jnp.float32)],
        [SMEM, VMEM, VMEM, VMEM, VMEM, VMEM],
        [pltpu.VMEM((total, rows, chunk), jnp.float32), pltpu.SemaphoreType.DMA((total,))],
        out_specs=[ANY, VMEM],
        limit=40,
        flops=2 * rows * 2 * half * 512,
        moved=12 * MIB,
    )(offsets, taps, x4, other, low_edge, high_edge)


def filter_sources(offsets, taps, mine, other, power, chips):
    length = WIN + 2 * MAXLAG
    count = length // LANE
    half = mine.shape[1] - LEFT

    def kernel(off_ref, taps_ref, mine_ref, other_ref, power_ref, out_ref, energy_ref):
        tile = lax.axis_index("tm")
        core, chip = tile % 2, tile // 2
        mine_rows = mine_ref[...].astype(jnp.float32)
        other_rows = other_ref[...].astype(jnp.float32)
        low = jnp.where(core == 0, mine_rows, other_rows)
        high = jnp.where(core == 0, other_rows, mine_rows)
        raw = [low[:, half:], low[:, :half], high[:, :half], high[:, half : half + LANE]]
        raw = jnp.concatenate(raw, axis=1)
        blocks = [raw[:, j * LANE : (j + 1) * LANE] for j in range(count + 1)]
        before = jnp.concatenate(blocks[:-1], axis=0)
        after = jnp.concatenate(blocks[1:], axis=0)
        framed = jnp.concatenate([before, after], axis=1).astype(jnp.bfloat16)
        value = jnp.dot(framed, fir_tile(taps_ref[...]), preferred_element_type=jnp.float32)
        total = jnp.zeros((NS, LANE), jnp.float32)
        first_kept = [
            off_ref[jnp.maximum(chip - 1, 0)],
            off_ref[chip],
            off_ref[jnp.minimum(chip + 1, chips - 1)],
        ]
        for j in range(count):
            piece = value[j * NS : (j + 1) * NS, :]
            start = j * LANE - MAXLAG
            window = start // WIN
            if window == 0:
                total = total + piece * piece
            place = lax.broadcasted_iota(jnp.int32, (1, LANE), 1) + (start - window * WIN)
            keep = jnp.where(place >= first_kept[window + 1], 1.0, 0.0)
            if window < 0:
                keep = keep * jnp.where(chip > 0, 1.0, 0.0)
            if window > 0:
                keep = keep * jnp.where(chip < chips - 1, 1.0, 0.0)
            out_ref[:, j * LANE : (j + 1) * LANE] = piece * keep
        lines = []
        for r in range(power_ref.shape[0] // LANE):
            turned = power_ref[r * LANE : (r + 1) * LANE, :].T
            lines.append(jnp.sum(turned, axis=0, keepdims=True))
        repeated = jnp.concatenate([total] * SHIFTS, axis=0)
        lines.append(jnp.sum(repeated.T, axis=0, keepdims=True))
        lines.append(jnp.zeros((8 - len(lines), LANE), jnp.float32))
        energy = jnp.concatenate(lines, axis=0)
        energy_ref[...] = jnp.broadcast_to(energy[None], energy_ref.shape)

    return call(
        kernel,
        "filter_sources",
        [shape((NS, length), jnp.float32), shape((chips, 8, LANE), jnp.float32)],
        [SMEM, VMEM, VMEM, VMEM, VMEM],
        moved=MIB,
    )(offsets, taps, mine, other, power)


def lag_products(white, table_ref, pairs, keep_ref, send_ref, half_groups):
    rows, depth = white.shape
    sub = rows // half_groups // 2
    own_low = (lax.axis_index("tm") // 2) % 2 == 0
    for place, pair in enumerate(pairs):
        offset = pair * 2 * SHIFTS
        left = table_ref[offset : offset + depth, :]
        right = table_ref[offset + SHIFTS : offset + SHIFTS + depth, :]
        lags = jnp.concatenate([left, right], axis=1)
        value = jnp.dot(white[...], lags, preferred_element_type=jnp.float32)
        value = value.reshape(half_groups, 2, sub, 2 * LANE)
        low, high = value[:, 0], value[:, 1]
        cols = slice(place * 2 * LANE, (place + 1) * 2 * LANE)
        keep_ref[:, :, cols] = jnp.where(own_low, low, high)
        send_ref[:, :, cols] = jnp.where(own_low, high, low).astype(jnp.bfloat16)


def correlate_first(energies, traces, rows, pairs, half_groups, total_samples):
    channels, depth = rows.shape
    length = traces.shape[1]
    chunk = 1024
    loads = depth // chunk

    def kernel(
        energy_ref, traces_ref, rows_ref, keep_ref, send_ref, white, table, buf, shifted, sems
    ):
        copies = []
        for i in range(loads):
            cols = pl.ds(i * chunk, chunk)
            copies.append(pltpu.make_async_copy(rows_ref.at[:, cols], buf.at[i], sems.at[i]))
        for copy in copies:
            copy.start()
        energy = jnp.sum(energy_ref[...], axis=0)
        scale = lax.rsqrt(energy / total_samples + EPS)
        padded = jnp.concatenate([scale, jnp.zeros((LANE - 8, LANE), jnp.float32)], axis=0)
        turned = padded.T
        parts = channels // LANE
        gain = jnp.concatenate([turned[:, r : r + 1] for r in range(parts)], axis=0)
        trace = traces_ref[...] * turned[:NS, parts : parts + 1]
        trace = trace.astype(jnp.bfloat16).astype(jnp.float32)
        for b in range(SHIFTS):
            moved = trace if b == 0 else pltpu.roll(trace, length - b, 1)
            shifted[b * NS : (b + 1) * NS, :] = moved
        for j in range(length // LANE):
            cols = slice(j * LANE, (j + 1) * LANE)
            table[cols, :] = shifted[:, cols].T.astype(jnp.bfloat16)
        for i in range(loads):
            copies[i].wait()
            white[:, i * chunk : (i + 1) * chunk] = (buf[i] * gain).astype(jnp.bfloat16)
        lag_products(white, table, pairs, keep_ref, send_ref, half_groups)

    sub = channels // half_groups // 2
    cols = len(pairs) * 2 * LANE
    return call(
        kernel,
        "correlate_first",
        [
            shape((half_groups, sub, cols), jnp.float32),
            shape((half_groups, sub, cols), jnp.bfloat16),
            shape((channels, depth), jnp.bfloat16),
            shape((length, LANE), jnp.bfloat16),
        ],
        [VMEM, VMEM, ANY],
        [
            pltpu.VMEM((loads, channels, chunk), jnp.float32),
            pltpu.VMEM((LANE, length), jnp.float32),
            pltpu.SemaphoreType.DMA((loads,)),
        ],
        limit=40,
        flops=2 * channels * depth * cols,
        moved=16 * MIB,
    )(energies, traces, rows)


def correlate_next(white, table, pairs, half_groups):
    channels, depth = white.shape

    def kernel(white_ref, table_ref, keep_ref, send_ref):
        lag_products(white_ref, table_ref, pairs, keep_ref, send_ref, half_groups)

    sub = channels // half_groups // 2
    cols = len(pairs) * 2 * LANE
    return call(
        kernel,
        "correlate_next",
        [
            shape((half_groups, sub, cols), jnp.float32),
            shape((half_groups, sub, cols), jnp.bfloat16),
        ],
        [VMEM, VMEM],
        flops=2 * channels * depth * cols,
        moved=8 * MIB,
    )(white, table)


def add_line(keeps, arrivals):
    groups, sub, _ = keeps[0].shape
    widths = [keep.shape[2] for keep in keeps]
    count = len(keeps)

    def kernel(*refs):
        start = 0
        for keep_ref, across_ref, width in zip(refs[:count], refs[count : 2 * count], widths):
            value = keep_ref[...] + across_ref[...].astype(jnp.float32)
            refs[-1][:, :, start : start + width] = value.astype(jnp.bfloat16)
            start += width

    return call(
        kernel,
        "add_line",
        [shape((groups, sub, sum(widths)), jnp.bfloat16)],
        [VMEM] * (2 * count),
        moved=MIB,
    )(*keeps, *arrivals)[0]


def finish(parts, factor):
    count, sub, cols = parts.shape

    def kernel(parts_ref, out_ref, turned):
        blank = jnp.zeros((LANE - sub, LANE), jnp.float32)
        value = parts_ref[0].astype(jnp.float32)
        for i in range(1, count):
            value = value + parts_ref[i].astype(jnp.float32)
        value = value * factor
        for j in range(cols // LANE):
            block = jnp.concatenate([value[:, j * LANE : (j + 1) * LANE], blank], axis=0)
            turned[j * LANE : (j + 1) * LANE, :] = block.T
        for m in range(NS):
            for j in range(LAGS // LANE):
                block = turned[pl.ds(j * LANE * NS + m, LANE, stride=NS), :]
                out_ref[:, m // SB, m % SB, j * LANE : (j + 1) * LANE] = block.T[:sub]

    return call(
        kernel,
        "finish",
        [shape((sub, NSRC, SB, LAGS), jnp.float32)],
        [VMEM],
        [pltpu.VMEM((NS * LAGS, LANE), jnp.float32)],
        moved=MIB,
    )(parts)[0]


def shards(strain_rate, whiten_taps, source_channels, window_offsets):
    channels, samples = strain_rate.shape
    tiles = lax.axis_size("tm")
    groups_chan = lax.axis_size("chan")
    total_samples = samples * tiles
    chips = tiles // 2
    sub = channels // tiles
    core = lax.axis_index("tm") % 2
    taps = wide_taps(whiten_taps)

    x4 = strain_rate.reshape(chips, 2, sub, samples)
    own, low_edge, high_edge = pick_sources(source_channels, x4)

    swap = [(i, i ^ 1) for i in range(tiles)]
    to_next = [(2 * k - 1, 2 * k) for k in range(1, chips)]
    skip_next = [(2 * k - 1, 2 * k + 1) for k in range(1, chips)]
    both_next = to_next + [(b, a) for a, b in to_next]

    parts = [
        lax.ppermute(own, "chan", [(i, (i + 2 * d) % groups_chan) for i in range(groups_chan)])
        for d in range(1, groups_chan // 2)
    ]
    piece = add_pieces(own, *parts)
    piece, core, low_edge, high_edge = lax.optimization_barrier(
        (piece, core, low_edge, high_edge)
    )
    away = lax.dynamic_index_in_dim(x4, 1 - core, axis=1, keepdims=False)
    other = lax.ppermute(away, "tm", swap)
    arrived = lax.ppermute(piece, "chan", [(i, i ^ 1) for i in range(groups_chan)])
    low_edge = lax.ppermute(low_edge, "tm", to_next)
    high_edge = lax.ppermute(high_edge, "tm", skip_next)
    piece, end = join_sources(piece, arrived)
    edge = lax.ppermute(end, "tm", both_next)
    filtered, power = filter_rows(window_offsets, taps, x4, other, low_edge, high_edge)
    edge, power = lax.optimization_barrier((edge, power))
    piece = extend_sources(piece, edge)
    piece_other = lax.ppermute(piece, "tm", swap)
    traces, energy = filter_sources(window_offsets, taps, piece, piece_other, power, chips)
    same = [[2 * k + c for k in range(chips)] for c in range(2)]
    energies = lax.all_to_all(energy, "tm", 0, 0, tiled=True, axis_index_groups=same)

    column = tiles // 4
    dots = LAGS // (2 * SHIFTS)
    first, second = range(dots // 2), range(dots // 2, dots)
    keep_a, send_a, white, table = correlate_first(
        energies, traces, filtered, first, column, total_samples
    )
    line = [(i, i ^ 2) for i in range(tiles)]
    across_a = lax.ppermute(send_a, "tm", line)
    keep_b, send_b = correlate_next(white, table, second, column)
    across_b = lax.ppermute(send_b, "tm", line)
    summed = add_line([keep_a, keep_b], [across_a, across_b])
    columns = [[4 * z + r for z in range(column)] for r in range(4)]
    parts = lax.all_to_all(summed, "tm", 0, 0, tiled=True, axis_index_groups=columns)
    return finish(parts, 1.0 / math.sqrt(total_samples))


def solution(mesh):
    return jax.shard_map(
        shards,
        mesh=mesh,
        in_specs=(P("chan", "tm"), P(), P(), P()),
        out_specs=P(("chan", "tm"), None, None, None),
        check_vma=False,
    )
```

```python
import math

import jax
import jax.numpy as jnp
from jax import lax
from jax.experimental import pallas as pl
from jax.experimental.pallas import tpu as pltpu
from jax.sharding import PartitionSpec as P

TAPS = 64
MAXLAG = 128
LAGS = 256
NSRC = 2
SB = 4
NS = NSRC * SB
WIN = 8192
LANE = 128
SHIFTS = 16
LEFT = 256
EPS = 1e-05
MIB = 1024 * 1024

VMEM = pl.BlockSpec(memory_space=pltpu.VMEM)
SMEM = pl.BlockSpec(memory_space=pltpu.SMEM)
ANY = pl.BlockSpec(memory_space=pl.ANY)


def call(kernel, name, out, in_specs, scratch=(), out_specs=None, limit=16, flops=0, moved=0):
    return pl.pallas_call(
        kernel,
        out_shape=out,
        in_specs=in_specs,
        out_specs=out_specs or [VMEM] * len(out),
        scratch_shapes=list(scratch),
        compiler_params=pltpu.CompilerParams(vmem_limit_bytes=limit * MIB),
        cost_estimate=pl.CostEstimate(flops=flops, bytes_accessed=moved, transcendentals=0),
        name=name,
    )


def shape(dims, dtype):
    return jax.ShapeDtypeStruct(dims, dtype)


def fir_tile(taps):
    wide = jnp.broadcast_to(taps.astype(jnp.float32), (2 * LANE, 2 * LANE))
    rolled = pltpu.roll(wide, LANE, 1, stride=1, stride_axis=0)
    return rolled[:, :LANE].astype(jnp.bfloat16)


def wide_taps(taps):
    return jnp.pad(taps, (0, 2 * LANE - TAPS)).reshape(1, 2 * LANE)


def pick_sources(source_channels, x4):
    groups, _, sub, samples = x4.shape
    channels = groups * 2 * sub

    def kernel(ids_ref, x_ref, own_ref, edge_ref, high_ref, away_ref, buf, sems):
        base = lax.axis_index("chan") * channels
        core = lax.axis_index("tm") % 2
        copies = []
        inner = []
        for j in range(NS):
            local = ids_ref[j // SB, j % SB] - base
            owned = (local >= 0) & (local < channels)
            row = jnp.clip(local, 0, channels - 1)
            group, half = row // (2 * sub), (row // sub) % 2
            inner.append(jnp.where(owned, row % sub, -1))
            copies.append(pltpu.make_async_copy(x_ref.at[group, half], buf.at[j], sems.at[j]))
        last = pl.ds(samples - LANE, LANE)
        rest = [
            pltpu.make_async_copy(
                x_ref.at[:, 0, :, last], edge_ref.at[pl.ds(0, groups)], sems.at[NS]
            ),
            pltpu.make_async_copy(x_ref.at[:, 1, :, last], high_ref, sems.at[NS + 1]),
            pltpu.make_async_copy(x_ref.at[:, 1 - core], away_ref, sems.at[NS + 2]),
        ]
        for copy in copies + rest:
            copy.start()
        rows = lax.broadcasted_iota(jnp.int32, (sub, 1), 0)
        own = jnp.zeros((NS, samples), jnp.float32)
        for j in range(NS):
            copies[j].wait()
            picked = buf[j].astype(jnp.float32) * jnp.where(rows == inner[j], 1.0, 0.0)
            picked = picked[:NS] + picked[NS:]
            own = own + pltpu.roll(picked, (j + NS - inner[j] % NS) % NS, 0)
        own_ref[...] = own.astype(jnp.bfloat16)
        end = jnp.where(core == 1, own[:, samples - LEFT :], own[:, :LEFT])
        for copy in rest:
            copy.wait()
        edge_ref[groups] = jnp.concatenate(
            [end[:, :LANE], end[:, LANE:]], axis=0
        ).astype(jnp.bfloat16)

    return call(
        kernel,
        "pick_sources",
        [
            shape((NS, samples), jnp.bfloat16),
            shape((groups + 1, sub, LANE), jnp.bfloat16),
            shape((groups, sub, LANE), jnp.bfloat16),
            shape((groups, sub, samples), jnp.bfloat16),
        ],
        [SMEM, ANY],
        [pltpu.VMEM((NS, sub, samples), jnp.bfloat16), pltpu.SemaphoreType.DMA((NS + 3,))],
        limit=50,
        moved=2 * MIB,
    )(source_channels, x4)


def extend_sources(own, edge):
    samples = own.shape[1]
    groups = edge.shape[0] - 1

    def kernel(own_ref, edge_ref, out_ref):
        end = edge_ref[groups].astype(jnp.float32)
        joined = [own_ref[...].astype(jnp.float32), end[:NS], end[NS:]]
        out_ref[...] = jnp.concatenate(joined, axis=1).astype(jnp.bfloat16)

    return call(
        kernel,
        "extend_sources",
        [shape((NS, samples + LEFT), jnp.bfloat16)],
        [VMEM, VMEM],
    )(own, edge)[0]


def add_pieces(*pieces):
    def kernel(*refs):
        total = refs[0][...].astype(jnp.float32)
        for ref in refs[1:-1]:
            total = total + ref[...].astype(jnp.float32)
        refs[-1][...] = total.astype(jnp.bfloat16)

    return call(
        kernel,
        "add_pieces",
        [shape(pieces[0].shape, jnp.bfloat16)],
        [VMEM] * len(pieces),
    )(*pieces)[0]


def filter_rows(offsets, taps, x4, other, low_edge, high_edge):
    groups, _, sub, half = x4.shape
    rows = groups * sub
    chunk = 1024
    parts = half // chunk
    total = 2 * parts

    def kernel(
        off_ref, taps_ref, x_ref, other_ref, low_ref, high_ref, out_ref, power_ref,
        value_buf, sems
    ):
        tile = lax.axis_index("tm")
        core = tile % 2
        matrix = fir_tile(taps_ref[...])
        first_kept = off_ref[tile // 2]

        def store(part):
            cols = pl.ds(part * chunk, chunk)
            return pltpu.make_async_copy(value_buf.at[part], out_ref.at[:, cols], sems.at[part])

        def run(read_low, read_high, previous):
            power = jnp.zeros((rows, LANE), jnp.float32)
            for part in range(total):
                read = read_low if part < parts else read_high
                for j in range(chunk // LANE):
                    first = (part % parts) * chunk + j * LANE
                    current = read(slice(first, first + LANE)).reshape(rows, LANE)
                    framed = jnp.concatenate([previous, current], axis=1)
                    value = jnp.dot(framed, matrix, preferred_element_type=jnp.float32)
                    power = power + value * value
                    place = lax.broadcasted_iota(jnp.int32, (1, LANE), 1) + part * chunk + j * LANE
                    value = value * jnp.where(place >= first_kept, 1.0, 0.0)
                    value_buf[part, :, j * LANE : (j + 1) * LANE] = value
                    previous = current
                store(part).start()
            power_ref[...] = power

        def own(cols):
            return x_ref[:, core, :, cols]

        def swapped(cols):
            return other_ref[:, :, cols]

        @pl.when(core == 0)
        def _():
            run(own, swapped, low_ref[:groups].reshape(rows, LANE))

        @pl.when(core == 1)
        def _():
            run(swapped, own, high_ref[...].reshape(rows, LANE))

        for part in range(total):
            store(part).wait()

    return call(
        kernel,
        "filter_rows",
        [shape((rows, 2 * half), jnp.float32), shape((rows, LANE), jnp.float32)],
        [SMEM, VMEM, VMEM, VMEM, VMEM, VMEM],
        [pltpu.VMEM((total, rows, chunk), jnp.float32), pltpu.SemaphoreType.DMA((total,))],
        out_specs=[ANY, VMEM],
        limit=40,
        flops=2 * rows * 2 * half * 512,
        moved=12 * MIB,
    )(offsets, taps, x4, other, low_edge, high_edge)


def filter_sources(offsets, taps, mine, other, power, chips):
    length = WIN + 2 * MAXLAG
    count = length // LANE
    half = mine.shape[1] - LEFT

    def kernel(off_ref, taps_ref, mine_ref, other_ref, power_ref, out_ref, energy_ref):
        tile = lax.axis_index("tm")
        core, chip = tile % 2, tile // 2
        mine_rows = mine_ref[...].astype(jnp.float32)
        other_rows = other_ref[...].astype(jnp.float32)
        low = jnp.where(core == 0, mine_rows, other_rows)
        high = jnp.where(core == 0, other_rows, mine_rows)
        raw = [low[:, half:], low[:, :half], high[:, :half], high[:, half : half + LANE]]
        raw = jnp.concatenate(raw, axis=1)
        blocks = [raw[:, j * LANE : (j + 1) * LANE] for j in range(count + 1)]
        before = jnp.concatenate(blocks[:-1], axis=0)
        after = jnp.concatenate(blocks[1:], axis=0)
        framed = jnp.concatenate([before, after], axis=1).astype(jnp.bfloat16)
        value = jnp.dot(framed, fir_tile(taps_ref[...]), preferred_element_type=jnp.float32)
        total = jnp.zeros((NS, LANE), jnp.float32)
        first_kept = [
            off_ref[jnp.maximum(chip - 1, 0)],
            off_ref[chip],
            off_ref[jnp.minimum(chip + 1, chips - 1)],
        ]
        for j in range(count):
            piece = value[j * NS : (j + 1) * NS, :]
            start = j * LANE - MAXLAG
            window = start // WIN
            if window == 0:
                total = total + piece * piece
            place = lax.broadcasted_iota(jnp.int32, (1, LANE), 1) + (start - window * WIN)
            keep = jnp.where(place >= first_kept[window + 1], 1.0, 0.0)
            if window < 0:
                keep = keep * jnp.where(chip > 0, 1.0, 0.0)
            if window > 0:
                keep = keep * jnp.where(chip < chips - 1, 1.0, 0.0)
            out_ref[:, j * LANE : (j + 1) * LANE] = piece * keep
        lines = []
        for r in range(power_ref.shape[0] // LANE):
            turned = power_ref[r * LANE : (r + 1) * LANE, :].T
            lines.append(jnp.sum(turned, axis=0, keepdims=True))
        repeated = jnp.concatenate([total] * SHIFTS, axis=0)
        lines.append(jnp.sum(repeated.T, axis=0, keepdims=True))
        lines.append(jnp.zeros((8 - len(lines), LANE), jnp.float32))
        energy = jnp.concatenate(lines, axis=0)
        energy_ref[...] = jnp.broadcast_to(energy[None], energy_ref.shape)

    return call(
        kernel,
        "filter_sources",
        [shape((NS, length), jnp.float32), shape((chips, 8, LANE), jnp.float32)],
        [SMEM, VMEM, VMEM, VMEM, VMEM],
        moved=MIB,
    )(offsets, taps, mine, other, power)


def lag_products(white, table_ref, pairs, keep_ref, send_ref, half_groups):
    rows, depth = white.shape
    sub = rows // half_groups // 2
    own_low = (lax.axis_index("tm") // 2) % 2 == 0
    for place, pair in enumerate(pairs):
        offset = pair * 2 * SHIFTS
        left = table_ref[offset : offset + depth, :]
        right = table_ref[offset + SHIFTS : offset + SHIFTS + depth, :]
        lags = jnp.concatenate([left, right], axis=1)
        value = jnp.dot(white[...], lags, preferred_element_type=jnp.float32)
        value = value.reshape(half_groups, 2, sub, 2 * LANE)
        low, high = value[:, 0], value[:, 1]
        cols = slice(place * 2 * LANE, (place + 1) * 2 * LANE)
        keep_ref[:, :, cols] = jnp.where(own_low, low, high)
        send_ref[:, :, cols] = jnp.where(own_low, high, low).astype(jnp.bfloat16)


def correlate_first(energies, traces, rows, pairs, half_groups, total_samples):
    channels, depth = rows.shape
    length = traces.shape[1]
    chunk = 1024
    loads = depth // chunk

    def kernel(
        energy_ref, traces_ref, rows_ref, keep_ref, send_ref, white, table, buf, shifted, sems
    ):
        copies = []
        for i in range(loads):
            cols = pl.ds(i * chunk, chunk)
            copies.append(pltpu.make_async_copy(rows_ref.at[:, cols], buf.at[i], sems.at[i]))
        for copy in copies:
            copy.start()
        energy = jnp.sum(energy_ref[...], axis=0)
        scale = lax.rsqrt(energy / total_samples + EPS)
        padded = jnp.concatenate([scale, jnp.zeros((LANE - 8, LANE), jnp.float32)], axis=0)
        turned = padded.T
        parts = channels // LANE
        gain = jnp.concatenate([turned[:, r : r + 1] for r in range(parts)], axis=0)
        trace = traces_ref[...] * turned[:NS, parts : parts + 1]
        trace = trace.astype(jnp.bfloat16).astype(jnp.float32)
        for b in range(SHIFTS):
            moved = trace if b == 0 else pltpu.roll(trace, length - b, 1)
            shifted[b * NS : (b + 1) * NS, :] = moved
        for j in range(length // LANE):
            cols = slice(j * LANE, (j + 1) * LANE)
            table[cols, :] = shifted[:, cols].T.astype(jnp.bfloat16)
        for i in range(loads):
            copies[i].wait()
            white[:, i * chunk : (i + 1) * chunk] = (buf[i] * gain).astype(jnp.bfloat16)
        lag_products(white, table, pairs, keep_ref, send_ref, half_groups)

    sub = channels // half_groups // 2
    cols = len(pairs) * 2 * LANE
    return call(
        kernel,
        "correlate_first",
        [
            shape((half_groups, sub, cols), jnp.float32),
            shape((half_groups, sub, cols), jnp.bfloat16),
            shape((channels, depth), jnp.bfloat16),
            shape((length, LANE), jnp.bfloat16),
        ],
        [VMEM, VMEM, ANY],
        [
            pltpu.VMEM((loads, channels, chunk), jnp.float32),
            pltpu.VMEM((LANE, length), jnp.float32),
            pltpu.SemaphoreType.DMA((loads,)),
        ],
        limit=40,
        flops=2 * channels * depth * cols,
        moved=16 * MIB,
    )(energies, traces, rows)


def correlate_next(white, table, pairs, half_groups):
    channels, depth = white.shape

    def kernel(white_ref, table_ref, keep_ref, send_ref):
        lag_products(white_ref, table_ref, pairs, keep_ref, send_ref, half_groups)

    sub = channels // half_groups // 2
    cols = len(pairs) * 2 * LANE
    return call(
        kernel,
        "correlate_next",
        [
            shape((half_groups, sub, cols), jnp.float32),
            shape((half_groups, sub, cols), jnp.bfloat16),
        ],
        [VMEM, VMEM],
        flops=2 * channels * depth * cols,
        moved=8 * MIB,
    )(white, table)


def add_line(keeps, arrivals):
    groups, sub, _ = keeps[0].shape
    widths = [keep.shape[2] for keep in keeps]
    count = len(keeps)

    def kernel(*refs):
        start = 0
        for keep_ref, across_ref, width in zip(refs[:count], refs[count : 2 * count], widths):
            value = keep_ref[...] + across_ref[...].astype(jnp.float32)
            refs[-1][:, :, start : start + width] = value.astype(jnp.bfloat16)
            start += width

    return call(
        kernel,
        "add_line",
        [shape((groups, sub, sum(widths)), jnp.bfloat16)],
        [VMEM] * (2 * count),
        moved=MIB,
    )(*keeps, *arrivals)[0]


def finish(parts, factor):
    count, sub, cols = parts.shape

    def kernel(parts_ref, out_ref, turned):
        blank = jnp.zeros((LANE - sub, LANE), jnp.float32)
        value = parts_ref[0].astype(jnp.float32)
        for i in range(1, count):
            value = value + parts_ref[i].astype(jnp.float32)
        value = value * factor
        for j in range(cols // LANE):
            block = jnp.concatenate([value[:, j * LANE : (j + 1) * LANE], blank], axis=0)
            turned[j * LANE : (j + 1) * LANE, :] = block.T
        for m in range(NS):
            for j in range(LAGS // LANE):
                block = turned[pl.ds(j * LANE * NS + m, LANE, stride=NS), :]
                out_ref[:, m // SB, m % SB, j * LANE : (j + 1) * LANE] = block.T[:sub]

    return call(
        kernel,
        "finish",
        [shape((sub, NSRC, SB, LAGS), jnp.float32)],
        [VMEM],
        [pltpu.VMEM((NS * LAGS, LANE), jnp.float32)],
        moved=MIB,
    )(parts)[0]


def shards(strain_rate, whiten_taps, source_channels, window_offsets):
    channels, samples = strain_rate.shape
    tiles = lax.axis_size("tm")
    groups_chan = lax.axis_size("chan")
    total_samples = samples * tiles
    chips = tiles // 2
    sub = channels // tiles
    taps = wide_taps(whiten_taps)

    x4 = strain_rate.reshape(chips, 2, sub, samples)
    own, edge, high, away = pick_sources(source_channels, x4)

    swap = [(i, i ^ 1) for i in range(tiles)]
    to_next = [(2 * k - 1, 2 * k) for k in range(1, chips)]
    both_next = to_next + [(b, a) for a, b in to_next]
    edge = lax.ppermute(edge, "tm", both_next)
    other = lax.ppermute(away, "tm", swap)
    high = lax.ppermute(high, "tm", [(2 * k - 1, 2 * k + 1) for k in range(1, chips)])

    edge, high = lax.optimization_barrier((edge, high))
    piece = extend_sources(own, edge)
    parts = [
        lax.ppermute(piece, "chan", [(i, (i + 2 * d) % groups_chan) for i in range(groups_chan)])
        for d in range(1, groups_chan // 2)
    ]
    piece = add_pieces(piece, *parts)
    arrived = lax.ppermute(piece, "chan", [(i, i ^ 1) for i in range(groups_chan)])
    filtered, power = filter_rows(window_offsets, taps, x4, other, edge, high)
    arrived, power = lax.optimization_barrier((arrived, power))
    piece = add_pieces(piece, arrived)
    piece_other = lax.ppermute(piece, "tm", swap)
    traces, energy = filter_sources(window_offsets, taps, piece, piece_other, power, chips)
    same = [[2 * k + c for k in range(chips)] for c in range(2)]
    energies = lax.all_to_all(energy, "tm", 0, 0, tiled=True, axis_index_groups=same)

    column = tiles // 4
    dots = LAGS // (2 * SHIFTS)
    first, second = range(dots // 2), range(dots // 2, dots)
    keep_a, send_a, white, table = correlate_first(
        energies, traces, filtered, first, column, total_samples
    )
    line = [(i, i ^ 2) for i in range(tiles)]
    across_a = lax.ppermute(send_a, "tm", line)
    keep_b, send_b = correlate_next(white, table, second, column)
    across_b = lax.ppermute(send_b, "tm", line)
    summed = add_line([keep_a, keep_b], [across_a, across_b])
    columns = [[4 * z + r for z in range(column)] for r in range(4)]
    parts = lax.all_to_all(summed, "tm", 0, 0, tiled=True, axis_index_groups=columns)
    return finish(parts, 1.0 / math.sqrt(total_samples))


def solution(mesh):
    return jax.shard_map(
        shards,
        mesh=mesh,
        in_specs=(P("chan", "tm"), P(), P(), P()),
        out_specs=P(("chan", "tm"), None, None, None),
        check_vma=False,
    )
```

```python
import math

import jax
import jax.numpy as jnp
from jax import lax
from jax.experimental import pallas as pl
from jax.experimental.pallas import tpu as pltpu
from jax.sharding import PartitionSpec as P

TAPS = 64
MAXLAG = 128
LAGS = 256
NSRC = 2
SB = 4
NS = NSRC * SB
WIN = 8192
LANE = 128
SHIFTS = 16
LEFT = 256
EPS = 1e-05
MIB = 1024 * 1024

VMEM = pl.BlockSpec(memory_space=pltpu.VMEM)
SMEM = pl.BlockSpec(memory_space=pltpu.SMEM)
ANY = pl.BlockSpec(memory_space=pl.ANY)


def call(
    kernel, name, out, in_specs, scratch=(), out_specs=None, limit=16, flops=0, moved=0, aliases=None
):
    return pl.pallas_call(
        kernel,
        out_shape=out,
        in_specs=in_specs,
        out_specs=out_specs or [VMEM] * len(out),
        scratch_shapes=list(scratch),
        input_output_aliases=aliases or {},
        compiler_params=pltpu.CompilerParams(vmem_limit_bytes=limit * MIB),
        cost_estimate=pl.CostEstimate(flops=flops, bytes_accessed=moved, transcendentals=0),
        name=name,
    )


def shape(dims, dtype):
    return jax.ShapeDtypeStruct(dims, dtype)


def fir_tile(taps):
    wide = jnp.broadcast_to(taps.astype(jnp.float32), (2 * LANE, 2 * LANE))
    rolled = pltpu.roll(wide, LANE, 1, stride=1, stride_axis=0)
    return rolled[:, :LANE].astype(jnp.bfloat16)


def wide_taps(taps):
    return jnp.pad(taps, (0, 2 * LANE - TAPS)).reshape(1, 2 * LANE)


def pick_sources(source_channels, x4):
    groups, _, sub, samples = x4.shape
    channels = groups * 2 * sub

    def kernel(ids_ref, x_ref, own_ref, edge_ref, high_ref, away_ref, buf, sems):
        base = lax.axis_index("chan") * channels
        core = lax.axis_index("tm") % 2
        copies = []
        inner = []
        for j in range(NS):
            local = ids_ref[j // SB, j % SB] - base
            owned = (local >= 0) & (local < channels)
            row = jnp.clip(local, 0, channels - 1)
            group, half = row // (2 * sub), (row // sub) % 2
            inner.append(jnp.where(owned, row % sub, -1))
            copies.append(pltpu.make_async_copy(x_ref.at[group, half], buf.at[j], sems.at[j]))
        last = pl.ds(samples - LANE, LANE)
        rest = [
            pltpu.make_async_copy(
                x_ref.at[:, 0, :, last], edge_ref.at[pl.ds(0, groups)], sems.at[NS]
            ),
            pltpu.make_async_copy(x_ref.at[:, 1, :, last], high_ref, sems.at[NS + 1]),
            pltpu.make_async_copy(x_ref.at[:, 1 - core], away_ref, sems.at[NS + 2]),
        ]
        for copy in copies + rest:
            copy.start()
        rows = lax.broadcasted_iota(jnp.int32, (sub, 1), 0)
        own = jnp.zeros((NS, samples), jnp.float32)
        for j in range(NS):
            copies[j].wait()
            picked = buf[j].astype(jnp.float32) * jnp.where(rows == inner[j], 1.0, 0.0)
            picked = picked[:NS] + picked[NS:]
            own = own + pltpu.roll(picked, (j + NS - inner[j] % NS) % NS, 0)
        own_ref[...] = own.astype(jnp.bfloat16)
        end = jnp.where(core == 1, own[:, samples - LEFT :], own[:, :LEFT])
        for copy in rest:
            copy.wait()
        edge_ref[groups] = jnp.concatenate(
            [end[:, :LANE], end[:, LANE:]], axis=0
        ).astype(jnp.bfloat16)

    return call(
        kernel,
        "pick_sources",
        [
            shape((NS, samples), jnp.bfloat16),
            shape((groups + 1, sub, LANE), jnp.bfloat16),
            shape((groups, sub, LANE), jnp.bfloat16),
            shape((groups, sub, samples), jnp.bfloat16),
        ],
        [SMEM, ANY],
        [pltpu.VMEM((NS, sub, samples), jnp.bfloat16), pltpu.SemaphoreType.DMA((NS + 3,))],
        limit=50,
        moved=2 * MIB,
    )(source_channels, x4)


def extend_sources(own, edge):
    samples = own.shape[1]
    groups = edge.shape[0] - 1

    def kernel(own_ref, edge_ref, out_ref):
        end = edge_ref[groups].astype(jnp.float32)
        joined = [own_ref[...].astype(jnp.float32), end[:NS], end[NS:]]
        out_ref[...] = jnp.concatenate(joined, axis=1).astype(jnp.bfloat16)

    return call(
        kernel,
        "extend_sources",
        [shape((NS, samples + LEFT), jnp.bfloat16)],
        [VMEM, VMEM],
    )(own, edge)[0]


def add_pieces(*pieces):
    def kernel(*refs):
        total = refs[0][...].astype(jnp.float32)
        for ref in refs[1:-1]:
            total = total + ref[...].astype(jnp.float32)
        refs[-1][...] = total.astype(jnp.bfloat16)

    return call(
        kernel,
        "add_pieces",
        [shape(pieces[0].shape, jnp.bfloat16)],
        [VMEM] * len(pieces),
    )(*pieces)[0]


def filter_rows(offsets, taps, x4, other, edge, high, first_group, groups, filled=None):
    all_groups, _, sub, half = x4.shape
    filled = [] if filled is None else [filled]
    rows = groups * sub
    chosen = slice(first_group, first_group + groups)
    chunk = 1024
    parts = half // chunk
    total = 2 * parts

    def kernel(
        off_ref, taps_ref, x_ref, other_ref, edge_ref, high_ref, *refs
    ):
        out_ref, power_ref, value_buf, sems = refs[len(filled) :]
        tile = lax.axis_index("tm")
        core = tile % 2
        matrix = fir_tile(taps_ref[...])
        first_kept = off_ref[tile // 2]

        def store(part):
            place = out_ref.at[pl.ds(first_group * sub, rows), pl.ds(part * chunk, chunk)]
            return pltpu.make_async_copy(value_buf.at[part], place, sems.at[part])

        def run(read_low, read_high, previous):
            power = jnp.zeros((rows, LANE), jnp.float32)
            for part in range(total):
                read = read_low if part < parts else read_high
                for j in range(chunk // LANE):
                    first = (part % parts) * chunk + j * LANE
                    current = read(slice(first, first + LANE)).reshape(rows, LANE)
                    framed = jnp.concatenate([previous, current], axis=1)
                    value = jnp.dot(framed, matrix, preferred_element_type=jnp.float32)
                    power = power + value * value
                    place = lax.broadcasted_iota(jnp.int32, (1, LANE), 1) + part * chunk + j * LANE
                    value = value * jnp.where(place >= first_kept, 1.0, 0.0)
                    value_buf[part, :, j * LANE : (j + 1) * LANE] = value
                    previous = current
                store(part).start()
            power_ref[...] = power

        def own(cols):
            return x_ref[chosen, core, :, cols]

        def swapped(cols):
            return other_ref[chosen, :, cols]

        @pl.when(core == 0)
        def _():
            run(own, swapped, edge_ref[chosen].reshape(rows, LANE))

        @pl.when(core == 1)
        def _():
            run(swapped, own, high_ref[chosen].reshape(rows, LANE))

        for part in range(total):
            store(part).wait()

    return call(
        kernel,
        "filter_rows",
        [shape((all_groups * sub, 2 * half), jnp.float32), shape((rows, LANE), jnp.float32)],
        [SMEM, VMEM, VMEM, VMEM, VMEM, VMEM] + [ANY] * len(filled),
        [pltpu.VMEM((total, rows, chunk), jnp.float32), pltpu.SemaphoreType.DMA((total,))],
        out_specs=[ANY, VMEM],
        limit=40,
        flops=2 * rows * 2 * half * 512,
        moved=6 * MIB,
        aliases={6: 0} if filled else None,
    )(offsets, taps, x4, other, edge, high, *filled)


def filter_sources(offsets, taps, mine, other, powers, chips):
    length = WIN + 2 * MAXLAG
    count = length // LANE
    half = mine.shape[1] - LEFT

    def kernel(off_ref, taps_ref, mine_ref, other_ref, *refs):
        *power_refs, out_ref, energy_ref = refs
        tile = lax.axis_index("tm")
        core, chip = tile % 2, tile // 2
        mine_rows = mine_ref[...].astype(jnp.float32)
        other_rows = other_ref[...].astype(jnp.float32)
        low = jnp.where(core == 0, mine_rows, other_rows)
        high = jnp.where(core == 0, other_rows, mine_rows)
        raw = [low[:, half:], low[:, :half], high[:, :half], high[:, half : half + LANE]]
        raw = jnp.concatenate(raw, axis=1)
        blocks = [raw[:, j * LANE : (j + 1) * LANE] for j in range(count + 1)]
        before = jnp.concatenate(blocks[:-1], axis=0)
        after = jnp.concatenate(blocks[1:], axis=0)
        framed = jnp.concatenate([before, after], axis=1).astype(jnp.bfloat16)
        value = jnp.dot(framed, fir_tile(taps_ref[...]), preferred_element_type=jnp.float32)
        total = jnp.zeros((NS, LANE), jnp.float32)
        first_kept = [
            off_ref[jnp.maximum(chip - 1, 0)],
            off_ref[chip],
            off_ref[jnp.minimum(chip + 1, chips - 1)],
        ]
        for j in range(count):
            piece = value[j * NS : (j + 1) * NS, :]
            start = j * LANE - MAXLAG
            window = start // WIN
            if window == 0:
                total = total + piece * piece
            place = lax.broadcasted_iota(jnp.int32, (1, LANE), 1) + (start - window * WIN)
            keep = jnp.where(place >= first_kept[window + 1], 1.0, 0.0)
            if window < 0:
                keep = keep * jnp.where(chip > 0, 1.0, 0.0)
            if window > 0:
                keep = keep * jnp.where(chip < chips - 1, 1.0, 0.0)
            out_ref[:, j * LANE : (j + 1) * LANE] = piece * keep
        lines = []
        for power_ref in power_refs:
            lines.append(jnp.sum(power_ref[...].T, axis=0, keepdims=True))
        repeated = jnp.concatenate([total] * SHIFTS, axis=0)
        lines.append(jnp.sum(repeated.T, axis=0, keepdims=True))
        lines.append(jnp.zeros((8 - len(lines), LANE), jnp.float32))
        energy = jnp.concatenate(lines, axis=0)
        energy_ref[...] = jnp.broadcast_to(energy[None], energy_ref.shape)

    return call(
        kernel,
        "filter_sources",
        [shape((NS, length), jnp.float32), shape((chips, 8, LANE), jnp.float32)],
        [SMEM, VMEM, VMEM, VMEM] + [VMEM] * len(powers),
        moved=MIB,
    )(offsets, taps, mine, other, *powers)


def lag_products(white, table_ref, pairs, keep_ref, send_ref, half_groups):
    rows, depth = white.shape
    sub = rows // half_groups // 2
    own_low = (lax.axis_index("tm") // 2) % 2 == 0
    for place, pair in enumerate(pairs):
        offset = pair * 2 * SHIFTS
        left = table_ref[offset : offset + depth, :]
        right = table_ref[offset + SHIFTS : offset + SHIFTS + depth, :]
        lags = jnp.concatenate([left, right], axis=1)
        value = jnp.dot(white[...], lags, preferred_element_type=jnp.float32)
        value = value.reshape(half_groups, 2, sub, 2 * LANE)
        low, high = value[:, 0], value[:, 1]
        cols = slice(place * 2 * LANE, (place + 1) * 2 * LANE)
        keep_ref[:, :, cols] = jnp.where(own_low, low, high)
        send_ref[:, :, cols] = jnp.where(own_low, high, low).astype(jnp.bfloat16)


def correlate_first(energies, traces, row_blocks, pairs, half_groups, total_samples):
    block_rows, depth = row_blocks[0].shape
    parts = len(row_blocks)
    channels = block_rows * parts
    length = traces.shape[1]
    chunk = 1024
    loads = depth // chunk

    def kernel(energy_ref, traces_ref, *refs):
        row_refs = refs[:parts]
        keep_ref, send_ref, white, table, buf, shifted, sems = refs[parts:]
        copies = []
        for i in range(loads):
            for r, rows_ref in enumerate(row_refs):
                source = rows_ref.at[:, pl.ds(i * chunk, chunk)]
                place = buf.at[i, pl.ds(r * block_rows, block_rows)]
                copies.append(pltpu.make_async_copy(source, place, sems.at[i * parts + r]))
        for copy in copies:
            copy.start()
        energy = jnp.sum(energy_ref[...], axis=0)
        scale = lax.rsqrt(energy / total_samples + EPS)
        padded = jnp.concatenate([scale, jnp.zeros((LANE - 8, LANE), jnp.float32)], axis=0)
        turned = padded.T
        blocks = channels // LANE
        gain = jnp.concatenate([turned[:, r : r + 1] for r in range(blocks)], axis=0)
        trace = traces_ref[...] * turned[:NS, blocks : blocks + 1]
        trace = trace.astype(jnp.bfloat16).astype(jnp.float32)
        for b in range(SHIFTS):
            moved = trace if b == 0 else pltpu.roll(trace, length - b, 1)
            shifted[b * NS : (b + 1) * NS, :] = moved
        for j in range(length // LANE):
            cols = slice(j * LANE, (j + 1) * LANE)
            table[cols, :] = shifted[:, cols].T.astype(jnp.bfloat16)
        for i in range(loads):
            for copy in copies[i * parts : (i + 1) * parts]:
                copy.wait()
            white[:, i * chunk : (i + 1) * chunk] = (buf[i] * gain).astype(jnp.bfloat16)
        lag_products(white, table, pairs, keep_ref, send_ref, half_groups)

    sub = channels // half_groups // 2
    cols = len(pairs) * 2 * LANE
    return call(
        kernel,
        "correlate_first",
        [
            shape((half_groups, sub, cols), jnp.float32),
            shape((half_groups, sub, cols), jnp.bfloat16),
            shape((channels, depth), jnp.bfloat16),
            shape((length, LANE), jnp.bfloat16),
        ],
        [VMEM, VMEM] + [ANY] * parts,
        [
            pltpu.VMEM((loads, channels, chunk), jnp.float32),
            pltpu.VMEM((LANE, length), jnp.float32),
            pltpu.SemaphoreType.DMA((loads * parts,)),
        ],
        limit=40,
        flops=2 * channels * depth * cols,
        moved=16 * MIB,
    )(energies, traces, *row_blocks)


def correlate_next(white, table, pairs, half_groups):
    channels, depth = white.shape

    def kernel(white_ref, table_ref, keep_ref, send_ref):
        lag_products(white_ref, table_ref, pairs, keep_ref, send_ref, half_groups)

    sub = channels // half_groups // 2
    cols = len(pairs) * 2 * LANE
    return call(
        kernel,
        "correlate_next",
        [
            shape((half_groups, sub, cols), jnp.float32),
            shape((half_groups, sub, cols), jnp.bfloat16),
        ],
        [VMEM, VMEM],
        flops=2 * channels * depth * cols,
        moved=8 * MIB,
    )(white, table)


def add_line(keeps, arrivals):
    groups, sub, _ = keeps[0].shape
    widths = [keep.shape[2] for keep in keeps]
    count = len(keeps)

    def kernel(*refs):
        start = 0
        for keep_ref, across_ref, width in zip(refs[:count], refs[count : 2 * count], widths):
            value = keep_ref[...] + across_ref[...].astype(jnp.float32)
            refs[-1][:, :, start : start + width] = value.astype(jnp.bfloat16)
            start += width

    return call(
        kernel,
        "add_line",
        [shape((groups, sub, sum(widths)), jnp.bfloat16)],
        [VMEM] * (2 * count),
        moved=MIB,
    )(*keeps, *arrivals)[0]


def finish(parts, factor):
    count, sub, cols = parts.shape

    def kernel(parts_ref, out_ref, turned):
        blank = jnp.zeros((LANE - sub, LANE), jnp.float32)
        value = parts_ref[0].astype(jnp.float32)
        for i in range(1, count):
            value = value + parts_ref[i].astype(jnp.float32)
        value = value * factor
        for j in range(cols // LANE):
            block = jnp.concatenate([value[:, j * LANE : (j + 1) * LANE], blank], axis=0)
            turned[j * LANE : (j + 1) * LANE, :] = block.T
        for m in range(NS):
            for j in range(LAGS // LANE):
                block = turned[pl.ds(j * LANE * NS + m, LANE, stride=NS), :]
                out_ref[:, m // SB, m % SB, j * LANE : (j + 1) * LANE] = block.T[:sub]

    return call(
        kernel,
        "finish",
        [shape((sub, NSRC, SB, LAGS), jnp.float32)],
        [VMEM],
        [pltpu.VMEM((NS * LAGS, LANE), jnp.float32)],
        moved=MIB,
    )(parts)[0]


def shards(strain_rate, whiten_taps, source_channels, window_offsets):
    channels, samples = strain_rate.shape
    tiles = lax.axis_size("tm")
    groups_chan = lax.axis_size("chan")
    total_samples = samples * tiles
    chips = tiles // 2
    sub = channels // tiles
    taps = wide_taps(whiten_taps)

    x4 = strain_rate.reshape(chips, 2, sub, samples)
    own, edge, high, away = pick_sources(source_channels, x4)

    swap = [(i, i ^ 1) for i in range(tiles)]
    to_next = [(2 * k - 1, 2 * k) for k in range(1, chips)]
    both_next = to_next + [(b, a) for a, b in to_next]
    edge = lax.ppermute(edge, "tm", both_next)
    other = lax.ppermute(away, "tm", swap)
    high = lax.ppermute(high, "tm", [(2 * k - 1, 2 * k + 1) for k in range(1, chips)])

    edge, high = lax.optimization_barrier((edge, high))
    piece = extend_sources(own, edge)
    parts = [
        lax.ppermute(piece, "chan", [(i, (i + 2 * d) % groups_chan) for i in range(groups_chan)])
        for d in range(1, groups_chan // 2)
    ]
    half = chips // 2
    filtered, power_a = filter_rows(window_offsets, taps, x4, other, edge, high, 0, half)
    *parts, power_a = lax.optimization_barrier((*parts, power_a))
    piece = add_pieces(piece, *parts)
    arrived = lax.ppermute(piece, "chan", [(i, i ^ 1) for i in range(groups_chan)])
    filtered, power_b = filter_rows(
        window_offsets, taps, x4, other, edge, high, half, half, filtered
    )
    arrived, power_b = lax.optimization_barrier((arrived, power_b))
    piece = add_pieces(piece, arrived)
    piece_other = lax.ppermute(piece, "tm", swap)
    traces, energy = filter_sources(
        window_offsets, taps, piece, piece_other, [power_a, power_b], chips
    )
    same = [[2 * k + c for k in range(chips)] for c in range(2)]
    energies = lax.all_to_all(energy, "tm", 0, 0, tiled=True, axis_index_groups=same)

    column = tiles // 4
    dots = LAGS // (2 * SHIFTS)
    splits = [range(0, dots // 4), range(dots // 4, dots * 5 // 8), range(dots * 5 // 8, dots)]
    line = [(i, i ^ 2) for i in range(tiles)]
    keep, send, white, table = correlate_first(
        energies, traces, [filtered], splits[0], column, total_samples
    )
    keeps, arrivals = [keep], [lax.ppermute(send, "tm", line)]
    for pairs in splits[1:]:
        if len(keeps) > 1:
            white, arrivals[-2] = lax.optimization_barrier((white, arrivals[-2]))
        keep, send = correlate_next(white, table, pairs, column)
        keeps.append(keep)
        arrivals.append(lax.ppermute(send, "tm", line))
    summed = add_line(keeps, arrivals)
    columns = [[4 * z + r for z in range(column)] for r in range(4)]
    parts = lax.all_to_all(summed, "tm", 0, 0, tiled=True, axis_index_groups=columns)
    return finish(parts, 1.0 / math.sqrt(total_samples))


def solution(mesh):
    return jax.shard_map(
        shards,
        mesh=mesh,
        in_specs=(P("chan", "tm"), P(), P(), P()),
        out_specs=P(("chan", "tm"), None, None, None),
        check_vma=False,
    )
```

```python
import math

import jax
import jax.numpy as jnp
from jax import lax
from jax.experimental import pallas as pl
from jax.experimental.pallas import tpu as pltpu
from jax.sharding import PartitionSpec as P

TAPS = 64
MAXLAG = 128
LAGS = 256
NSRC = 2
SB = 4
NS = NSRC * SB
WIN = 8192
LANE = 128
SHIFTS = 16
LEFT = 256
EPS = 1e-05
MIB = 1024 * 1024

VMEM = pl.BlockSpec(memory_space=pltpu.VMEM)
SMEM = pl.BlockSpec(memory_space=pltpu.SMEM)
ANY = pl.BlockSpec(memory_space=pl.ANY)


def call(
    kernel, name, out, in_specs, scratch=(), out_specs=None, limit=16, flops=0, moved=0, aliases=None
):
    return pl.pallas_call(
        kernel,
        out_shape=out,
        in_specs=in_specs,
        out_specs=out_specs or [VMEM] * len(out),
        scratch_shapes=list(scratch),
        input_output_aliases=aliases or {},
        compiler_params=pltpu.CompilerParams(vmem_limit_bytes=limit * MIB),
        cost_estimate=pl.CostEstimate(flops=flops, bytes_accessed=moved, transcendentals=0),
        name=name,
    )


def shape(dims, dtype):
    return jax.ShapeDtypeStruct(dims, dtype)


def fir_tile(taps):
    wide = jnp.broadcast_to(taps.astype(jnp.float32), (2 * LANE, 2 * LANE))
    rolled = pltpu.roll(wide, LANE, 1, stride=1, stride_axis=0)
    return rolled[:, :LANE].astype(jnp.bfloat16)


def wide_taps(taps):
    return jnp.pad(taps, (0, 2 * LANE - TAPS)).reshape(1, 2 * LANE)


def pick_sources(source_channels, x4):
    groups, _, sub, samples = x4.shape
    channels = groups * 2 * sub

    def kernel(ids_ref, x_ref, own_ref, tail_ref, away_ref, buf, sems):
        base = lax.axis_index("chan") * channels
        core = lax.axis_index("tm") % 2
        copies = []
        inner = []
        for j in range(NS):
            local = ids_ref[j // SB, j % SB] - base
            owned = (local >= 0) & (local < channels)
            row = jnp.clip(local, 0, channels - 1)
            group, half = row // (2 * sub), (row // sub) % 2
            inner.append(jnp.where(owned, row % sub, -1))
            copies.append(pltpu.make_async_copy(x_ref.at[group, half], buf.at[j], sems.at[j]))
        last = pl.ds(samples - LANE, LANE)
        rest = [
            pltpu.make_async_copy(x_ref.at[:, :, :, last], tail_ref, sems.at[NS]),
            pltpu.make_async_copy(x_ref.at[:, 1 - core], away_ref, sems.at[NS + 1]),
        ]
        for copy in copies + rest:
            copy.start()
        rows = lax.broadcasted_iota(jnp.int32, (sub, 1), 0)
        own = jnp.zeros((NS, samples), jnp.float32)
        for j in range(NS):
            copies[j].wait()
            picked = buf[j].astype(jnp.float32) * jnp.where(rows == inner[j], 1.0, 0.0)
            picked = picked[:NS] + picked[NS:]
            own = own + pltpu.roll(picked, (j + NS - inner[j] % NS) % NS, 0)
        own_ref[...] = own.astype(jnp.bfloat16)
        for copy in rest:
            copy.wait()

    return call(
        kernel,
        "pick_sources",
        [
            shape((NS, samples), jnp.bfloat16),
            shape((groups, 2, sub, LANE), jnp.bfloat16),
            shape((groups, sub, samples), jnp.bfloat16),
        ],
        [SMEM, ANY],
        [pltpu.VMEM((NS, sub, samples), jnp.bfloat16), pltpu.SemaphoreType.DMA((NS + 2,))],
        limit=50,
        moved=4 * MIB,
    )(source_channels, x4)


def join_sources(piece, arrived):
    samples = piece.shape[1]

    def kernel(piece_ref, arrived_ref, out_ref, end_ref):
        core = lax.axis_index("tm") % 2
        total = piece_ref[...].astype(jnp.float32) + arrived_ref[...].astype(jnp.float32)
        out_ref[...] = total.astype(jnp.bfloat16)
        end = jnp.where(core == 1, total[:, samples - LEFT :], total[:, :LEFT])
        end_ref[...] = end.astype(jnp.bfloat16)

    return call(
        kernel,
        "join_sources",
        [shape(piece.shape, jnp.bfloat16), shape((NS, LEFT), jnp.bfloat16)],
        [VMEM, VMEM],
    )(piece, arrived)


def extend_sources(piece, edge):
    samples = piece.shape[1]

    def kernel(piece_ref, edge_ref, out_ref):
        out_ref[:, :samples] = piece_ref[...]
        out_ref[:, samples:] = edge_ref[...]

    return call(
        kernel,
        "extend_sources",
        [shape((NS, samples + LEFT), jnp.bfloat16)],
        [VMEM, VMEM],
    )(piece, edge)[0]


def add_pieces(*pieces):
    def kernel(*refs):
        total = refs[0][...].astype(jnp.float32)
        for ref in refs[1:-1]:
            total = total + ref[...].astype(jnp.float32)
        refs[-1][...] = total.astype(jnp.bfloat16)

    return call(
        kernel,
        "add_pieces",
        [shape(pieces[0].shape, jnp.bfloat16)],
        [VMEM] * len(pieces),
    )(*pieces)[0]


def filter_rows(offsets, taps, x4, other, edge, high, first_group, groups, filled=None):
    all_groups, _, sub, half = x4.shape
    filled = [] if filled is None else [filled]
    rows = groups * sub
    chosen = slice(first_group, first_group + groups)
    chunk = 1024
    parts = half // chunk
    total = 2 * parts

    def kernel(
        off_ref, taps_ref, x_ref, other_ref, edge_ref, high_ref, *refs
    ):
        out_ref, power_ref, value_buf, sems = refs[len(filled) :]
        tile = lax.axis_index("tm")
        core = tile % 2
        matrix = fir_tile(taps_ref[...])
        first_kept = off_ref[tile // 2]

        def store(part):
            place = out_ref.at[pl.ds(first_group * sub, rows), pl.ds(part * chunk, chunk)]
            return pltpu.make_async_copy(value_buf.at[part], place, sems.at[part])

        def run(read_low, read_high, previous):
            power = jnp.zeros((rows, LANE), jnp.float32)
            for part in range(total):
                read = read_low if part < parts else read_high
                for j in range(chunk // LANE):
                    first = (part % parts) * chunk + j * LANE
                    current = read(slice(first, first + LANE)).reshape(rows, LANE)
                    framed = jnp.concatenate([previous, current], axis=1)
                    value = jnp.dot(framed, matrix, preferred_element_type=jnp.float32)
                    power = power + value * value
                    place = lax.broadcasted_iota(jnp.int32, (1, LANE), 1) + part * chunk + j * LANE
                    value = value * jnp.where(place >= first_kept, 1.0, 0.0)
                    value_buf[part, :, j * LANE : (j + 1) * LANE] = value
                    previous = current
                store(part).start()
            power_ref[...] = power

        def own(cols):
            return x_ref[chosen, core, :, cols]

        def swapped(cols):
            return other_ref[chosen, :, cols]

        @pl.when(core == 0)
        def _():
            run(own, swapped, edge_ref[chosen, 0].reshape(rows, LANE))

        @pl.when(core == 1)
        def _():
            run(swapped, own, high_ref[chosen, 1].reshape(rows, LANE))

        for part in range(total):
            store(part).wait()

    return call(
        kernel,
        "filter_rows",
        [shape((all_groups * sub, 2 * half), jnp.float32), shape((rows, LANE), jnp.float32)],
        [SMEM, VMEM, VMEM, VMEM, VMEM, VMEM] + [ANY] * len(filled),
        [pltpu.VMEM((total, rows, chunk), jnp.float32), pltpu.SemaphoreType.DMA((total,))],
        out_specs=[ANY, VMEM],
        limit=40,
        flops=2 * rows * 2 * half * 512,
        moved=6 * MIB,
        aliases={6: 0} if filled else None,
    )(offsets, taps, x4, other, edge, high, *filled)


def filter_sources(offsets, taps, mine, other, powers, chips):
    length = WIN + 2 * MAXLAG
    count = length // LANE
    half = mine.shape[1] - LEFT

    def kernel(off_ref, taps_ref, mine_ref, other_ref, *refs):
        *power_refs, out_ref, energy_ref = refs
        tile = lax.axis_index("tm")
        core, chip = tile % 2, tile // 2
        mine_rows = mine_ref[...].astype(jnp.float32)
        other_rows = other_ref[...].astype(jnp.float32)
        low = jnp.where(core == 0, mine_rows, other_rows)
        high = jnp.where(core == 0, other_rows, mine_rows)
        raw = [low[:, half:], low[:, :half], high[:, :half], high[:, half : half + LANE]]
        raw = jnp.concatenate(raw, axis=1)
        blocks = [raw[:, j * LANE : (j + 1) * LANE] for j in range(count + 1)]
        before = jnp.concatenate(blocks[:-1], axis=0)
        after = jnp.concatenate(blocks[1:], axis=0)
        framed = jnp.concatenate([before, after], axis=1).astype(jnp.bfloat16)
        value = jnp.dot(framed, fir_tile(taps_ref[...]), preferred_element_type=jnp.float32)
        total = jnp.zeros((NS, LANE), jnp.float32)
        first_kept = [
            off_ref[jnp.maximum(chip - 1, 0)],
            off_ref[chip],
            off_ref[jnp.minimum(chip + 1, chips - 1)],
        ]
        for j in range(count):
            piece = value[j * NS : (j + 1) * NS, :]
            start = j * LANE - MAXLAG
            window = start // WIN
            if window == 0:
                total = total + piece * piece
            place = lax.broadcasted_iota(jnp.int32, (1, LANE), 1) + (start - window * WIN)
            keep = jnp.where(place >= first_kept[window + 1], 1.0, 0.0)
            if window < 0:
                keep = keep * jnp.where(chip > 0, 1.0, 0.0)
            if window > 0:
                keep = keep * jnp.where(chip < chips - 1, 1.0, 0.0)
            out_ref[:, j * LANE : (j + 1) * LANE] = piece * keep
        lines = []
        for power_ref in power_refs:
            lines.append(jnp.sum(power_ref[...].T, axis=0, keepdims=True))
        repeated = jnp.concatenate([total] * SHIFTS, axis=0)
        lines.append(jnp.sum(repeated.T, axis=0, keepdims=True))
        lines.append(jnp.zeros((8 - len(lines), LANE), jnp.float32))
        energy = jnp.concatenate(lines, axis=0)
        energy_ref[...] = jnp.broadcast_to(energy[None], energy_ref.shape)

    return call(
        kernel,
        "filter_sources",
        [shape((NS, length), jnp.float32), shape((chips, 8, LANE), jnp.float32)],
        [SMEM, VMEM, VMEM, VMEM] + [VMEM] * len(powers),
        moved=MIB,
    )(offsets, taps, mine, other, *powers)


def lag_products(white, table_ref, pairs, keep_ref, send_ref, half_groups):
    rows, depth = white.shape
    sub = rows // half_groups // 2
    own_low = (lax.axis_index("tm") // 2) % 2 == 0
    for place, pair in enumerate(pairs):
        offset = pair * 2 * SHIFTS
        left = table_ref[offset : offset + depth, :]
        right = table_ref[offset + SHIFTS : offset + SHIFTS + depth, :]
        lags = jnp.concatenate([left, right], axis=1)
        value = jnp.dot(white[...], lags, preferred_element_type=jnp.float32)
        value = value.reshape(half_groups, 2, sub, 2 * LANE)
        low, high = value[:, 0], value[:, 1]
        cols = slice(place * 2 * LANE, (place + 1) * 2 * LANE)
        keep_ref[:, :, cols] = jnp.where(own_low, low, high)
        send_ref[:, :, cols] = jnp.where(own_low, high, low).astype(jnp.bfloat16)


def correlate_first(energies, traces, row_blocks, pairs, half_groups, total_samples):
    block_rows, depth = row_blocks[0].shape
    parts = len(row_blocks)
    channels = block_rows * parts
    length = traces.shape[1]
    chunk = 1024
    loads = depth // chunk

    def kernel(energy_ref, traces_ref, *refs):
        row_refs = refs[:parts]
        keep_ref, send_ref, white, table, buf, shifted, sems = refs[parts:]
        copies = []
        for i in range(loads):
            for r, rows_ref in enumerate(row_refs):
                source = rows_ref.at[:, pl.ds(i * chunk, chunk)]
                place = buf.at[i, pl.ds(r * block_rows, block_rows)]
                copies.append(pltpu.make_async_copy(source, place, sems.at[i * parts + r]))
        for copy in copies:
            copy.start()
        energy = jnp.sum(energy_ref[...], axis=0)
        scale = lax.rsqrt(energy / total_samples + EPS)
        padded = jnp.concatenate([scale, jnp.zeros((LANE - 8, LANE), jnp.float32)], axis=0)
        turned = padded.T
        blocks = channels // LANE
        gain = jnp.concatenate([turned[:, r : r + 1] for r in range(blocks)], axis=0)
        trace = traces_ref[...] * turned[:NS, blocks : blocks + 1]
        trace = trace.astype(jnp.bfloat16).astype(jnp.float32)
        for b in range(SHIFTS):
            moved = trace if b == 0 else pltpu.roll(trace, length - b, 1)
            shifted[b * NS : (b + 1) * NS, :] = moved
        for j in range(length // LANE):
            cols = slice(j * LANE, (j + 1) * LANE)
            table[cols, :] = shifted[:, cols].T.astype(jnp.bfloat16)
        for i in range(loads):
            for copy in copies[i * parts : (i + 1) * parts]:
                copy.wait()
            white[:, i * chunk : (i + 1) * chunk] = (buf[i] * gain).astype(jnp.bfloat16)
        lag_products(white, table, pairs, keep_ref, send_ref, half_groups)

    sub = channels // half_groups // 2
    cols = len(pairs) * 2 * LANE
    return call(
        kernel,
        "correlate_first",
        [
            shape((half_groups, sub, cols), jnp.float32),
            shape((half_groups, sub, cols), jnp.bfloat16),
            shape((channels, depth), jnp.bfloat16),
            shape((length, LANE), jnp.bfloat16),
        ],
        [VMEM, VMEM] + [ANY] * parts,
        [
            pltpu.VMEM((loads, channels, chunk), jnp.float32),
            pltpu.VMEM((LANE, length), jnp.float32),
            pltpu.SemaphoreType.DMA((loads * parts,)),
        ],
        limit=40,
        flops=2 * channels * depth * cols,
        moved=16 * MIB,
    )(energies, traces, *row_blocks)


def correlate_next(white, table, pairs, half_groups):
    channels, depth = white.shape

    def kernel(white_ref, table_ref, keep_ref, send_ref):
        lag_products(white_ref, table_ref, pairs, keep_ref, send_ref, half_groups)

    sub = channels // half_groups // 2
    cols = len(pairs) * 2 * LANE
    return call(
        kernel,
        "correlate_next",
        [
            shape((half_groups, sub, cols), jnp.float32),
            shape((half_groups, sub, cols), jnp.bfloat16),
        ],
        [VMEM, VMEM],
        flops=2 * channels * depth * cols,
        moved=8 * MIB,
    )(white, table)


def add_line(keeps, arrivals):
    groups, sub, _ = keeps[0].shape
    widths = [keep.shape[2] for keep in keeps]
    count = len(keeps)

    def kernel(*refs):
        start = 0
        for keep_ref, across_ref, width in zip(refs[:count], refs[count : 2 * count], widths):
            value = keep_ref[...] + across_ref[...].astype(jnp.float32)
            refs[-1][:, :, start : start + width] = value.astype(jnp.bfloat16)
            start += width

    return call(
        kernel,
        "add_line",
        [shape((groups, sub, sum(widths)), jnp.bfloat16)],
        [VMEM] * (2 * count),
        moved=MIB,
    )(*keeps, *arrivals)[0]


def finish(parts, factor):
    count, sub, cols = parts.shape

    def kernel(parts_ref, out_ref, turned):
        blank = jnp.zeros((LANE - sub, LANE), jnp.float32)
        value = parts_ref[0].astype(jnp.float32)
        for i in range(1, count):
            value = value + parts_ref[i].astype(jnp.float32)
        value = value * factor
        for j in range(cols // LANE):
            block = jnp.concatenate([value[:, j * LANE : (j + 1) * LANE], blank], axis=0)
            turned[j * LANE : (j + 1) * LANE, :] = block.T
        for m in range(NS):
            for j in range(LAGS // LANE):
                block = turned[pl.ds(j * LANE * NS + m, LANE, stride=NS), :]
                out_ref[:, m // SB, m % SB, j * LANE : (j + 1) * LANE] = block.T[:sub]

    return call(
        kernel,
        "finish",
        [shape((sub, NSRC, SB, LAGS), jnp.float32)],
        [VMEM],
        [pltpu.VMEM((NS * LAGS, LANE), jnp.float32)],
        moved=MIB,
    )(parts)[0]


def shards(strain_rate, whiten_taps, source_channels, window_offsets):
    channels, samples = strain_rate.shape
    tiles = lax.axis_size("tm")
    groups_chan = lax.axis_size("chan")
    total_samples = samples * tiles
    chips = tiles // 2
    sub = channels // tiles
    taps = wide_taps(whiten_taps)

    x4 = strain_rate.reshape(chips, 2, sub, samples)
    own, tail, away = pick_sources(source_channels, x4)

    swap = [(i, i ^ 1) for i in range(tiles)]
    to_next = [(2 * k - 1, 2 * k) for k in range(1, chips)]
    both_next = to_next + [(b, a) for a, b in to_next]
    other = lax.ppermute(away, "tm", swap)
    parts = [
        lax.ppermute(own, "chan", [(i, (i + 2 * d) % groups_chan) for i in range(groups_chan)])
        for d in range(1, groups_chan // 2)
    ]
    tail = lax.ppermute(tail, "tm", to_next)
    *parts, tail = lax.optimization_barrier((*parts, tail))
    tail_odd = lax.ppermute(tail, "tm", [(2 * k, 2 * k + 1) for k in range(chips)])
    piece = add_pieces(own, *parts)
    arrived = lax.ppermute(piece, "chan", [(i, i ^ 1) for i in range(groups_chan)])
    half = chips // 2
    filtered, power_a = filter_rows(window_offsets, taps, x4, other, tail, tail_odd, 0, half)
    arrived, power_a = lax.optimization_barrier((arrived, power_a))
    piece, end = join_sources(piece, arrived)
    edge = lax.ppermute(end, "tm", both_next)
    filtered, power_b = filter_rows(
        window_offsets, taps, x4, other, tail, tail_odd, half, half, filtered
    )
    edge, power_b = lax.optimization_barrier((edge, power_b))
    piece = extend_sources(piece, edge)
    piece_other = lax.ppermute(piece, "tm", swap)
    traces, energy = filter_sources(
        window_offsets, taps, piece, piece_other, [power_a, power_b], chips
    )
    same = [[2 * k + c for k in range(chips)] for c in range(2)]
    energies = lax.all_to_all(energy, "tm", 0, 0, tiled=True, axis_index_groups=same)

    column = tiles // 4
    dots = LAGS // (2 * SHIFTS)
    splits = [range(0, dots // 4), range(dots // 4, dots * 5 // 8), range(dots * 5 // 8, dots)]
    line = [(i, i ^ 2) for i in range(tiles)]
    keep, send, white, table = correlate_first(
        energies, traces, [filtered], splits[0], column, total_samples
    )
    keeps, arrivals = [keep], [lax.ppermute(send, "tm", line)]
    for pairs in splits[1:]:
        if len(keeps) > 1:
            white, arrivals[-2] = lax.optimization_barrier((white, arrivals[-2]))
        keep, send = correlate_next(white, table, pairs, column)
        keeps.append(keep)
        arrivals.append(lax.ppermute(send, "tm", line))
    summed = add_line(keeps, arrivals)
    columns = [[4 * z + r for z in range(column)] for r in range(4)]
    parts = lax.all_to_all(summed, "tm", 0, 0, tiled=True, axis_index_groups=columns)
    return finish(parts, 1.0 / math.sqrt(total_samples))


def solution(mesh):
    return jax.shard_map(
        shards,
        mesh=mesh,
        in_specs=(P("chan", "tm"), P(), P(), P()),
        out_specs=P(("chan", "tm"), None, None, None),
        check_vma=False,
    )
```

```python
import math

import jax
import jax.numpy as jnp
from jax import lax
from jax.experimental import pallas as pl
from jax.experimental.pallas import tpu as pltpu
from jax.sharding import PartitionSpec as P

TAPS = 64
MAXLAG = 128
LAGS = 256
NSRC = 2
SB = 4
NS = NSRC * SB
WIN = 8192
LANE = 128
SHIFTS = 16
LEFT = 256
EPS = 1e-05
MIB = 1024 * 1024

VMEM = pl.BlockSpec(memory_space=pltpu.VMEM)
SMEM = pl.BlockSpec(memory_space=pltpu.SMEM)
ANY = pl.BlockSpec(memory_space=pl.ANY)


def call(
    kernel, name, out, in_specs, scratch=(), out_specs=None, limit=16, flops=0, moved=0, aliases=None
):
    return pl.pallas_call(
        kernel,
        out_shape=out,
        in_specs=in_specs,
        out_specs=out_specs or [VMEM] * len(out),
        scratch_shapes=list(scratch),
        input_output_aliases=aliases or {},
        compiler_params=pltpu.CompilerParams(vmem_limit_bytes=limit * MIB),
        cost_estimate=pl.CostEstimate(flops=flops, bytes_accessed=moved, transcendentals=0),
        name=name,
    )


def shape(dims, dtype):
    return jax.ShapeDtypeStruct(dims, dtype)


def fir_tile(taps):
    wide = jnp.broadcast_to(taps.astype(jnp.float32), (2 * LANE, 2 * LANE))
    rolled = pltpu.roll(wide, LANE, 1, stride=1, stride_axis=0)
    return rolled[:, :LANE].astype(jnp.bfloat16)


def wide_taps(taps):
    return jnp.pad(taps, (0, 2 * LANE - TAPS)).reshape(1, 2 * LANE)


def pick_sources(source_channels, x4):
    groups, _, sub, samples = x4.shape
    channels = groups * 2 * sub

    def kernel(ids_ref, x_ref, own_ref, edge_ref, away_ref, buf, sems):
        base = lax.axis_index("chan") * channels
        core = lax.axis_index("tm") % 2
        copies = []
        inner = []
        for j in range(NS):
            local = ids_ref[j // SB, j % SB] - base
            owned = (local >= 0) & (local < channels)
            row = jnp.clip(local, 0, channels - 1)
            group, half = row // (2 * sub), (row // sub) % 2
            inner.append(jnp.where(owned, row % sub, -1))
            copies.append(pltpu.make_async_copy(x_ref.at[group, half], buf.at[j], sems.at[j]))
        last = pl.ds(samples - LANE, LANE)
        rest = [
            pltpu.make_async_copy(
                x_ref.at[:, 0, :, last], edge_ref.at[pl.ds(0, groups)], sems.at[NS]
            ),
            pltpu.make_async_copy(
                x_ref.at[:, 1, :, last], edge_ref.at[pl.ds(groups, groups)], sems.at[NS + 1]
            ),
            pltpu.make_async_copy(x_ref.at[:, 1 - core], away_ref, sems.at[NS + 2]),
        ]
        for copy in copies + rest:
            copy.start()
        rows = lax.broadcasted_iota(jnp.int32, (sub, 1), 0)
        own = jnp.zeros((NS, samples), jnp.float32)
        for j in range(NS):
            copies[j].wait()
            picked = buf[j].astype(jnp.float32) * jnp.where(rows == inner[j], 1.0, 0.0)
            picked = picked[:NS] + picked[NS:]
            own = own + pltpu.roll(picked, (j + NS - inner[j] % NS) % NS, 0)
        own_ref[...] = own.astype(jnp.bfloat16)
        end = jnp.where(core == 1, own[:, samples - LEFT :], own[:, :LEFT])
        for copy in rest:
            copy.wait()
        edge_ref[2 * groups] = jnp.concatenate(
            [end[:, :LANE], end[:, LANE:]], axis=0
        ).astype(jnp.bfloat16)

    return call(
        kernel,
        "pick_sources",
        [
            shape((NS, samples), jnp.bfloat16),
            shape((2 * groups + 1, sub, LANE), jnp.bfloat16),
            shape((groups, sub, samples), jnp.bfloat16),
        ],
        [SMEM, ANY],
        [pltpu.VMEM((NS, sub, samples), jnp.bfloat16), pltpu.SemaphoreType.DMA((NS + 3,))],
        limit=50,
        moved=2 * MIB,
    )(source_channels, x4)


def extend_sources(own, edge):
    samples = own.shape[1]
    groups = edge.shape[0] - 1

    def kernel(own_ref, edge_ref, out_ref):
        end = edge_ref[groups].astype(jnp.float32)
        joined = [own_ref[...].astype(jnp.float32), end[:NS], end[NS:]]
        out_ref[...] = jnp.concatenate(joined, axis=1).astype(jnp.bfloat16)

    return call(
        kernel,
        "extend_sources",
        [shape((NS, samples + LEFT), jnp.bfloat16)],
        [VMEM, VMEM],
    )(own, edge)[0]


def add_pieces(*pieces):
    def kernel(*refs):
        total = refs[0][...].astype(jnp.float32)
        for ref in refs[1:-1]:
            total = total + ref[...].astype(jnp.float32)
        refs[-1][...] = total.astype(jnp.bfloat16)

    return call(
        kernel,
        "add_pieces",
        [shape(pieces[0].shape, jnp.bfloat16)],
        [VMEM] * len(pieces),
    )(*pieces)[0]


def filter_rows(offsets, taps, x4, other, edge, high, first_group, groups, filled=None):
    all_groups, _, sub, half = x4.shape
    filled = [] if filled is None else [filled]
    rows = groups * sub
    chosen = slice(first_group, first_group + groups)
    chosen_high = slice(all_groups + first_group, all_groups + first_group + groups)
    chunk = 1024
    parts = half // chunk
    total = 2 * parts

    def kernel(
        off_ref, taps_ref, x_ref, other_ref, edge_ref, high_ref, *refs
    ):
        out_ref, power_ref, value_buf, sems = refs[len(filled) :]
        tile = lax.axis_index("tm")
        core = tile % 2
        matrix = fir_tile(taps_ref[...])
        first_kept = off_ref[tile // 2]

        def store(part):
            place = out_ref.at[pl.ds(first_group * sub, rows), pl.ds(part * chunk, chunk)]
            return pltpu.make_async_copy(value_buf.at[part], place, sems.at[part])

        def run(read_low, read_high, previous):
            power = jnp.zeros((rows, LANE), jnp.float32)
            for part in range(total):
                read = read_low if part < parts else read_high
                for j in range(chunk // LANE):
                    first = (part % parts) * chunk + j * LANE
                    current = read(slice(first, first + LANE)).reshape(rows, LANE)
                    framed = jnp.concatenate([previous, current], axis=1)
                    value = jnp.dot(framed, matrix, preferred_element_type=jnp.float32)
                    power = power + value * value
                    place = lax.broadcasted_iota(jnp.int32, (1, LANE), 1) + part * chunk + j * LANE
                    value = value * jnp.where(place >= first_kept, 1.0, 0.0)
                    value_buf[part, :, j * LANE : (j + 1) * LANE] = value
                    previous = current
                store(part).start()
            power_ref[...] = power

        def own(cols):
            return x_ref[chosen, core, :, cols]

        def swapped(cols):
            return other_ref[chosen, :, cols]

        @pl.when(core == 0)
        def _():
            run(own, swapped, edge_ref[chosen].reshape(rows, LANE))

        @pl.when(core == 1)
        def _():
            run(swapped, own, high_ref[chosen_high].reshape(rows, LANE))

        for part in range(total):
            store(part).wait()

    return call(
        kernel,
        "filter_rows",
        [shape((all_groups * sub, 2 * half), jnp.float32), shape((rows, LANE), jnp.float32)],
        [SMEM, VMEM, VMEM, VMEM, VMEM, VMEM] + [ANY] * len(filled),
        [pltpu.VMEM((total, rows, chunk), jnp.float32), pltpu.SemaphoreType.DMA((total,))],
        out_specs=[ANY, VMEM],
        limit=40,
        flops=2 * rows * 2 * half * 512,
        moved=6 * MIB,
        aliases={6: 0} if filled else None,
    )(offsets, taps, x4, other, edge, high, *filled)


def filter_sources(offsets, taps, mine, other, powers, chips):
    length = WIN + 2 * MAXLAG
    count = length // LANE
    half = mine.shape[1] - LEFT

    def kernel(off_ref, taps_ref, mine_ref, other_ref, *refs):
        *power_refs, out_ref, energy_ref = refs
        tile = lax.axis_index("tm")
        core, chip = tile % 2, tile // 2
        mine_rows = mine_ref[...].astype(jnp.float32)
        other_rows = other_ref[...].astype(jnp.float32)
        low = jnp.where(core == 0, mine_rows, other_rows)
        high = jnp.where(core == 0, other_rows, mine_rows)
        raw = [low[:, half:], low[:, :half], high[:, :half], high[:, half : half + LANE]]
        raw = jnp.concatenate(raw, axis=1)
        blocks = [raw[:, j * LANE : (j + 1) * LANE] for j in range(count + 1)]
        before = jnp.concatenate(blocks[:-1], axis=0)
        after = jnp.concatenate(blocks[1:], axis=0)
        framed = jnp.concatenate([before, after], axis=1).astype(jnp.bfloat16)
        value = jnp.dot(framed, fir_tile(taps_ref[...]), preferred_element_type=jnp.float32)
        total = jnp.zeros((NS, LANE), jnp.float32)
        first_kept = [
            off_ref[jnp.maximum(chip - 1, 0)],
            off_ref[chip],
            off_ref[jnp.minimum(chip + 1, chips - 1)],
        ]
        for j in range(count):
            piece = value[j * NS : (j + 1) * NS, :]
            start = j * LANE - MAXLAG
            window = start // WIN
            if window == 0:
                total = total + piece * piece
            place = lax.broadcasted_iota(jnp.int32, (1, LANE), 1) + (start - window * WIN)
            keep = jnp.where(place >= first_kept[window + 1], 1.0, 0.0)
            if window < 0:
                keep = keep * jnp.where(chip > 0, 1.0, 0.0)
            if window > 0:
                keep = keep * jnp.where(chip < chips - 1, 1.0, 0.0)
            out_ref[:, j * LANE : (j + 1) * LANE] = piece * keep
        lines = []
        for power_ref in power_refs:
            lines.append(jnp.sum(power_ref[...].T, axis=0, keepdims=True))
        repeated = jnp.concatenate([total] * SHIFTS, axis=0)
        lines.append(jnp.sum(repeated.T, axis=0, keepdims=True))
        lines.append(jnp.zeros((8 - len(lines), LANE), jnp.float32))
        energy = jnp.concatenate(lines, axis=0)
        energy_ref[...] = jnp.broadcast_to(energy[None], energy_ref.shape)

    return call(
        kernel,
        "filter_sources",
        [shape((NS, length), jnp.float32), shape((chips, 8, LANE), jnp.float32)],
        [SMEM, VMEM, VMEM, VMEM] + [VMEM] * len(powers),
        moved=MIB,
    )(offsets, taps, mine, other, *powers)


def lag_products(white, table_ref, pairs, keep_ref, send_ref, half_groups):
    rows, depth = white.shape
    sub = rows // half_groups // 2
    own_low = (lax.axis_index("tm") // 2) % 2 == 0
    for place, pair in enumerate(pairs):
        offset = pair * 2 * SHIFTS
        left = table_ref[offset : offset + depth, :]
        right = table_ref[offset + SHIFTS : offset + SHIFTS + depth, :]
        lags = jnp.concatenate([left, right], axis=1)
        value = jnp.dot(white[...], lags, preferred_element_type=jnp.float32)
        value = value.reshape(half_groups, 2, sub, 2 * LANE)
        low, high = value[:, 0], value[:, 1]
        cols = slice(place * 2 * LANE, (place + 1) * 2 * LANE)
        keep_ref[:, :, cols] = jnp.where(own_low, low, high)
        send_ref[:, :, cols] = jnp.where(own_low, high, low).astype(jnp.bfloat16)


def correlate_first(energies, traces, row_blocks, pairs, half_groups, total_samples):
    block_rows, depth = row_blocks[0].shape
    parts = len(row_blocks)
    channels = block_rows * parts
    length = traces.shape[1]
    chunk = 1024
    loads = depth // chunk

    def kernel(energy_ref, traces_ref, *refs):
        row_refs = refs[:parts]
        keep_ref, send_ref, white, table, buf, shifted, sems = refs[parts:]
        copies = []
        for i in range(loads):
            for r, rows_ref in enumerate(row_refs):
                source = rows_ref.at[:, pl.ds(i * chunk, chunk)]
                place = buf.at[i, pl.ds(r * block_rows, block_rows)]
                copies.append(pltpu.make_async_copy(source, place, sems.at[i * parts + r]))
        for copy in copies:
            copy.start()
        energy = jnp.sum(energy_ref[...], axis=0)
        scale = lax.rsqrt(energy / total_samples + EPS)
        padded = jnp.concatenate([scale, jnp.zeros((LANE - 8, LANE), jnp.float32)], axis=0)
        turned = padded.T
        blocks = channels // LANE
        gain = jnp.concatenate([turned[:, r : r + 1] for r in range(blocks)], axis=0)
        trace = traces_ref[...] * turned[:NS, blocks : blocks + 1]
        trace = trace.astype(jnp.bfloat16).astype(jnp.float32)
        for b in range(SHIFTS):
            moved = trace if b == 0 else pltpu.roll(trace, length - b, 1)
            shifted[b * NS : (b + 1) * NS, :] = moved
        for j in range(length // LANE):
            cols = slice(j * LANE, (j + 1) * LANE)
            table[cols, :] = shifted[:, cols].T.astype(jnp.bfloat16)
        for i in range(loads):
            for copy in copies[i * parts : (i + 1) * parts]:
                copy.wait()
            white[:, i * chunk : (i + 1) * chunk] = (buf[i] * gain).astype(jnp.bfloat16)
        lag_products(white, table, pairs, keep_ref, send_ref, half_groups)

    sub = channels // half_groups // 2
    cols = len(pairs) * 2 * LANE
    return call(
        kernel,
        "correlate_first",
        [
            shape((half_groups, sub, cols), jnp.float32),
            shape((half_groups, sub, cols), jnp.bfloat16),
            shape((channels, depth), jnp.bfloat16),
            shape((length, LANE), jnp.bfloat16),
        ],
        [VMEM, VMEM] + [ANY] * parts,
        [
            pltpu.VMEM((loads, channels, chunk), jnp.float32),
            pltpu.VMEM((LANE, length), jnp.float32),
            pltpu.SemaphoreType.DMA((loads * parts,)),
        ],
        limit=40,
        flops=2 * channels * depth * cols,
        moved=16 * MIB,
    )(energies, traces, *row_blocks)


def correlate_next(white, table, pairs, half_groups):
    channels, depth = white.shape

    def kernel(white_ref, table_ref, keep_ref, send_ref):
        lag_products(white_ref, table_ref, pairs, keep_ref, send_ref, half_groups)

    sub = channels // half_groups // 2
    cols = len(pairs) * 2 * LANE
    return call(
        kernel,
        "correlate_next",
        [
            shape((half_groups, sub, cols), jnp.float32),
            shape((half_groups, sub, cols), jnp.bfloat16),
        ],
        [VMEM, VMEM],
        flops=2 * channels * depth * cols,
        moved=8 * MIB,
    )(white, table)


def add_line(keeps, arrivals):
    groups, sub, _ = keeps[0].shape
    widths = [keep.shape[2] for keep in keeps]
    count = len(keeps)

    def kernel(*refs):
        start = 0
        for keep_ref, across_ref, width in zip(refs[:count], refs[count : 2 * count], widths):
            value = keep_ref[...] + across_ref[...].astype(jnp.float32)
            refs[-1][:, :, start : start + width] = value.astype(jnp.bfloat16)
            start += width

    return call(
        kernel,
        "add_line",
        [shape((groups, sub, sum(widths)), jnp.bfloat16)],
        [VMEM] * (2 * count),
        moved=MIB,
    )(*keeps, *arrivals)[0]


def finish(parts, factor):
    count, sub, cols = parts.shape

    def kernel(parts_ref, out_ref, turned):
        blank = jnp.zeros((LANE - sub, LANE), jnp.float32)
        value = parts_ref[0].astype(jnp.float32)
        for i in range(1, count):
            value = value + parts_ref[i].astype(jnp.float32)
        value = value * factor
        for j in range(cols // LANE):
            block = jnp.concatenate([value[:, j * LANE : (j + 1) * LANE], blank], axis=0)
            turned[j * LANE : (j + 1) * LANE, :] = block.T
        for m in range(NS):
            for j in range(LAGS // LANE):
                block = turned[pl.ds(j * LANE * NS + m, LANE, stride=NS), :]
                out_ref[:, m // SB, m % SB, j * LANE : (j + 1) * LANE] = block.T[:sub]

    return call(
        kernel,
        "finish",
        [shape((sub, NSRC, SB, LAGS), jnp.float32)],
        [VMEM],
        [pltpu.VMEM((NS * LAGS, LANE), jnp.float32)],
        moved=MIB,
    )(parts)[0]


def shards(strain_rate, whiten_taps, source_channels, window_offsets):
    channels, samples = strain_rate.shape
    tiles = lax.axis_size("tm")
    groups_chan = lax.axis_size("chan")
    total_samples = samples * tiles
    chips = tiles // 2
    sub = channels // tiles
    taps = wide_taps(whiten_taps)

    x4 = strain_rate.reshape(chips, 2, sub, samples)
    own, edge, away = pick_sources(source_channels, x4)

    swap = [(i, i ^ 1) for i in range(tiles)]
    to_next = [(2 * k - 1, 2 * k) for k in range(1, chips)]
    both_next = to_next + [(b, a) for a, b in to_next]
    edge = lax.ppermute(edge, "tm", both_next)
    edge, away = lax.optimization_barrier((edge, away))
    other = lax.ppermute(away, "tm", swap)
    high = lax.ppermute(edge, "tm", [(2 * k, 2 * k + 1) for k in range(chips)])
    piece = extend_sources(own, edge)
    parts = [
        lax.ppermute(piece, "chan", [(i, (i + 2 * d) % groups_chan) for i in range(groups_chan)])
        for d in range(1, groups_chan // 2)
    ]
    half = chips // 2
    filtered, power_a = filter_rows(window_offsets, taps, x4, other, edge, high, 0, half)
    *parts, power_a = lax.optimization_barrier((*parts, power_a))
    piece = add_pieces(piece, *parts)
    arrived = lax.ppermute(piece, "chan", [(i, i ^ 1) for i in range(groups_chan)])
    filtered, power_b = filter_rows(
        window_offsets, taps, x4, other, edge, high, half, half, filtered
    )
    arrived, power_b = lax.optimization_barrier((arrived, power_b))
    piece = add_pieces(piece, arrived)
    piece_other = lax.ppermute(piece, "tm", swap)
    traces, energy = filter_sources(
        window_offsets, taps, piece, piece_other, [power_a, power_b], chips
    )
    same = [[2 * k + c for k in range(chips)] for c in range(2)]
    energies = lax.all_to_all(energy, "tm", 0, 0, tiled=True, axis_index_groups=same)

    column = tiles // 4
    dots = LAGS // (2 * SHIFTS)
    splits = [range(i, i + 2) for i in range(0, dots, 2)]
    line = [(i, i ^ 2) for i in range(tiles)]
    keep, send, white, table = correlate_first(
        energies, traces, [filtered], splits[0], column, total_samples
    )
    keeps, arrivals = [keep], [lax.ppermute(send, "tm", line)]
    for pairs in splits[1:]:
        if len(keeps) > 1:
            white, arrivals[-2] = lax.optimization_barrier((white, arrivals[-2]))
        keep, send = correlate_next(white, table, pairs, column)
        keeps.append(keep)
        arrivals.append(lax.ppermute(send, "tm", line))
    summed = add_line(keeps, arrivals)
    columns = [[4 * z + r for z in range(column)] for r in range(4)]
    parts = lax.all_to_all(summed, "tm", 0, 0, tiled=True, axis_index_groups=columns)
    return finish(parts, 1.0 / math.sqrt(total_samples))


def solution(mesh):
    return jax.shard_map(
        shards,
        mesh=mesh,
        in_specs=(P("chan", "tm"), P(), P(), P()),
        out_specs=P(("chan", "tm"), None, None, None),
        check_vma=False,
    )
```

```python
import math

import jax
import jax.numpy as jnp
from jax import lax
from jax.experimental import pallas as pl
from jax.experimental.pallas import tpu as pltpu
from jax.sharding import PartitionSpec as P

TAPS = 64
MAXLAG = 128
LAGS = 256
NSRC = 2
SB = 4
NS = NSRC * SB
WIN = 8192
LANE = 128
SHIFTS = 16
LEFT = 256
EPS = 1e-05
MIB = 1024 * 1024

VMEM = pl.BlockSpec(memory_space=pltpu.VMEM)
SMEM = pl.BlockSpec(memory_space=pltpu.SMEM)
ANY = pl.BlockSpec(memory_space=pl.ANY)


def call(
    kernel, name, out, in_specs, scratch=(), out_specs=None, limit=16, flops=0, moved=0, aliases=None
):
    return pl.pallas_call(
        kernel,
        out_shape=out,
        in_specs=in_specs,
        out_specs=out_specs or [VMEM] * len(out),
        scratch_shapes=list(scratch),
        input_output_aliases=aliases or {},
        compiler_params=pltpu.CompilerParams(vmem_limit_bytes=limit * MIB),
        cost_estimate=pl.CostEstimate(flops=flops, bytes_accessed=moved, transcendentals=0),
        name=name,
    )


def shape(dims, dtype):
    return jax.ShapeDtypeStruct(dims, dtype)


def fir_tile(taps):
    wide = jnp.broadcast_to(taps.astype(jnp.float32), (2 * LANE, 2 * LANE))
    rolled = pltpu.roll(wide, LANE, 1, stride=1, stride_axis=0)
    return rolled[:, :LANE].astype(jnp.bfloat16)


def wide_taps(taps):
    return jnp.pad(taps, (0, 2 * LANE - TAPS)).reshape(1, 2 * LANE)


def pick_sources(source_channels, x4):
    groups, _, sub, samples = x4.shape
    channels = groups * 2 * sub

    def kernel(ids_ref, x_ref, own_ref, edge_ref, high_ref, away_ref, buf, sems):
        base = lax.axis_index("chan") * channels
        core = lax.axis_index("tm") % 2
        copies = []
        inner = []
        for j in range(NS):
            local = ids_ref[j // SB, j % SB] - base
            owned = (local >= 0) & (local < channels)
            row = jnp.clip(local, 0, channels - 1)
            group, half = row // (2 * sub), (row // sub) % 2
            inner.append(jnp.where(owned, row % sub, -1))
            copies.append(pltpu.make_async_copy(x_ref.at[group, half], buf.at[j], sems.at[j]))
        last = pl.ds(samples - LANE, LANE)
        rest = [
            pltpu.make_async_copy(
                x_ref.at[:, 0, :, last], edge_ref.at[pl.ds(0, groups)], sems.at[NS]
            ),
            pltpu.make_async_copy(x_ref.at[:, 1, :, last], high_ref, sems.at[NS + 1]),
            pltpu.make_async_copy(x_ref.at[:, 1 - core], away_ref, sems.at[NS + 2]),
        ]
        for copy in copies + rest:
            copy.start()
        rows = lax.broadcasted_iota(jnp.int32, (sub, 1), 0)
        own = jnp.zeros((NS, samples), jnp.float32)
        for j in range(NS):
            copies[j].wait()
            picked = buf[j].astype(jnp.float32) * jnp.where(rows == inner[j], 1.0, 0.0)
            picked = picked[:NS] + picked[NS:]
            own = own + pltpu.roll(picked, (j + NS - inner[j] % NS) % NS, 0)
        own_ref[...] = own.astype(jnp.bfloat16)
        end = jnp.where(core == 1, own[:, samples - LEFT :], own[:, :LEFT])
        for copy in rest:
            copy.wait()
        edge_ref[groups] = jnp.concatenate(
            [end[:, :LANE], end[:, LANE:]], axis=0
        ).astype(jnp.bfloat16)

    return call(
        kernel,
        "pick_sources",
        [
            shape((NS, samples), jnp.bfloat16),
            shape((groups + 1, sub, LANE), jnp.bfloat16),
            shape((groups, sub, LANE), jnp.bfloat16),
            shape((groups, sub, samples), jnp.bfloat16),
        ],
        [SMEM, ANY],
        [pltpu.VMEM((NS, sub, samples), jnp.bfloat16), pltpu.SemaphoreType.DMA((NS + 3,))],
        limit=50,
        moved=2 * MIB,
    )(source_channels, x4)


def extend_sources(own, edge):
    samples = own.shape[1]
    groups = edge.shape[0] - 1

    def kernel(own_ref, edge_ref, out_ref):
        end = edge_ref[groups].astype(jnp.float32)
        joined = [own_ref[...].astype(jnp.float32), end[:NS], end[NS:]]
        out_ref[...] = jnp.concatenate(joined, axis=1).astype(jnp.bfloat16)

    return call(
        kernel,
        "extend_sources",
        [shape((NS, samples + LEFT), jnp.bfloat16)],
        [VMEM, VMEM],
    )(own, edge)[0]


def add_pieces(*pieces):
    def kernel(*refs):
        total = refs[0][...].astype(jnp.float32)
        for ref in refs[1:-1]:
            total = total + ref[...].astype(jnp.float32)
        refs[-1][...] = total.astype(jnp.bfloat16)

    return call(
        kernel,
        "add_pieces",
        [shape(pieces[0].shape, jnp.bfloat16)],
        [VMEM] * len(pieces),
    )(*pieces)[0]


def filter_rows(offsets, taps, x4, other, edge, high, first_group, groups, filled=None):
    all_groups, _, sub, half = x4.shape
    filled = [] if filled is None else [filled]
    rows = groups * sub
    chosen = slice(first_group, first_group + groups)
    chunk = 1024
    parts = half // chunk
    total = 2 * parts

    def kernel(
        off_ref, taps_ref, x_ref, other_ref, edge_ref, high_ref, *refs
    ):
        out_ref, power_ref, value_buf, sems = refs[len(filled) :]
        tile = lax.axis_index("tm")
        core = tile % 2
        matrix = fir_tile(taps_ref[...])
        first_kept = off_ref[tile // 2]

        def store(part):
            place = out_ref.at[pl.ds(first_group * sub, rows), pl.ds(part * chunk, chunk)]
            return pltpu.make_async_copy(value_buf.at[part], place, sems.at[part])

        def run(read_low, read_high, previous):
            power = jnp.zeros((rows, LANE), jnp.float32)
            for part in range(total):
                read = read_low if part < parts else read_high
                for j in range(chunk // LANE):
                    first = (part % parts) * chunk + j * LANE
                    current = read(slice(first, first + LANE)).reshape(rows, LANE)
                    framed = jnp.concatenate([previous, current], axis=1)
                    value = jnp.dot(framed, matrix, preferred_element_type=jnp.float32)
                    power = power + value * value
                    place = lax.broadcasted_iota(jnp.int32, (1, LANE), 1) + part * chunk + j * LANE
                    value = value * jnp.where(place >= first_kept, 1.0, 0.0)
                    value_buf[part, :, j * LANE : (j + 1) * LANE] = value
                    previous = current
                store(part).start()
            power_ref[...] = power

        def own(cols):
            return x_ref[chosen, core, :, cols]

        def swapped(cols):
            return other_ref[chosen, :, cols]

        @pl.when(core == 0)
        def _():
            run(own, swapped, edge_ref[chosen].reshape(rows, LANE))

        @pl.when(core == 1)
        def _():
            run(swapped, own, high_ref[chosen].reshape(rows, LANE))

        for part in range(total):
            store(part).wait()

    return call(
        kernel,
        "filter_rows",
        [shape((all_groups * sub, 2 * half), jnp.float32), shape((rows, LANE), jnp.float32)],
        [SMEM, VMEM, VMEM, VMEM, VMEM, VMEM] + [ANY] * len(filled),
        [pltpu.VMEM((total, rows, chunk), jnp.float32), pltpu.SemaphoreType.DMA((total,))],
        out_specs=[ANY, VMEM],
        limit=40,
        flops=2 * rows * 2 * half * 512,
        moved=6 * MIB,
        aliases={6: 0} if filled else None,
    )(offsets, taps, x4, other, edge, high, *filled)


def filter_sources(offsets, taps, mine, other, powers, chips):
    length = WIN + 2 * MAXLAG
    count = length // LANE
    half = mine.shape[1] - LEFT

    def kernel(off_ref, taps_ref, mine_ref, other_ref, *refs):
        *power_refs, out_ref, energy_ref = refs
        tile = lax.axis_index("tm")
        core, chip = tile % 2, tile // 2
        mine_rows = mine_ref[...].astype(jnp.float32)
        other_rows = other_ref[...].astype(jnp.float32)
        low = jnp.where(core == 0, mine_rows, other_rows)
        high = jnp.where(core == 0, other_rows, mine_rows)
        raw = [low[:, half:], low[:, :half], high[:, :half], high[:, half : half + LANE]]
        raw = jnp.concatenate(raw, axis=1)
        blocks = [raw[:, j * LANE : (j + 1) * LANE] for j in range(count + 1)]
        before = jnp.concatenate(blocks[:-1], axis=0)
        after = jnp.concatenate(blocks[1:], axis=0)
        framed = jnp.concatenate([before, after], axis=1).astype(jnp.bfloat16)
        value = jnp.dot(framed, fir_tile(taps_ref[...]), preferred_element_type=jnp.float32)
        total = jnp.zeros((NS, LANE), jnp.float32)
        first_kept = [
            off_ref[jnp.maximum(chip - 1, 0)],
            off_ref[chip],
            off_ref[jnp.minimum(chip + 1, chips - 1)],
        ]
        for j in range(count):
            piece = value[j * NS : (j + 1) * NS, :]
            start = j * LANE - MAXLAG
            window = start // WIN
            if window == 0:
                total = total + piece * piece
            place = lax.broadcasted_iota(jnp.int32, (1, LANE), 1) + (start - window * WIN)
            keep = jnp.where(place >= first_kept[window + 1], 1.0, 0.0)
            if window < 0:
                keep = keep * jnp.where(chip > 0, 1.0, 0.0)
            if window > 0:
                keep = keep * jnp.where(chip < chips - 1, 1.0, 0.0)
            out_ref[:, j * LANE : (j + 1) * LANE] = piece * keep
        lines = []
        for power_ref in power_refs:
            lines.append(jnp.sum(power_ref[...].T, axis=0, keepdims=True))
        repeated = jnp.concatenate([total] * SHIFTS, axis=0)
        lines.append(jnp.sum(repeated.T, axis=0, keepdims=True))
        lines.append(jnp.zeros((8 - len(lines), LANE), jnp.float32))
        energy = jnp.concatenate(lines, axis=0)
        energy_ref[...] = jnp.broadcast_to(energy[None], energy_ref.shape)

    return call(
        kernel,
        "filter_sources",
        [shape((NS, length), jnp.float32), shape((chips, 8, LANE), jnp.float32)],
        [SMEM, VMEM, VMEM, VMEM] + [VMEM] * len(powers),
        moved=MIB,
    )(offsets, taps, mine, other, *powers)


def lag_block(table_ref, start, depth, pair):
    offset = start + pair * 2 * SHIFTS
    left = table_ref[offset : offset + depth, :]
    right = table_ref[offset + SHIFTS : offset + SHIFTS + depth, :]
    return jnp.concatenate([left, right], axis=1)


def split_line(value, cols, keep_ref, send_ref, half_groups):
    rows, width = value.shape
    own_low = (lax.axis_index("tm") // 2) % 2 == 0
    value = value.reshape(half_groups, 2, rows // half_groups // 2, width)
    low, high = value[:, 0], value[:, 1]
    keep_ref[:, :, cols] = jnp.where(own_low, low, high)
    send_ref[:, :, cols] = jnp.where(own_low, high, low).astype(jnp.bfloat16)


def correlate_first(energies, traces, row_blocks, pairs, half_groups, total_samples):
    block_rows, depth = row_blocks[0].shape
    parts = len(row_blocks)
    channels = block_rows * parts
    length = traces.shape[1]
    chunk = 1024
    loads = depth // chunk

    def kernel(energy_ref, traces_ref, *refs):
        row_refs = refs[:parts]
        keep_ref, send_ref, white, table, buf, total, sems = refs[parts:]
        copies = []
        for i in range(loads):
            for r, rows_ref in enumerate(row_refs):
                source = rows_ref.at[:, pl.ds(i * chunk, chunk)]
                place = buf.at[i, pl.ds(r * block_rows, block_rows)]
                copies.append(pltpu.make_async_copy(source, place, sems.at[i * parts + r]))
        for copy in copies:
            copy.start()
        energy = jnp.sum(energy_ref[...], axis=0)
        scale = lax.rsqrt(energy / total_samples + EPS)
        padded = jnp.concatenate([scale, jnp.zeros((LANE - 8, LANE), jnp.float32)], axis=0)
        turned = padded.T
        blocks = channels // LANE
        gain = jnp.concatenate([turned[:, r : r + 1] for r in range(blocks)], axis=0)
        source_gain = turned[:NS, blocks : blocks + 1]
        lane = lax.broadcasted_iota(jnp.int32, (NS, LANE), 1)

        def traces_block(j):
            if j * LANE >= length:
                return jnp.zeros((NS, LANE), jnp.float32)
            block = traces_ref[:, j * LANE : (j + 1) * LANE] * source_gain
            return block.astype(jnp.bfloat16).astype(jnp.float32)

        def build(low, high):
            for j in range(low // LANE, high // LANE):
                here, after = traces_block(j), traces_block(j + 1)
                lines = [here]
                for b in range(1, SHIFTS):
                    lines.append(pltpu.roll(jnp.where(lane < b, after, here), LANE - b, 1))
                turned_block = jnp.concatenate(lines, axis=0).T
                table[j * LANE : (j + 1) * LANE, :] = turned_block.astype(jnp.bfloat16)

        ahead = chunk + LAGS
        build(0, ahead)
        for i in range(loads):
            for copy in copies[i * parts : (i + 1) * parts]:
                copy.wait()
            span = slice(i * chunk, (i + 1) * chunk)
            white[:, span] = (buf[i] * gain).astype(jnp.bfloat16)
            if i + 1 < loads:
                build(i * chunk + ahead, min((i + 1) * chunk + ahead, length))
            for place, pair in enumerate(pairs):
                value = jnp.dot(
                    white[:, span],
                    lag_block(table, i * chunk, chunk, pair),
                    preferred_element_type=jnp.float32,
                )
                cols = slice(place * 2 * LANE, (place + 1) * 2 * LANE)
                total[:, cols] = value if i == 0 else total[:, cols] + value
        for place in range(len(pairs)):
            cols = slice(place * 2 * LANE, (place + 1) * 2 * LANE)
            split_line(total[:, cols], cols, keep_ref, send_ref, half_groups)

    sub = channels // half_groups // 2
    cols = len(pairs) * 2 * LANE
    return call(
        kernel,
        "correlate_first",
        [
            shape((half_groups, sub, cols), jnp.float32),
            shape((half_groups, sub, cols), jnp.bfloat16),
            shape((channels, depth), jnp.bfloat16),
            shape((length, LANE), jnp.bfloat16),
        ],
        [VMEM, VMEM] + [ANY] * parts,
        [
            pltpu.VMEM((loads, channels, chunk), jnp.float32),
            pltpu.VMEM((channels, len(pairs) * 2 * LANE), jnp.float32),
            pltpu.SemaphoreType.DMA((loads * parts,)),
        ],
        limit=40,
        flops=2 * channels * depth * cols,
        moved=16 * MIB,
    )(energies, traces, *row_blocks)


def correlate_next(white, table, pairs, half_groups):
    channels, depth = white.shape

    def kernel(white_ref, table_ref, keep_ref, send_ref):
        for place, pair in enumerate(pairs):
            lags = lag_block(table_ref, 0, depth, pair)
            value = jnp.dot(white_ref[...], lags, preferred_element_type=jnp.float32)
            cols = slice(place * 2 * LANE, (place + 1) * 2 * LANE)
            split_line(value, cols, keep_ref, send_ref, half_groups)

    sub = channels // half_groups // 2
    cols = len(pairs) * 2 * LANE
    return call(
        kernel,
        "correlate_next",
        [
            shape((half_groups, sub, cols), jnp.float32),
            shape((half_groups, sub, cols), jnp.bfloat16),
        ],
        [VMEM, VMEM],
        flops=2 * channels * depth * cols,
        moved=8 * MIB,
    )(white, table)


def add_line(keeps, arrivals):
    groups, sub, _ = keeps[0].shape
    widths = [keep.shape[2] for keep in keeps]
    count = len(keeps)

    def kernel(*refs):
        start = 0
        for keep_ref, across_ref, width in zip(refs[:count], refs[count : 2 * count], widths):
            value = keep_ref[...] + across_ref[...].astype(jnp.float32)
            refs[-1][:, :, start : start + width] = value.astype(jnp.bfloat16)
            start += width

    return call(
        kernel,
        "add_line",
        [shape((groups, sub, sum(widths)), jnp.bfloat16)],
        [VMEM] * (2 * count),
        moved=MIB,
    )(*keeps, *arrivals)[0]


def finish(parts, factor):
    count, sub, cols = parts.shape

    def kernel(parts_ref, out_ref, turned):
        blank = jnp.zeros((LANE - sub, LANE), jnp.float32)
        value = parts_ref[0].astype(jnp.float32)
        for i in range(1, count):
            value = value + parts_ref[i].astype(jnp.float32)
        value = value * factor
        for j in range(cols // LANE):
            block = jnp.concatenate([value[:, j * LANE : (j + 1) * LANE], blank], axis=0)
            turned[j * LANE : (j + 1) * LANE, :] = block.T
        for m in range(NS):
            for j in range(LAGS // LANE):
                block = turned[pl.ds(j * LANE * NS + m, LANE, stride=NS), :]
                out_ref[:, m // SB, m % SB, j * LANE : (j + 1) * LANE] = block.T[:sub]

    return call(
        kernel,
        "finish",
        [shape((sub, NSRC, SB, LAGS), jnp.float32)],
        [VMEM],
        [pltpu.VMEM((NS * LAGS, LANE), jnp.float32)],
        moved=MIB,
    )(parts)[0]


def shards(strain_rate, whiten_taps, source_channels, window_offsets):
    channels, samples = strain_rate.shape
    tiles = lax.axis_size("tm")
    groups_chan = lax.axis_size("chan")
    total_samples = samples * tiles
    chips = tiles // 2
    sub = channels // tiles
    taps = wide_taps(whiten_taps)

    x4 = strain_rate.reshape(chips, 2, sub, samples)
    own, edge, high, away = pick_sources(source_channels, x4)

    swap = [(i, i ^ 1) for i in range(tiles)]
    to_next = [(2 * k - 1, 2 * k) for k in range(1, chips)]
    both_next = to_next + [(b, a) for a, b in to_next]
    edge = lax.ppermute(edge, "tm", both_next)
    other = lax.ppermute(away, "tm", swap)
    high = lax.ppermute(high, "tm", [(2 * k - 1, 2 * k + 1) for k in range(1, chips)])

    edge, high = lax.optimization_barrier((edge, high))
    piece = extend_sources(own, edge)
    parts = [
        lax.ppermute(piece, "chan", [(i, (i + 2 * d) % groups_chan) for i in range(groups_chan)])
        for d in range(1, groups_chan // 2)
    ]
    half = chips // 2
    filtered, power_a = filter_rows(window_offsets, taps, x4, other, edge, high, 0, half)
    *parts, power_a = lax.optimization_barrier((*parts, power_a))
    piece = add_pieces(piece, *parts)
    arrived = lax.ppermute(piece, "chan", [(i, i ^ 1) for i in range(groups_chan)])
    filtered, power_b = filter_rows(
        window_offsets, taps, x4, other, edge, high, half, half, filtered
    )
    arrived, power_b = lax.optimization_barrier((arrived, power_b))
    piece = add_pieces(piece, arrived)
    piece_other = lax.ppermute(piece, "tm", swap)
    traces, energy = filter_sources(
        window_offsets, taps, piece, piece_other, [power_a, power_b], chips
    )
    same = [[2 * k + c for k in range(chips)] for c in range(2)]
    energies = lax.all_to_all(energy, "tm", 0, 0, tiled=True, axis_index_groups=same)

    column = tiles // 4
    dots = LAGS // (2 * SHIFTS)
    splits = [range(0, dots // 4), range(dots // 4, dots * 5 // 8), range(dots * 5 // 8, dots)]
    line = [(i, i ^ 2) for i in range(tiles)]
    keep, send, white, table = correlate_first(
        energies, traces, [filtered], splits[0], column, total_samples
    )
    keeps, arrivals = [keep], [lax.ppermute(send, "tm", line)]
    for pairs in splits[1:]:
        if len(keeps) > 1:
            white, arrivals[-2] = lax.optimization_barrier((white, arrivals[-2]))
        keep, send = correlate_next(white, table, pairs, column)
        keeps.append(keep)
        arrivals.append(lax.ppermute(send, "tm", line))
    summed = add_line(keeps, arrivals)
    columns = [[4 * z + r for z in range(column)] for r in range(4)]
    parts = lax.all_to_all(summed, "tm", 0, 0, tiled=True, axis_index_groups=columns)
    return finish(parts, 1.0 / math.sqrt(total_samples))


def solution(mesh):
    return jax.shard_map(
        shards,
        mesh=mesh,
        in_specs=(P("chan", "tm"), P(), P(), P()),
        out_specs=P(("chan", "tm"), None, None, None),
        check_vma=False,
    )
```

```python
import math

import jax
import jax.numpy as jnp
from jax import lax
from jax.experimental import pallas as pl
from jax.experimental.pallas import tpu as pltpu
from jax.sharding import PartitionSpec as P

TAPS = 64
MAXLAG = 128
LAGS = 256
NSRC = 2
SB = 4
NS = NSRC * SB
WIN = 8192
LANE = 128
SHIFTS = 16
LEFT = 256
EPS = 1e-05
MIB = 1024 * 1024

VMEM = pl.BlockSpec(memory_space=pltpu.VMEM)
SMEM = pl.BlockSpec(memory_space=pltpu.SMEM)
ANY = pl.BlockSpec(memory_space=pl.ANY)


def call(
    kernel, name, out, in_specs, scratch=(), out_specs=None, limit=16, flops=0, moved=0, aliases=None
):
    return pl.pallas_call(
        kernel,
        out_shape=out,
        in_specs=in_specs,
        out_specs=out_specs or [VMEM] * len(out),
        scratch_shapes=list(scratch),
        input_output_aliases=aliases or {},
        compiler_params=pltpu.CompilerParams(vmem_limit_bytes=limit * MIB),
        cost_estimate=pl.CostEstimate(flops=flops, bytes_accessed=moved, transcendentals=0),
        name=name,
    )


def shape(dims, dtype):
    return jax.ShapeDtypeStruct(dims, dtype)


def fir_tile(taps):
    wide = jnp.broadcast_to(taps.astype(jnp.float32), (2 * LANE, 2 * LANE))
    rolled = pltpu.roll(wide, LANE, 1, stride=1, stride_axis=0)
    return rolled[:, :LANE].astype(jnp.bfloat16)


def wide_taps(taps):
    return jnp.pad(taps, (0, 2 * LANE - TAPS)).reshape(1, 2 * LANE)


def pick_sources(source_channels, x4):
    groups, _, sub, samples = x4.shape
    channels = groups * 2 * sub

    def kernel(ids_ref, x_ref, own_ref, edge_ref, high_ref, away_ref, mine_ref, buf, sems):
        base = lax.axis_index("chan") * channels
        core = lax.axis_index("tm") % 2
        copies = []
        inner = []
        for j in range(NS):
            local = ids_ref[j // SB, j % SB] - base
            owned = (local >= 0) & (local < channels)
            row = jnp.clip(local, 0, channels - 1)
            group, half = row // (2 * sub), (row // sub) % 2
            inner.append(jnp.where(owned, row % sub, -1))
            copies.append(pltpu.make_async_copy(x_ref.at[group, half], buf.at[j], sems.at[j]))
        last = pl.ds(samples - LANE, LANE)
        rest = [
            pltpu.make_async_copy(
                x_ref.at[:, 0, :, last], edge_ref.at[pl.ds(0, groups)], sems.at[NS]
            ),
            pltpu.make_async_copy(x_ref.at[:, 1, :, last], high_ref, sems.at[NS + 1]),
            pltpu.make_async_copy(x_ref.at[:, 1 - core], away_ref, sems.at[NS + 2]),
            pltpu.make_async_copy(x_ref.at[:, core], mine_ref, sems.at[NS + 3]),
        ]
        for copy in copies + rest:
            copy.start()
        rows = lax.broadcasted_iota(jnp.int32, (sub, 1), 0)
        own = jnp.zeros((NS, samples), jnp.float32)
        for j in range(NS):
            copies[j].wait()
            picked = buf[j].astype(jnp.float32) * jnp.where(rows == inner[j], 1.0, 0.0)
            picked = picked[:NS] + picked[NS:]
            own = own + pltpu.roll(picked, (j + NS - inner[j] % NS) % NS, 0)
        own_ref[...] = own.astype(jnp.bfloat16)
        end = jnp.where(core == 1, own[:, samples - LEFT :], own[:, :LEFT])
        for copy in rest:
            copy.wait()
        edge_ref[groups] = jnp.concatenate(
            [end[:, :LANE], end[:, LANE:]], axis=0
        ).astype(jnp.bfloat16)

    return call(
        kernel,
        "pick_sources",
        [
            shape((NS, samples), jnp.bfloat16),
            shape((groups + 1, sub, LANE), jnp.bfloat16),
            shape((groups, sub, LANE), jnp.bfloat16),
            shape((groups, sub, samples), jnp.bfloat16),
            shape((groups, sub, samples), jnp.bfloat16),
        ],
        [SMEM, ANY],
        [pltpu.VMEM((NS, sub, samples), jnp.bfloat16), pltpu.SemaphoreType.DMA((NS + 4,))],
        limit=48,
        moved=2 * MIB,
    )(source_channels, x4)


def extend_sources(own, edge):
    samples = own.shape[1]
    groups = edge.shape[0] - 1

    def kernel(own_ref, edge_ref, out_ref):
        end = edge_ref[groups].astype(jnp.float32)
        joined = [own_ref[...].astype(jnp.float32), end[:NS], end[NS:]]
        out_ref[...] = jnp.concatenate(joined, axis=1).astype(jnp.bfloat16)

    return call(
        kernel,
        "extend_sources",
        [shape((NS, samples + LEFT), jnp.bfloat16)],
        [VMEM, VMEM],
    )(own, edge)[0]


def add_pieces(*pieces):
    def kernel(*refs):
        total = refs[0][...].astype(jnp.float32)
        for ref in refs[1:-1]:
            total = total + ref[...].astype(jnp.float32)
        refs[-1][...] = total.astype(jnp.bfloat16)

    return call(
        kernel,
        "add_pieces",
        [shape(pieces[0].shape, jnp.bfloat16)],
        [VMEM] * len(pieces),
    )(*pieces)[0]


def filter_rows(offsets, taps, mine, other, edge, high, first_group, groups, filled=None):
    all_groups, sub, half = mine.shape
    filled = [] if filled is None else [filled]
    rows = groups * sub
    chosen = slice(first_group, first_group + groups)
    chunk = 1024
    parts = half // chunk
    total = 2 * parts

    def kernel(
        off_ref, taps_ref, mine_ref, other_ref, edge_ref, high_ref, *refs
    ):
        out_ref, power_ref, value_buf, sems = refs[len(filled) :]
        tile = lax.axis_index("tm")
        core = tile % 2
        matrix = fir_tile(taps_ref[...])
        first_kept = off_ref[tile // 2]

        def store(part):
            place = out_ref.at[pl.ds(first_group * sub, rows), pl.ds(part * chunk, chunk)]
            return pltpu.make_async_copy(value_buf.at[part], place, sems.at[part])

        def run(read_low, read_high, previous):
            power = jnp.zeros((rows, LANE), jnp.float32)
            for part in range(total):
                read = read_low if part < parts else read_high
                for j in range(chunk // LANE):
                    first = (part % parts) * chunk + j * LANE
                    current = read(slice(first, first + LANE)).reshape(rows, LANE)
                    framed = jnp.concatenate([previous, current], axis=1)
                    value = jnp.dot(framed, matrix, preferred_element_type=jnp.float32)
                    power = power + value * value
                    place = lax.broadcasted_iota(jnp.int32, (1, LANE), 1) + part * chunk + j * LANE
                    value = value * jnp.where(place >= first_kept, 1.0, 0.0)
                    value_buf[part, :, j * LANE : (j + 1) * LANE] = value
                    previous = current
                store(part).start()
            power_ref[...] = power

        def own(cols):
            return mine_ref[chosen, :, cols]

        def swapped(cols):
            return other_ref[chosen, :, cols]

        @pl.when(core == 0)
        def _():
            run(own, swapped, edge_ref[chosen].reshape(rows, LANE))

        @pl.when(core == 1)
        def _():
            run(swapped, own, high_ref[chosen].reshape(rows, LANE))

        for part in range(total):
            store(part).wait()

    return call(
        kernel,
        "filter_rows",
        [shape((all_groups * sub, 2 * half), jnp.float32), shape((rows, LANE), jnp.float32)],
        [SMEM, VMEM, VMEM, VMEM, VMEM, VMEM] + [ANY] * len(filled),
        [pltpu.VMEM((total, rows, chunk), jnp.float32), pltpu.SemaphoreType.DMA((total,))],
        out_specs=[ANY, VMEM],
        limit=45,
        flops=2 * rows * 2 * half * 512,
        moved=6 * MIB,
        aliases={6: 0} if filled else None,
    )(offsets, taps, mine, other, edge, high, *filled)


def filter_sources(offsets, taps, mine, other, powers, chips):
    length = WIN + 2 * MAXLAG
    count = length // LANE
    half = mine.shape[1] - LEFT

    def kernel(off_ref, taps_ref, mine_ref, other_ref, *refs):
        *power_refs, out_ref, energy_ref = refs
        tile = lax.axis_index("tm")
        core, chip = tile % 2, tile // 2
        mine_rows = mine_ref[...].astype(jnp.float32)
        other_rows = other_ref[...].astype(jnp.float32)
        low = jnp.where(core == 0, mine_rows, other_rows)
        high = jnp.where(core == 0, other_rows, mine_rows)
        raw = [low[:, half:], low[:, :half], high[:, :half], high[:, half : half + LANE]]
        raw = jnp.concatenate(raw, axis=1)
        blocks = [raw[:, j * LANE : (j + 1) * LANE] for j in range(count + 1)]
        before = jnp.concatenate(blocks[:-1], axis=0)
        after = jnp.concatenate(blocks[1:], axis=0)
        framed = jnp.concatenate([before, after], axis=1).astype(jnp.bfloat16)
        value = jnp.dot(framed, fir_tile(taps_ref[...]), preferred_element_type=jnp.float32)
        total = jnp.zeros((NS, LANE), jnp.float32)
        first_kept = [
            off_ref[jnp.maximum(chip - 1, 0)],
            off_ref[chip],
            off_ref[jnp.minimum(chip + 1, chips - 1)],
        ]
        for j in range(count):
            piece = value[j * NS : (j + 1) * NS, :]
            start = j * LANE - MAXLAG
            window = start // WIN
            if window == 0:
                total = total + piece * piece
            place = lax.broadcasted_iota(jnp.int32, (1, LANE), 1) + (start - window * WIN)
            keep = jnp.where(place >= first_kept[window + 1], 1.0, 0.0)
            if window < 0:
                keep = keep * jnp.where(chip > 0, 1.0, 0.0)
            if window > 0:
                keep = keep * jnp.where(chip < chips - 1, 1.0, 0.0)
            out_ref[:, j * LANE : (j + 1) * LANE] = piece * keep
        lines = []
        for power_ref in power_refs:
            lines.append(jnp.sum(power_ref[...].T, axis=0, keepdims=True))
        repeated = jnp.concatenate([total] * SHIFTS, axis=0)
        lines.append(jnp.sum(repeated.T, axis=0, keepdims=True))
        lines.append(jnp.zeros((8 - len(lines), LANE), jnp.float32))
        energy = jnp.concatenate(lines, axis=0)
        energy_ref[...] = jnp.broadcast_to(energy[None], energy_ref.shape)

    return call(
        kernel,
        "filter_sources",
        [shape((NS, length), jnp.float32), shape((chips, 8, LANE), jnp.float32)],
        [SMEM, VMEM, VMEM, VMEM] + [VMEM] * len(powers),
        moved=MIB,
    )(offsets, taps, mine, other, *powers)


def lag_block(table_ref, start, depth, pair):
    offset = start + pair * 2 * SHIFTS
    left = table_ref[offset : offset + depth, :]
    right = table_ref[offset + SHIFTS : offset + SHIFTS + depth, :]
    return jnp.concatenate([left, right], axis=1)


def split_line(value, cols, keep_ref, send_ref, half_groups):
    rows, width = value.shape
    own_low = (lax.axis_index("tm") // 2) % 2 == 0
    value = value.reshape(half_groups, 2, rows // half_groups // 2, width)
    low, high = value[:, 0], value[:, 1]
    keep_ref[:, :, cols] = jnp.where(own_low, low, high)
    send_ref[:, :, cols] = jnp.where(own_low, high, low).astype(jnp.bfloat16)


def correlate_first(energies, traces, row_blocks, pairs, half_groups, total_samples):
    block_rows, depth = row_blocks[0].shape
    parts = len(row_blocks)
    channels = block_rows * parts
    length = traces.shape[1]
    chunk = 1024
    loads = depth // chunk

    def kernel(energy_ref, traces_ref, *refs):
        row_refs = refs[:parts]
        keep_ref, send_ref, white, table, buf, total, sems = refs[parts:]
        copies = []
        for i in range(loads):
            for r, rows_ref in enumerate(row_refs):
                source = rows_ref.at[:, pl.ds(i * chunk, chunk)]
                place = buf.at[i, pl.ds(r * block_rows, block_rows)]
                copies.append(pltpu.make_async_copy(source, place, sems.at[i * parts + r]))
        for copy in copies:
            copy.start()
        energy = jnp.sum(energy_ref[...], axis=0)
        scale = lax.rsqrt(energy / total_samples + EPS)
        padded = jnp.concatenate([scale, jnp.zeros((LANE - 8, LANE), jnp.float32)], axis=0)
        turned = padded.T
        blocks = channels // LANE
        gain = jnp.concatenate([turned[:, r : r + 1] for r in range(blocks)], axis=0)
        source_gain = turned[:NS, blocks : blocks + 1]
        lane = lax.broadcasted_iota(jnp.int32, (NS, LANE), 1)

        def traces_block(j):
            if j * LANE >= length:
                return jnp.zeros((NS, LANE), jnp.float32)
            block = traces_ref[:, j * LANE : (j + 1) * LANE] * source_gain
            return block.astype(jnp.bfloat16).astype(jnp.float32)

        def build(low, high):
            for j in range(low // LANE, high // LANE):
                here, after = traces_block(j), traces_block(j + 1)
                lines = [here]
                for b in range(1, SHIFTS):
                    lines.append(pltpu.roll(jnp.where(lane < b, after, here), LANE - b, 1))
                turned_block = jnp.concatenate(lines, axis=0).T
                table[j * LANE : (j + 1) * LANE, :] = turned_block.astype(jnp.bfloat16)

        ahead = chunk + LAGS
        build(0, ahead)
        for i in range(loads):
            for copy in copies[i * parts : (i + 1) * parts]:
                copy.wait()
            span = slice(i * chunk, (i + 1) * chunk)
            white[:, span] = (buf[i] * gain).astype(jnp.bfloat16)
            if i + 1 < loads:
                build(i * chunk + ahead, min((i + 1) * chunk + ahead, length))
            for place, pair in enumerate(pairs):
                value = jnp.dot(
                    white[:, span],
                    lag_block(table, i * chunk, chunk, pair),
                    preferred_element_type=jnp.float32,
                )
                cols = slice(place * 2 * LANE, (place + 1) * 2 * LANE)
                total[:, cols] = value if i == 0 else total[:, cols] + value
        for place in range(len(pairs)):
            cols = slice(place * 2 * LANE, (place + 1) * 2 * LANE)
            split_line(total[:, cols], cols, keep_ref, send_ref, half_groups)

    sub = channels // half_groups // 2
    cols = len(pairs) * 2 * LANE
    return call(
        kernel,
        "correlate_first",
        [
            shape((half_groups, sub, cols), jnp.float32),
            shape((half_groups, sub, cols), jnp.bfloat16),
            shape((channels, depth), jnp.bfloat16),
            shape((length, LANE), jnp.bfloat16),
        ],
        [VMEM, VMEM] + [ANY] * parts,
        [
            pltpu.VMEM((loads, channels, chunk), jnp.float32),
            pltpu.VMEM((channels, len(pairs) * 2 * LANE), jnp.float32),
            pltpu.SemaphoreType.DMA((loads * parts,)),
        ],
        limit=40,
        flops=2 * channels * depth * cols,
        moved=16 * MIB,
    )(energies, traces, *row_blocks)


def correlate_next(white, table, pairs, half_groups):
    channels, depth = white.shape

    def kernel(white_ref, table_ref, keep_ref, send_ref):
        for place, pair in enumerate(pairs):
            lags = lag_block(table_ref, 0, depth, pair)
            value = jnp.dot(white_ref[...], lags, preferred_element_type=jnp.float32)
            cols = slice(place * 2 * LANE, (place + 1) * 2 * LANE)
            split_line(value, cols, keep_ref, send_ref, half_groups)

    sub = channels // half_groups // 2
    cols = len(pairs) * 2 * LANE
    return call(
        kernel,
        "correlate_next",
        [
            shape((half_groups, sub, cols), jnp.float32),
            shape((half_groups, sub, cols), jnp.bfloat16),
        ],
        [VMEM, VMEM],
        flops=2 * channels * depth * cols,
        moved=8 * MIB,
    )(white, table)


def add_line(keeps, arrivals):
    groups, sub, _ = keeps[0].shape
    widths = [keep.shape[2] for keep in keeps]
    count = len(keeps)

    def kernel(*refs):
        start = 0
        for keep_ref, across_ref, width in zip(refs[:count], refs[count : 2 * count], widths):
            value = keep_ref[...] + across_ref[...].astype(jnp.float32)
            refs[-1][:, :, start : start + width] = value.astype(jnp.bfloat16)
            start += width

    return call(
        kernel,
        "add_line",
        [shape((groups, sub, sum(widths)), jnp.bfloat16)],
        [VMEM] * (2 * count),
        moved=MIB,
    )(*keeps, *arrivals)[0]


def finish(parts, factor):
    count, sub, cols = parts.shape

    stack = LANE // sub

    def kernel(parts_ref, out_ref, turned):
        lane = lax.broadcasted_iota(jnp.int32, (sub, LANE), 1)
        value = parts_ref[0].astype(jnp.float32)
        for i in range(1, count):
            value = value + parts_ref[i].astype(jnp.float32)
        value = value * factor
        for g in range(cols // LANE // stack):
            first = g * stack
            blocks = [value[:, (first + k) * LANE : (first + k + 1) * LANE] for k in range(stack)]
            turned[...] = jnp.concatenate(blocks, axis=0).T
            by_source = [turned[pl.ds(m, SHIFTS, stride=NS), :] for m in range(NS)]
            ordered = jnp.concatenate(by_source, axis=0).T
            for m in range(NS):
                line = jnp.zeros((sub, LANE), jnp.float32)
                for k in range(stack):
                    block = ordered[k * sub : (k + 1) * sub, :]
                    moved = pltpu.roll(block, ((k - m) * SHIFTS) % LANE, 1) if k != m else block
                    line = jnp.where(lane // SHIFTS == k, moved, line)
                out_ref[:, m // SB, m % SB, g * LANE : (g + 1) * LANE] = line

    return call(
        kernel,
        "finish",
        [shape((sub, NSRC, SB, LAGS), jnp.float32)],
        [VMEM],
        [pltpu.VMEM((LANE, LANE), jnp.float32)],
        moved=MIB,
    )(parts)[0]


def shards(strain_rate, whiten_taps, source_channels, window_offsets):
    channels, samples = strain_rate.shape
    tiles = lax.axis_size("tm")
    groups_chan = lax.axis_size("chan")
    total_samples = samples * tiles
    chips = tiles // 2
    sub = channels // tiles
    taps = wide_taps(whiten_taps)

    x4 = strain_rate.reshape(chips, 2, sub, samples)
    own, edge, high, away, mine = pick_sources(source_channels, x4)

    swap = [(i, i ^ 1) for i in range(tiles)]
    to_next = [(2 * k - 1, 2 * k) for k in range(1, chips)]
    both_next = to_next + [(b, a) for a, b in to_next]
    edge = lax.ppermute(edge, "tm", both_next)
    other = lax.ppermute(away, "tm", swap)
    high = lax.ppermute(high, "tm", [(2 * k - 1, 2 * k + 1) for k in range(1, chips)])

    edge, high = lax.optimization_barrier((edge, high))
    piece = extend_sources(own, edge)
    parts = [
        lax.ppermute(piece, "chan", [(i, (i + 2 * d) % groups_chan) for i in range(groups_chan)])
        for d in range(1, groups_chan // 2)
    ]
    half = chips // 2
    filtered, power_a = filter_rows(window_offsets, taps, mine, other, edge, high, 0, half)
    *parts, power_a = lax.optimization_barrier((*parts, power_a))
    piece = add_pieces(piece, *parts)
    arrived = lax.ppermute(piece, "chan", [(i, i ^ 1) for i in range(groups_chan)])
    filtered, power_b = filter_rows(
        window_offsets, taps, mine, other, edge, high, half, half, filtered
    )
    arrived, power_b = lax.optimization_barrier((arrived, power_b))
    piece = add_pieces(piece, arrived)
    piece_other = lax.ppermute(piece, "tm", swap)
    traces, energy = filter_sources(
        window_offsets, taps, piece, piece_other, [power_a, power_b], chips
    )
    same = [[2 * k + c for k in range(chips)] for c in range(2)]
    energies = lax.all_to_all(energy, "tm", 0, 0, tiled=True, axis_index_groups=same)

    column = tiles // 4
    dots = LAGS // (2 * SHIFTS)
    splits = [range(0, dots // 4), range(dots // 4, dots * 5 // 8), range(dots * 5 // 8, dots)]
    line = [(i, i ^ 2) for i in range(tiles)]
    keep, send, white, table = correlate_first(
        energies, traces, [filtered], splits[0], column, total_samples
    )
    keeps, arrivals = [keep], [lax.ppermute(send, "tm", line)]
    for pairs in splits[1:]:
        if len(keeps) > 1:
            white, arrivals[-2] = lax.optimization_barrier((white, arrivals[-2]))
        keep, send = correlate_next(white, table, pairs, column)
        keeps.append(keep)
        arrivals.append(lax.ppermute(send, "tm", line))
    summed = add_line(keeps, arrivals)
    columns = [[4 * z + r for z in range(column)] for r in range(4)]
    parts = lax.all_to_all(summed, "tm", 0, 0, tiled=True, axis_index_groups=columns)
    return finish(parts, 1.0 / math.sqrt(total_samples))


def solution(mesh):
    return jax.shard_map(
        shards,
        mesh=mesh,
        in_specs=(P("chan", "tm"), P(), P(), P()),
        out_specs=P(("chan", "tm"), None, None, None),
        check_vma=False,
    )
```

```python
import math

import jax
import jax.numpy as jnp
from jax import lax
from jax.experimental import pallas as pl
from jax.experimental.pallas import tpu as pltpu
from jax.sharding import PartitionSpec as P

TAPS = 64
MAXLAG = 128
LAGS = 256
NSRC = 2
SB = 4
NS = NSRC * SB
WIN = 8192
LANE = 128
SHIFTS = 16
LEFT = 256
EPS = 1e-05
MIB = 1024 * 1024

VMEM = pl.BlockSpec(memory_space=pltpu.VMEM)
SMEM = pl.BlockSpec(memory_space=pltpu.SMEM)
ANY = pl.BlockSpec(memory_space=pl.ANY)


def call(
    kernel, name, out, in_specs, scratch=(), out_specs=None, limit=16, flops=0, moved=0, aliases=None
):
    return pl.pallas_call(
        kernel,
        out_shape=out,
        in_specs=in_specs,
        out_specs=out_specs or [VMEM] * len(out),
        scratch_shapes=list(scratch),
        input_output_aliases=aliases or {},
        compiler_params=pltpu.CompilerParams(vmem_limit_bytes=limit * MIB),
        cost_estimate=pl.CostEstimate(flops=flops, bytes_accessed=moved, transcendentals=0),
        name=name,
    )


def shape(dims, dtype):
    return jax.ShapeDtypeStruct(dims, dtype)


def fir_tile(taps):
    wide = jnp.broadcast_to(taps.astype(jnp.float32), (2 * LANE, 2 * LANE))
    rolled = pltpu.roll(wide, LANE, 1, stride=1, stride_axis=0)
    return rolled[:, :LANE].astype(jnp.bfloat16)


def wide_taps(taps):
    return jnp.pad(taps, (0, 2 * LANE - TAPS)).reshape(1, 2 * LANE)


def pick_sources(source_channels, x4):
    groups, _, sub, samples = x4.shape
    channels = groups * 2 * sub

    def kernel(ids_ref, x_ref, own_ref, edge_ref, high_ref, away_ref, buf, sems):
        base = lax.axis_index("chan") * channels
        core = lax.axis_index("tm") % 2
        copies = []
        inner = []
        for j in range(NS):
            local = ids_ref[j // SB, j % SB] - base
            owned = (local >= 0) & (local < channels)
            row = jnp.clip(local, 0, channels - 1)
            group, half = row // (2 * sub), (row // sub) % 2
            inner.append(jnp.where(owned, row % sub, -1))
            copies.append(pltpu.make_async_copy(x_ref.at[group, half], buf.at[j], sems.at[j]))
        last = pl.ds(samples - LANE, LANE)
        rest = [
            pltpu.make_async_copy(
                x_ref.at[:, 0, :, last], edge_ref.at[pl.ds(0, groups)], sems.at[NS]
            ),
            pltpu.make_async_copy(x_ref.at[:, 1, :, last], high_ref, sems.at[NS + 1]),
            pltpu.make_async_copy(x_ref.at[:, 1 - core], away_ref, sems.at[NS + 2]),
        ]
        for copy in copies + rest:
            copy.start()
        rows = lax.broadcasted_iota(jnp.int32, (sub, 1), 0)
        own = jnp.zeros((NS, samples), jnp.float32)
        for j in range(NS):
            copies[j].wait()
            picked = buf[j].astype(jnp.float32) * jnp.where(rows == inner[j], 1.0, 0.0)
            picked = picked[:NS] + picked[NS:]
            own = own + pltpu.roll(picked, (j + NS - inner[j] % NS) % NS, 0)
        own_ref[...] = own.astype(jnp.bfloat16)
        end = jnp.where(core == 1, own[:, samples - LEFT :], own[:, :LEFT])
        for copy in rest:
            copy.wait()
        edge_ref[groups] = jnp.concatenate(
            [end[:, :LANE], end[:, LANE:]], axis=0
        ).astype(jnp.bfloat16)

    return call(
        kernel,
        "pick_sources",
        [
            shape((NS, samples), jnp.bfloat16),
            shape((groups + 1, sub, LANE), jnp.bfloat16),
            shape((groups, sub, LANE), jnp.bfloat16),
            shape((groups, sub, samples), jnp.bfloat16),
        ],
        [SMEM, ANY],
        [pltpu.VMEM((NS, sub, samples), jnp.bfloat16), pltpu.SemaphoreType.DMA((NS + 3,))],
        limit=50,
        moved=2 * MIB,
    )(source_channels, x4)


def extend_sources(own, edge):
    samples = own.shape[1]
    groups = edge.shape[0] - 1

    def kernel(own_ref, edge_ref, out_ref):
        end = edge_ref[groups].astype(jnp.float32)
        joined = [own_ref[...].astype(jnp.float32), end[:NS], end[NS:]]
        out_ref[...] = jnp.concatenate(joined, axis=1).astype(jnp.bfloat16)

    return call(
        kernel,
        "extend_sources",
        [shape((NS, samples + LEFT), jnp.bfloat16)],
        [VMEM, VMEM],
    )(own, edge)[0]


def add_pieces(*pieces):
    def kernel(*refs):
        total = refs[0][...].astype(jnp.float32)
        for ref in refs[1:-1]:
            total = total + ref[...].astype(jnp.float32)
        refs[-1][...] = total.astype(jnp.bfloat16)

    return call(
        kernel,
        "add_pieces",
        [shape(pieces[0].shape, jnp.bfloat16)],
        [VMEM] * len(pieces),
    )(*pieces)[0]


def filter_rows(offsets, taps, x4, other, edges, part, filled=None):
    groups, _, sub, half = x4.shape
    rows = groups * sub
    chunk = 1024
    count = half // chunk
    extra = list(edges) + ([] if filled is None else [filled])

    def kernel(off_ref, taps_ref, x_ref, other_ref, *refs):
        edge_refs = refs[: len(edges)]
        out_ref, power_ref, value_buf, sems = refs[len(extra) :]
        tile = lax.axis_index("tm")
        core = tile % 2
        matrix = fir_tile(taps_ref[...])
        first_kept = off_ref[tile // 2]

        def store(index):
            place = out_ref.at[:, pl.ds(part * half + index * chunk, chunk)]
            return pltpu.make_async_copy(value_buf.at[index], place, sems.at[index])

        def run(read, previous):
            power = jnp.zeros((rows, LANE), jnp.float32)
            for index in range(count):
                for j in range(chunk // LANE):
                    first = index * chunk + j * LANE
                    current = read(slice(first, first + LANE)).reshape(rows, LANE)
                    framed = jnp.concatenate([previous, current], axis=1)
                    value = jnp.dot(framed, matrix, preferred_element_type=jnp.float32)
                    power = power + value * value
                    place = lax.broadcasted_iota(jnp.int32, (1, LANE), 1) + part * half + first
                    value = value * jnp.where(place >= first_kept, 1.0, 0.0)
                    value_buf[index, :, j * LANE : (j + 1) * LANE] = value
                    previous = current
                store(index).start()
            power_ref[...] = power

        def own(cols):
            return x_ref[:, core, :, cols]

        def swapped(cols):
            return other_ref[:, :, cols]

        last = slice(half - LANE, half)
        readers = (own, swapped)
        for index in range(2):
            low, high = readers[index], readers[1 - index]

            @pl.when(core == index)
            def _(index=index, low=low, high=high):
                if part == 1:
                    run(high, low(last).reshape(rows, LANE))
                else:
                    run(low, edge_refs[index][:groups].reshape(rows, LANE))

        for index in range(count):
            store(index).wait()

    return call(
        kernel,
        "filter_rows",
        [shape((rows, 2 * half), jnp.float32), shape((rows, LANE), jnp.float32)],
        [SMEM, VMEM, VMEM, VMEM] + [VMEM] * len(edges) + ([] if filled is None else [ANY]),
        [pltpu.VMEM((count, rows, chunk), jnp.float32), pltpu.SemaphoreType.DMA((count,))],
        out_specs=[ANY, VMEM],
        limit=40,
        flops=rows * 2 * half * 512,
        moved=6 * MIB,
        aliases=None if filled is None else {4 + len(edges): 0},
    )(offsets, taps, x4, other, *extra)


def filter_sources(offsets, taps, mine, other, powers, chips):
    length = WIN + 2 * MAXLAG
    count = length // LANE
    half = mine.shape[1] - LEFT

    def kernel(off_ref, taps_ref, mine_ref, other_ref, *refs):
        *power_refs, out_ref, energy_ref = refs
        tile = lax.axis_index("tm")
        core, chip = tile % 2, tile // 2
        mine_rows = mine_ref[...].astype(jnp.float32)
        other_rows = other_ref[...].astype(jnp.float32)
        low = jnp.where(core == 0, mine_rows, other_rows)
        high = jnp.where(core == 0, other_rows, mine_rows)
        raw = [low[:, half:], low[:, :half], high[:, :half], high[:, half : half + LANE]]
        raw = jnp.concatenate(raw, axis=1)
        blocks = [raw[:, j * LANE : (j + 1) * LANE] for j in range(count + 1)]
        before = jnp.concatenate(blocks[:-1], axis=0)
        after = jnp.concatenate(blocks[1:], axis=0)
        framed = jnp.concatenate([before, after], axis=1).astype(jnp.bfloat16)
        value = jnp.dot(framed, fir_tile(taps_ref[...]), preferred_element_type=jnp.float32)
        total = jnp.zeros((NS, LANE), jnp.float32)
        first_kept = [
            off_ref[jnp.maximum(chip - 1, 0)],
            off_ref[chip],
            off_ref[jnp.minimum(chip + 1, chips - 1)],
        ]
        for j in range(count):
            piece = value[j * NS : (j + 1) * NS, :]
            start = j * LANE - MAXLAG
            window = start // WIN
            if window == 0:
                total = total + piece * piece
            place = lax.broadcasted_iota(jnp.int32, (1, LANE), 1) + (start - window * WIN)
            keep = jnp.where(place >= first_kept[window + 1], 1.0, 0.0)
            if window < 0:
                keep = keep * jnp.where(chip > 0, 1.0, 0.0)
            if window > 0:
                keep = keep * jnp.where(chip < chips - 1, 1.0, 0.0)
            out_ref[:, j * LANE : (j + 1) * LANE] = piece * keep
        lines = []
        for r in range(power_refs[0].shape[0] // LANE):
            block = sum(ref[r * LANE : (r + 1) * LANE, :] for ref in power_refs)
            lines.append(jnp.sum(block.T, axis=0, keepdims=True))
        repeated = jnp.concatenate([total] * SHIFTS, axis=0)
        lines.append(jnp.sum(repeated.T, axis=0, keepdims=True))
        lines.append(jnp.zeros((8 - len(lines), LANE), jnp.float32))
        energy = jnp.concatenate(lines, axis=0)
        energy_ref[...] = jnp.broadcast_to(energy[None], energy_ref.shape)

    return call(
        kernel,
        "filter_sources",
        [shape((NS, length), jnp.float32), shape((chips, 8, LANE), jnp.float32)],
        [SMEM, VMEM, VMEM, VMEM] + [VMEM] * len(powers),
        moved=MIB,
    )(offsets, taps, mine, other, *powers)


def lag_block(table_ref, start, depth, pair):
    offset = start + pair * 2 * SHIFTS
    left = table_ref[offset : offset + depth, :]
    right = table_ref[offset + SHIFTS : offset + SHIFTS + depth, :]
    return jnp.concatenate([left, right], axis=1)


def split_line(value, cols, keep_ref, send_ref, half_groups):
    rows, width = value.shape
    own_low = (lax.axis_index("tm") // 2) % 2 == 0
    value = value.reshape(half_groups, 2, rows // half_groups // 2, width)
    low, high = value[:, 0], value[:, 1]
    keep_ref[:, :, cols] = jnp.where(own_low, low, high)
    send_ref[:, :, cols] = jnp.where(own_low, high, low).astype(jnp.bfloat16)


def correlate_first(energies, traces, row_blocks, pairs, half_groups, total_samples):
    block_rows, depth = row_blocks[0].shape
    parts = len(row_blocks)
    channels = block_rows * parts
    length = traces.shape[1]
    chunk = 1024
    loads = depth // chunk

    def kernel(energy_ref, traces_ref, *refs):
        row_refs = refs[:parts]
        keep_ref, send_ref, white, table, buf, total, sems = refs[parts:]
        copies = []
        for i in range(loads):
            for r, rows_ref in enumerate(row_refs):
                source = rows_ref.at[:, pl.ds(i * chunk, chunk)]
                place = buf.at[i, pl.ds(r * block_rows, block_rows)]
                copies.append(pltpu.make_async_copy(source, place, sems.at[i * parts + r]))
        for copy in copies:
            copy.start()
        energy = jnp.sum(energy_ref[...], axis=0)
        scale = lax.rsqrt(energy / total_samples + EPS)
        padded = jnp.concatenate([scale, jnp.zeros((LANE - 8, LANE), jnp.float32)], axis=0)
        turned = padded.T
        blocks = channels // LANE
        gain = jnp.concatenate([turned[:, r : r + 1] for r in range(blocks)], axis=0)
        source_gain = turned[:NS, blocks : blocks + 1]
        lane = lax.broadcasted_iota(jnp.int32, (NS, LANE), 1)

        def traces_block(j):
            if j * LANE >= length:
                return jnp.zeros((NS, LANE), jnp.float32)
            block = traces_ref[:, j * LANE : (j + 1) * LANE] * source_gain
            return block.astype(jnp.bfloat16).astype(jnp.float32)

        def build(low, high):
            for j in range(low // LANE, high // LANE):
                here, after = traces_block(j), traces_block(j + 1)
                lines = [here]
                for b in range(1, SHIFTS):
                    lines.append(pltpu.roll(jnp.where(lane < b, after, here), LANE - b, 1))
                turned_block = jnp.concatenate(lines, axis=0).T
                table[j * LANE : (j + 1) * LANE, :] = turned_block.astype(jnp.bfloat16)

        ahead = chunk + LAGS
        build(0, ahead)
        for i in range(loads):
            for copy in copies[i * parts : (i + 1) * parts]:
                copy.wait()
            span = slice(i * chunk, (i + 1) * chunk)
            white[:, span] = (buf[i] * gain).astype(jnp.bfloat16)
            if i + 1 < loads:
                build(i * chunk + ahead, min((i + 1) * chunk + ahead, length))
            for place, pair in enumerate(pairs):
                value = jnp.dot(
                    white[:, span],
                    lag_block(table, i * chunk, chunk, pair),
                    preferred_element_type=jnp.float32,
                )
                cols = slice(place * 2 * LANE, (place + 1) * 2 * LANE)
                total[:, cols] = value if i == 0 else total[:, cols] + value
        for place in range(len(pairs)):
            cols = slice(place * 2 * LANE, (place + 1) * 2 * LANE)
            split_line(total[:, cols], cols, keep_ref, send_ref, half_groups)

    sub = channels // half_groups // 2
    cols = len(pairs) * 2 * LANE
    return call(
        kernel,
        "correlate_first",
        [
            shape((half_groups, sub, cols), jnp.float32),
            shape((half_groups, sub, cols), jnp.bfloat16),
            shape((channels, depth), jnp.bfloat16),
            shape((length, LANE), jnp.bfloat16),
        ],
        [VMEM, VMEM] + [ANY] * parts,
        [
            pltpu.VMEM((loads, channels, chunk), jnp.float32),
            pltpu.VMEM((channels, len(pairs) * 2 * LANE), jnp.float32),
            pltpu.SemaphoreType.DMA((loads * parts,)),
        ],
        limit=40,
        flops=2 * channels * depth * cols,
        moved=16 * MIB,
    )(energies, traces, *row_blocks)


def correlate_next(white, table, pairs, half_groups):
    channels, depth = white.shape

    def kernel(white_ref, table_ref, keep_ref, send_ref):
        for place, pair in enumerate(pairs):
            lags = lag_block(table_ref, 0, depth, pair)
            value = jnp.dot(white_ref[...], lags, preferred_element_type=jnp.float32)
            cols = slice(place * 2 * LANE, (place + 1) * 2 * LANE)
            split_line(value, cols, keep_ref, send_ref, half_groups)

    sub = channels // half_groups // 2
    cols = len(pairs) * 2 * LANE
    return call(
        kernel,
        "correlate_next",
        [
            shape((half_groups, sub, cols), jnp.float32),
            shape((half_groups, sub, cols), jnp.bfloat16),
        ],
        [VMEM, VMEM],
        flops=2 * channels * depth * cols,
        moved=8 * MIB,
    )(white, table)


def add_line(keeps, arrivals):
    groups, sub, _ = keeps[0].shape
    widths = [keep.shape[2] for keep in keeps]
    count = len(keeps)

    def kernel(*refs):
        start = 0
        for keep_ref, across_ref, width in zip(refs[:count], refs[count : 2 * count], widths):
            value = keep_ref[...] + across_ref[...].astype(jnp.float32)
            refs[-1][:, :, start : start + width] = value.astype(jnp.bfloat16)
            start += width

    return call(
        kernel,
        "add_line",
        [shape((groups, sub, sum(widths)), jnp.bfloat16)],
        [VMEM] * (2 * count),
        moved=MIB,
    )(*keeps, *arrivals)[0]


def finish(parts, factor):
    count, sub, cols = parts.shape

    stack = LANE // sub

    def kernel(parts_ref, out_ref, turned):
        lane = lax.broadcasted_iota(jnp.int32, (sub, LANE), 1)
        value = parts_ref[0].astype(jnp.float32)
        for i in range(1, count):
            value = value + parts_ref[i].astype(jnp.float32)
        value = value * factor
        for g in range(cols // LANE // stack):
            first = g * stack
            blocks = [value[:, (first + k) * LANE : (first + k + 1) * LANE] for k in range(stack)]
            turned[...] = jnp.concatenate(blocks, axis=0).T
            by_source = [turned[pl.ds(m, SHIFTS, stride=NS), :] for m in range(NS)]
            ordered = jnp.concatenate(by_source, axis=0).T
            for m in range(NS):
                line = jnp.zeros((sub, LANE), jnp.float32)
                for k in range(stack):
                    block = ordered[k * sub : (k + 1) * sub, :]
                    moved = pltpu.roll(block, ((k - m) * SHIFTS) % LANE, 1) if k != m else block
                    line = jnp.where(lane // SHIFTS == k, moved, line)
                out_ref[:, m // SB, m % SB, g * LANE : (g + 1) * LANE] = line

    return call(
        kernel,
        "finish",
        [shape((sub, NSRC, SB, LAGS), jnp.float32)],
        [VMEM],
        [pltpu.VMEM((LANE, LANE), jnp.float32)],
        moved=MIB,
    )(parts)[0]


def shards(strain_rate, whiten_taps, source_channels, window_offsets):
    channels, samples = strain_rate.shape
    tiles = lax.axis_size("tm")
    groups_chan = lax.axis_size("chan")
    total_samples = samples * tiles
    chips = tiles // 2
    sub = channels // tiles
    taps = wide_taps(whiten_taps)

    x4 = strain_rate.reshape(chips, 2, sub, samples)
    own, edge, high, away = pick_sources(source_channels, x4)

    swap = [(i, i ^ 1) for i in range(tiles)]
    to_next = [(2 * k - 1, 2 * k) for k in range(1, chips)]
    both_next = to_next + [(b, a) for a, b in to_next]
    edge = lax.ppermute(edge, "tm", both_next)
    other = lax.ppermute(away, "tm", swap)
    high = lax.ppermute(high, "tm", [(2 * k - 1, 2 * k + 1) for k in range(1, chips)])

    piece = extend_sources(own, edge)
    parts = [
        lax.ppermute(piece, "chan", [(i, (i + 2 * d) % groups_chan) for i in range(groups_chan)])
        for d in range(1, groups_chan // 2)
    ]
    filtered, power_a = filter_rows(window_offsets, taps, x4, other, [], 1)
    *parts, power_a = lax.optimization_barrier((*parts, power_a))
    piece = add_pieces(piece, *parts)
    arrived = lax.ppermute(piece, "chan", [(i, i ^ 1) for i in range(groups_chan)])
    filtered, power_b = filter_rows(
        window_offsets, taps, x4, other, [edge, high], 0, filtered
    )
    arrived, power_b = lax.optimization_barrier((arrived, power_b))
    piece = add_pieces(piece, arrived)
    piece_other = lax.ppermute(piece, "tm", swap)
    traces, energy = filter_sources(
        window_offsets, taps, piece, piece_other, [power_a, power_b], chips
    )
    same = [[2 * k + c for k in range(chips)] for c in range(2)]
    energies = lax.all_to_all(energy, "tm", 0, 0, tiled=True, axis_index_groups=same)

    column = tiles // 4
    dots = LAGS // (2 * SHIFTS)
    splits = [range(0, dots // 4), range(dots // 4, dots * 5 // 8), range(dots * 5 // 8, dots)]
    line = [(i, i ^ 2) for i in range(tiles)]
    keep, send, white, table = correlate_first(
        energies, traces, [filtered], splits[0], column, total_samples
    )
    keeps, arrivals = [keep], [lax.ppermute(send, "tm", line)]
    for pairs in splits[1:]:
        if len(keeps) > 1:
            white, arrivals[-2] = lax.optimization_barrier((white, arrivals[-2]))
        keep, send = correlate_next(white, table, pairs, column)
        keeps.append(keep)
        arrivals.append(lax.ppermute(send, "tm", line))
    summed = add_line(keeps, arrivals)
    columns = [[4 * z + r for z in range(column)] for r in range(4)]
    parts = lax.all_to_all(summed, "tm", 0, 0, tiled=True, axis_index_groups=columns)
    return finish(parts, 1.0 / math.sqrt(total_samples))


def solution(mesh):
    return jax.shard_map(
        shards,
        mesh=mesh,
        in_specs=(P("chan", "tm"), P(), P(), P()),
        out_specs=P(("chan", "tm"), None, None, None),
        check_vma=False,
    )
```

```python
import math

import jax
import jax.numpy as jnp
from jax import lax
from jax.experimental import pallas as pl
from jax.experimental.pallas import tpu as pltpu
from jax.sharding import PartitionSpec as P

TAPS = 64
MAXLAG = 128
LAGS = 256
NSRC = 2
SB = 4
NS = NSRC * SB
WIN = 8192
LANE = 128
SHIFTS = 16
LEFT = 256
EPS = 1e-05
MIB = 1024 * 1024

VMEM = pl.BlockSpec(memory_space=pltpu.VMEM)
SMEM = pl.BlockSpec(memory_space=pltpu.SMEM)
ANY = pl.BlockSpec(memory_space=pl.ANY)


def call(
    kernel, name, out, in_specs, scratch=(), out_specs=None, limit=16, flops=0, moved=0, aliases=None
):
    return pl.pallas_call(
        kernel,
        out_shape=out,
        in_specs=in_specs,
        out_specs=out_specs or [VMEM] * len(out),
        scratch_shapes=list(scratch),
        input_output_aliases=aliases or {},
        compiler_params=pltpu.CompilerParams(vmem_limit_bytes=limit * MIB),
        cost_estimate=pl.CostEstimate(flops=flops, bytes_accessed=moved, transcendentals=0),
        name=name,
    )


def shape(dims, dtype):
    return jax.ShapeDtypeStruct(dims, dtype)


def fir_tile(taps):
    wide = jnp.broadcast_to(taps.astype(jnp.float32), (2 * LANE, 2 * LANE))
    rolled = pltpu.roll(wide, LANE, 1, stride=1, stride_axis=0)
    return rolled[:, :LANE].astype(jnp.bfloat16)


def wide_taps(taps):
    return jnp.pad(taps, (0, 2 * LANE - TAPS)).reshape(1, 2 * LANE)


def pick_sources(source_channels, x4):
    groups, _, sub, samples = x4.shape
    channels = groups * 2 * sub

    def kernel(ids_ref, x_ref, own_ref, edge_ref, high_ref, away_ref, buf, sems):
        base = lax.axis_index("chan") * channels
        core = lax.axis_index("tm") % 2
        copies = []
        inner = []
        for j in range(NS):
            local = ids_ref[j // SB, j % SB] - base
            owned = (local >= 0) & (local < channels)
            row = jnp.clip(local, 0, channels - 1)
            group, half = row // (2 * sub), (row // sub) % 2
            inner.append(jnp.where(owned, row % sub, -1))
            copies.append(pltpu.make_async_copy(x_ref.at[group, half], buf.at[j], sems.at[j]))
        last = pl.ds(samples - LANE, LANE)
        rest = [
            pltpu.make_async_copy(
                x_ref.at[:, 0, :, last], edge_ref.at[pl.ds(0, groups)], sems.at[NS]
            ),
            pltpu.make_async_copy(x_ref.at[:, 1, :, last], high_ref, sems.at[NS + 1]),
            pltpu.make_async_copy(x_ref.at[:, 1 - core], away_ref, sems.at[NS + 2]),
        ]
        for copy in copies + rest:
            copy.start()
        rows = lax.broadcasted_iota(jnp.int32, (sub, 1), 0)
        own = jnp.zeros((NS, samples), jnp.float32)
        for j in range(NS):
            copies[j].wait()
            picked = buf[j].astype(jnp.float32) * jnp.where(rows == inner[j], 1.0, 0.0)
            picked = picked[:NS] + picked[NS:]
            own = own + pltpu.roll(picked, (j + NS - inner[j] % NS) % NS, 0)
        own_ref[...] = own.astype(jnp.bfloat16)
        end = jnp.where(core == 1, own[:, samples - LEFT :], own[:, :LEFT])
        for copy in rest:
            copy.wait()
        edge_ref[groups] = jnp.concatenate(
            [end[:, :LANE], end[:, LANE:]], axis=0
        ).astype(jnp.bfloat16)

    return call(
        kernel,
        "pick_sources",
        [
            shape((NS, samples), jnp.bfloat16),
            shape((groups + 1, sub, LANE), jnp.bfloat16),
            shape((groups, sub, LANE), jnp.bfloat16),
            shape((groups, sub, samples), jnp.bfloat16),
        ],
        [SMEM, ANY],
        [pltpu.VMEM((NS, sub, samples), jnp.bfloat16), pltpu.SemaphoreType.DMA((NS + 3,))],
        limit=50,
        moved=2 * MIB,
    )(source_channels, x4)


def extend_sources(own, edge):
    samples = own.shape[1]
    groups = edge.shape[0] - 1

    def kernel(own_ref, edge_ref, out_ref):
        end = edge_ref[groups].astype(jnp.float32)
        joined = [own_ref[...].astype(jnp.float32), end[:NS], end[NS:]]
        out_ref[...] = jnp.concatenate(joined, axis=1).astype(jnp.bfloat16)

    return call(
        kernel,
        "extend_sources",
        [shape((NS, samples + LEFT), jnp.bfloat16)],
        [VMEM, VMEM],
    )(own, edge)[0]


def add_pieces(*pieces):
    def kernel(*refs):
        total = refs[0][...].astype(jnp.float32)
        for ref in refs[1:-1]:
            total = total + ref[...].astype(jnp.float32)
        refs[-1][...] = total.astype(jnp.bfloat16)

    return call(
        kernel,
        "add_pieces",
        [shape(pieces[0].shape, jnp.bfloat16)],
        [VMEM] * len(pieces),
    )(*pieces)[0]


def filter_rows(offsets, taps, x4, other, edges, part, filled=None):
    groups, _, sub, half = x4.shape
    rows = groups * sub
    chunk = 1024
    count = half // chunk
    extra = list(edges) + ([] if filled is None else [filled])

    def kernel(off_ref, taps_ref, x_ref, other_ref, *refs):
        edge_refs = refs[: len(edges)]
        out_ref, power_ref, value_buf, sems = refs[len(extra) :]
        tile = lax.axis_index("tm")
        core = tile % 2
        matrix = fir_tile(taps_ref[...])
        first_kept = off_ref[tile // 2]

        def store(index):
            place = out_ref.at[:, pl.ds(part * half + index * chunk, chunk)]
            return pltpu.make_async_copy(value_buf.at[index], place, sems.at[index])

        def run(read, previous):
            power = jnp.zeros((rows, LANE), jnp.float32)
            for index in range(count):
                for j in range(chunk // LANE):
                    first = index * chunk + j * LANE
                    current = read(slice(first, first + LANE)).reshape(rows, LANE)
                    framed = jnp.concatenate([previous, current], axis=1)
                    value = jnp.dot(framed, matrix, preferred_element_type=jnp.float32)
                    power = power + value * value
                    place = lax.broadcasted_iota(jnp.int32, (1, LANE), 1) + part * half + first
                    value = value * jnp.where(place >= first_kept, 1.0, 0.0)
                    value_buf[index, :, j * LANE : (j + 1) * LANE] = value
                    previous = current
                store(index).start()
            power_ref[...] = power

        def own(cols):
            return x_ref[:, core, :, cols]

        def swapped(cols):
            return other_ref[:, :, cols]

        last = slice(half - LANE, half)
        readers = (own, swapped)
        for index in range(2):
            low, high = readers[index], readers[1 - index]

            @pl.when(core == index)
            def _(index=index, low=low, high=high):
                if part == 1:
                    run(high, low(last).reshape(rows, LANE))
                else:
                    run(low, edge_refs[index][:groups].reshape(rows, LANE))

        for index in range(count):
            store(index).wait()

    return call(
        kernel,
        "filter_rows",
        [shape((rows, 2 * half), jnp.float32), shape((rows, LANE), jnp.float32)],
        [SMEM, VMEM, VMEM, VMEM] + [VMEM] * len(edges) + ([] if filled is None else [ANY]),
        [pltpu.VMEM((count, rows, chunk), jnp.float32), pltpu.SemaphoreType.DMA((count,))],
        out_specs=[ANY, VMEM],
        limit=40,
        flops=rows * 2 * half * 512,
        moved=6 * MIB,
        aliases=None if filled is None else {4 + len(edges): 0},
    )(offsets, taps, x4, other, *extra)


def filter_sources(offsets, taps, mine, other, powers, chips):
    length = WIN + 2 * MAXLAG
    count = length // LANE
    half = mine.shape[1] - LEFT

    def kernel(off_ref, taps_ref, mine_ref, other_ref, *refs):
        *power_refs, out_ref, energy_ref = refs
        tile = lax.axis_index("tm")
        core, chip = tile % 2, tile // 2
        mine_rows = mine_ref[...].astype(jnp.float32)
        other_rows = other_ref[...].astype(jnp.float32)
        low = jnp.where(core == 0, mine_rows, other_rows)
        high = jnp.where(core == 0, other_rows, mine_rows)
        raw = [low[:, half:], low[:, :half], high[:, :half], high[:, half : half + LANE]]
        raw = jnp.concatenate(raw, axis=1)
        blocks = [raw[:, j * LANE : (j + 1) * LANE] for j in range(count + 1)]
        before = jnp.concatenate(blocks[:-1], axis=0)
        after = jnp.concatenate(blocks[1:], axis=0)
        framed = jnp.concatenate([before, after], axis=1).astype(jnp.bfloat16)
        value = jnp.dot(framed, fir_tile(taps_ref[...]), preferred_element_type=jnp.float32)
        total = jnp.zeros((NS, LANE), jnp.float32)
        first_kept = [
            off_ref[jnp.maximum(chip - 1, 0)],
            off_ref[chip],
            off_ref[jnp.minimum(chip + 1, chips - 1)],
        ]
        for j in range(count):
            piece = value[j * NS : (j + 1) * NS, :]
            start = j * LANE - MAXLAG
            window = start // WIN
            if window == 0:
                total = total + piece * piece
            place = lax.broadcasted_iota(jnp.int32, (1, LANE), 1) + (start - window * WIN)
            keep = jnp.where(place >= first_kept[window + 1], 1.0, 0.0)
            if window < 0:
                keep = keep * jnp.where(chip > 0, 1.0, 0.0)
            if window > 0:
                keep = keep * jnp.where(chip < chips - 1, 1.0, 0.0)
            out_ref[:, j * LANE : (j + 1) * LANE] = piece * keep
        lines = []
        for r in range(power_refs[0].shape[0] // LANE):
            block = sum(ref[r * LANE : (r + 1) * LANE, :] for ref in power_refs)
            lines.append(jnp.sum(block.T, axis=0, keepdims=True))
        repeated = jnp.concatenate([total] * SHIFTS, axis=0)
        lines.append(jnp.sum(repeated.T, axis=0, keepdims=True))
        lines.append(jnp.zeros((8 - len(lines), LANE), jnp.float32))
        energy = jnp.concatenate(lines, axis=0)
        energy_ref[...] = jnp.broadcast_to(energy[None], energy_ref.shape)

    return call(
        kernel,
        "filter_sources",
        [shape((NS, length), jnp.float32), shape((chips, 8, LANE), jnp.float32)],
        [SMEM, VMEM, VMEM, VMEM] + [VMEM] * len(powers),
        moved=MIB,
    )(offsets, taps, mine, other, *powers)


def lag_block(table_ref, start, depth, pair):
    offset = start + pair * 2 * SHIFTS
    left = table_ref[offset : offset + depth, :]
    right = table_ref[offset + SHIFTS : offset + SHIFTS + depth, :]
    return jnp.concatenate([left, right], axis=1)


def split_line(value, cols, keep_ref, send_ref, half_groups):
    rows, width = value.shape
    own_low = (lax.axis_index("tm") // 2) % 2 == 0
    value = value.reshape(half_groups, 2, rows // half_groups // 2, width)
    low, high = value[:, 0], value[:, 1]
    keep_ref[:, :, cols] = jnp.where(own_low, low, high)
    send_ref[:, :, cols] = jnp.where(own_low, high, low).astype(jnp.bfloat16)


def correlate_first(energies, traces, row_blocks, pairs, half_groups, total_samples):
    block_rows, depth = row_blocks[0].shape
    parts = len(row_blocks)
    channels = block_rows * parts
    length = traces.shape[1]
    chunk = 1024
    loads = depth // chunk

    def kernel(energy_ref, traces_ref, *refs):
        row_refs = refs[:parts]
        keep_ref, send_ref, white, table, buf, total, sems = refs[parts:]
        copies = []
        for i in range(loads):
            for r, rows_ref in enumerate(row_refs):
                source = rows_ref.at[:, pl.ds(i * chunk, chunk)]
                place = buf.at[i, pl.ds(r * block_rows, block_rows)]
                copies.append(pltpu.make_async_copy(source, place, sems.at[i * parts + r]))
        for copy in copies:
            copy.start()
        energy = jnp.sum(energy_ref[...], axis=0)
        scale = lax.rsqrt(energy / total_samples + EPS)
        padded = jnp.concatenate([scale, jnp.zeros((LANE - 8, LANE), jnp.float32)], axis=0)
        turned = padded.T
        blocks = channels // LANE
        gain = jnp.concatenate([turned[:, r : r + 1] for r in range(blocks)], axis=0)
        source_gain = turned[:NS, blocks : blocks + 1]
        lane = lax.broadcasted_iota(jnp.int32, (NS, LANE), 1)

        def traces_block(j):
            if j * LANE >= length:
                return jnp.zeros((NS, LANE), jnp.float32)
            block = traces_ref[:, j * LANE : (j + 1) * LANE] * source_gain
            return block.astype(jnp.bfloat16).astype(jnp.float32)

        def build(low, high):
            for j in range(low // LANE, high // LANE):
                here, after = traces_block(j), traces_block(j + 1)
                lines = [here]
                for b in range(1, SHIFTS):
                    lines.append(pltpu.roll(jnp.where(lane < b, after, here), LANE - b, 1))
                turned_block = jnp.concatenate(lines, axis=0).T
                table[j * LANE : (j + 1) * LANE, :] = turned_block.astype(jnp.bfloat16)

        ahead = chunk + LAGS
        build(0, ahead)
        for i in range(loads):
            for copy in copies[i * parts : (i + 1) * parts]:
                copy.wait()
            span = slice(i * chunk, (i + 1) * chunk)
            white[:, span] = (buf[i] * gain).astype(jnp.bfloat16)
            if i + 1 < loads:
                build(i * chunk + ahead, min((i + 1) * chunk + ahead, length))
            for place, pair in enumerate(pairs):
                value = jnp.dot(
                    white[:, span],
                    lag_block(table, i * chunk, chunk, pair),
                    preferred_element_type=jnp.float32,
                )
                cols = slice(place * 2 * LANE, (place + 1) * 2 * LANE)
                total[:, cols] = value if i == 0 else total[:, cols] + value
        for place in range(len(pairs)):
            cols = slice(place * 2 * LANE, (place + 1) * 2 * LANE)
            split_line(total[:, cols], cols, keep_ref, send_ref, half_groups)

    sub = channels // half_groups // 2
    cols = len(pairs) * 2 * LANE
    return call(
        kernel,
        "correlate_first",
        [
            shape((half_groups, sub, cols), jnp.float32),
            shape((half_groups, sub, cols), jnp.bfloat16),
            shape((channels, depth), jnp.bfloat16),
            shape((length, LANE), jnp.bfloat16),
        ],
        [VMEM, VMEM] + [ANY] * parts,
        [
            pltpu.VMEM((loads, channels, chunk), jnp.float32),
            pltpu.VMEM((channels, len(pairs) * 2 * LANE), jnp.float32),
            pltpu.SemaphoreType.DMA((loads * parts,)),
        ],
        limit=40,
        flops=2 * channels * depth * cols,
        moved=16 * MIB,
    )(energies, traces, *row_blocks)


def correlate_next(white, table, pairs, half_groups):
    channels, depth = white.shape

    def kernel(white_ref, table_ref, keep_ref, send_ref):
        for place, pair in enumerate(pairs):
            lags = lag_block(table_ref, 0, depth, pair)
            value = jnp.dot(white_ref[...], lags, preferred_element_type=jnp.float32)
            cols = slice(place * 2 * LANE, (place + 1) * 2 * LANE)
            split_line(value, cols, keep_ref, send_ref, half_groups)

    sub = channels // half_groups // 2
    cols = len(pairs) * 2 * LANE
    return call(
        kernel,
        "correlate_next",
        [
            shape((half_groups, sub, cols), jnp.float32),
            shape((half_groups, sub, cols), jnp.bfloat16),
        ],
        [VMEM, VMEM],
        flops=2 * channels * depth * cols,
        moved=8 * MIB,
    )(white, table)


def add_line(keeps, arrivals):
    groups, sub, _ = keeps[0].shape
    widths = [keep.shape[2] for keep in keeps]
    count = len(keeps)

    def kernel(*refs):
        start = 0
        for keep_ref, across_ref, width in zip(refs[:count], refs[count : 2 * count], widths):
            value = keep_ref[...] + across_ref[...].astype(jnp.float32)
            refs[-1][:, :, start : start + width] = value.astype(jnp.bfloat16)
            start += width

    return call(
        kernel,
        "add_line",
        [shape((groups, sub, sum(widths)), jnp.bfloat16)],
        [VMEM] * (2 * count),
        moved=MIB,
    )(*keeps, *arrivals)[0]


def finish(parts, factor):
    count, sub, cols = parts.shape

    stack = LANE // sub

    def kernel(parts_ref, out_ref, turned):
        lane = lax.broadcasted_iota(jnp.int32, (sub, LANE), 1)
        value = parts_ref[0].astype(jnp.float32)
        for i in range(1, count):
            value = value + parts_ref[i].astype(jnp.float32)
        value = value * factor
        for g in range(cols // LANE // stack):
            first = g * stack
            blocks = [value[:, (first + k) * LANE : (first + k + 1) * LANE] for k in range(stack)]
            turned[...] = jnp.concatenate(blocks, axis=0).T
            by_source = [turned[pl.ds(m, SHIFTS, stride=NS), :] for m in range(NS)]
            ordered = jnp.concatenate(by_source, axis=0).T
            for m in range(NS):
                line = jnp.zeros((sub, LANE), jnp.float32)
                for k in range(stack):
                    block = ordered[k * sub : (k + 1) * sub, :]
                    moved = pltpu.roll(block, ((k - m) * SHIFTS) % LANE, 1) if k != m else block
                    line = jnp.where(lane // SHIFTS == k, moved, line)
                out_ref[:, m // SB, m % SB, g * LANE : (g + 1) * LANE] = line

    return call(
        kernel,
        "finish",
        [shape((sub, NSRC, SB, LAGS), jnp.float32)],
        [VMEM],
        [pltpu.VMEM((LANE, LANE), jnp.float32)],
        moved=MIB,
    )(parts)[0]


def shards(strain_rate, whiten_taps, source_channels, window_offsets):
    channels, samples = strain_rate.shape
    tiles = lax.axis_size("tm")
    groups_chan = lax.axis_size("chan")
    total_samples = samples * tiles
    chips = tiles // 2
    sub = channels // tiles
    taps = wide_taps(whiten_taps)

    x4 = strain_rate.reshape(chips, 2, sub, samples)
    own, edge, high, away = pick_sources(source_channels, x4)

    swap = [(i, i ^ 1) for i in range(tiles)]
    to_next = [(2 * k - 1, 2 * k) for k in range(1, chips)]
    both_next = to_next + [(b, a) for a, b in to_next]
    edge = lax.ppermute(edge, "tm", both_next)
    edge, away = lax.optimization_barrier((edge, away))
    other = lax.ppermute(away, "tm", swap)
    high = lax.ppermute(high, "tm", [(2 * k - 1, 2 * k + 1) for k in range(1, chips)])

    piece = extend_sources(own, edge)
    parts = [
        lax.ppermute(piece, "chan", [(i, (i + 2 * d) % groups_chan) for i in range(groups_chan)])
        for d in range(1, groups_chan // 2)
    ]
    filtered, power_a = filter_rows(window_offsets, taps, x4, other, [], 1)
    *parts, power_a = lax.optimization_barrier((*parts, power_a))
    piece = add_pieces(piece, *parts)
    arrived = lax.ppermute(piece, "chan", [(i, i ^ 1) for i in range(groups_chan)])
    filtered, power_b = filter_rows(
        window_offsets, taps, x4, other, [edge, high], 0, filtered
    )
    arrived, power_b = lax.optimization_barrier((arrived, power_b))
    piece = add_pieces(piece, arrived)
    piece_other = lax.ppermute(piece, "tm", swap)
    traces, energy = filter_sources(
        window_offsets, taps, piece, piece_other, [power_a, power_b], chips
    )
    same = [[2 * k + c for k in range(chips)] for c in range(2)]
    energies = lax.all_to_all(energy, "tm", 0, 0, tiled=True, axis_index_groups=same)

    column = tiles // 4
    dots = LAGS // (2 * SHIFTS)
    splits = [range(0, dots // 4), range(dots // 4, dots * 5 // 8), range(dots * 5 // 8, dots)]
    line = [(i, i ^ 2) for i in range(tiles)]
    keep, send, white, table = correlate_first(
        energies, traces, [filtered], splits[0], column, total_samples
    )
    keeps, arrivals = [keep], [lax.ppermute(send, "tm", line)]
    for pairs in splits[1:]:
        if len(keeps) > 1:
            white, arrivals[-2] = lax.optimization_barrier((white, arrivals[-2]))
        keep, send = correlate_next(white, table, pairs, column)
        keeps.append(keep)
        arrivals.append(lax.ppermute(send, "tm", line))
    summed = add_line(keeps, arrivals)
    columns = [[4 * z + r for z in range(column)] for r in range(4)]
    parts = lax.all_to_all(summed, "tm", 0, 0, tiled=True, axis_index_groups=columns)
    return finish(parts, 1.0 / math.sqrt(total_samples))


def solution(mesh):
    return jax.shard_map(
        shards,
        mesh=mesh,
        in_specs=(P("chan", "tm"), P(), P(), P()),
        out_specs=P(("chan", "tm"), None, None, None),
        check_vma=False,
    )
```

```python
import math

import jax
import jax.numpy as jnp
from jax import lax
from jax.experimental import pallas as pl
from jax.experimental.pallas import tpu as pltpu
from jax.sharding import PartitionSpec as P

TAPS = 64
MAXLAG = 128
LAGS = 256
NSRC = 2
SB = 4
NS = NSRC * SB
WIN = 8192
LANE = 128
SHIFTS = 16
LEFT = 256
EPS = 1e-05
MIB = 1024 * 1024

VMEM = pl.BlockSpec(memory_space=pltpu.VMEM)
SMEM = pl.BlockSpec(memory_space=pltpu.SMEM)
ANY = pl.BlockSpec(memory_space=pl.ANY)


def call(
    kernel, name, out, in_specs, scratch=(), out_specs=None, limit=16, flops=0, moved=0, aliases=None
):
    return pl.pallas_call(
        kernel,
        out_shape=out,
        in_specs=in_specs,
        out_specs=out_specs or [VMEM] * len(out),
        scratch_shapes=list(scratch),
        input_output_aliases=aliases or {},
        compiler_params=pltpu.CompilerParams(vmem_limit_bytes=limit * MIB),
        cost_estimate=pl.CostEstimate(flops=flops, bytes_accessed=moved, transcendentals=0),
        name=name,
    )


def shape(dims, dtype):
    return jax.ShapeDtypeStruct(dims, dtype)


def fir_tile(taps):
    wide = jnp.broadcast_to(taps.astype(jnp.float32), (2 * LANE, 2 * LANE))
    rolled = pltpu.roll(wide, LANE, 1, stride=1, stride_axis=0)
    return rolled[:, :LANE].astype(jnp.bfloat16)


def wide_taps(taps):
    return jnp.pad(taps, (0, 2 * LANE - TAPS)).reshape(1, 2 * LANE)


def pick_sources(source_channels, x4):
    groups, _, sub, samples = x4.shape
    channels = groups * 2 * sub

    def kernel(ids_ref, x_ref, own_ref, edge_ref, high_ref, away_ref, buf, sems):
        base = lax.axis_index("chan") * channels
        core = lax.axis_index("tm") % 2
        copies = []
        inner = []
        for j in range(NS):
            local = ids_ref[j // SB, j % SB] - base
            owned = (local >= 0) & (local < channels)
            row = jnp.clip(local, 0, channels - 1)
            group, half = row // (2 * sub), (row // sub) % 2
            inner.append(jnp.where(owned, row % sub, -1))
            copies.append(pltpu.make_async_copy(x_ref.at[group, half], buf.at[j], sems.at[j]))
        last = pl.ds(samples - LANE, LANE)
        rest = [
            pltpu.make_async_copy(
                x_ref.at[:, 0, :, last], edge_ref.at[pl.ds(0, groups)], sems.at[NS]
            ),
            pltpu.make_async_copy(x_ref.at[:, 1, :, last], high_ref, sems.at[NS + 1]),
            pltpu.make_async_copy(x_ref.at[:, 1 - core], away_ref, sems.at[NS + 2]),
        ]
        for copy in copies + rest:
            copy.start()
        rows = lax.broadcasted_iota(jnp.int32, (sub, 1), 0)
        own = jnp.zeros((NS, samples), jnp.float32)
        for j in range(NS):
            copies[j].wait()
            picked = buf[j].astype(jnp.float32) * jnp.where(rows == inner[j], 1.0, 0.0)
            picked = picked[:NS] + picked[NS:]
            own = own + pltpu.roll(picked, (j + NS - inner[j] % NS) % NS, 0)
        own_ref[...] = own.astype(jnp.bfloat16)
        end = jnp.where(core == 1, own[:, samples - LEFT :], own[:, :LEFT])
        for copy in rest:
            copy.wait()
        edge_ref[groups] = jnp.concatenate(
            [end[:, :LANE], end[:, LANE:]], axis=0
        ).astype(jnp.bfloat16)

    return call(
        kernel,
        "pick_sources",
        [
            shape((NS, samples), jnp.bfloat16),
            shape((groups + 1, sub, LANE), jnp.bfloat16),
            shape((groups, sub, LANE), jnp.bfloat16),
            shape((groups, sub, samples), jnp.bfloat16),
        ],
        [SMEM, ANY],
        [pltpu.VMEM((NS, sub, samples), jnp.bfloat16), pltpu.SemaphoreType.DMA((NS + 3,))],
        limit=50,
        moved=2 * MIB,
    )(source_channels, x4)


def extend_sources(own, edge):
    samples = own.shape[1]
    groups = edge.shape[0] - 1

    def kernel(own_ref, edge_ref, out_ref):
        end = edge_ref[groups].astype(jnp.float32)
        joined = [own_ref[...].astype(jnp.float32), end[:NS], end[NS:]]
        out_ref[...] = jnp.concatenate(joined, axis=1).astype(jnp.bfloat16)

    return call(
        kernel,
        "extend_sources",
        [shape((NS, samples + LEFT), jnp.bfloat16)],
        [VMEM, VMEM],
    )(own, edge)[0]


def add_pieces(*pieces):
    def kernel(*refs):
        total = refs[0][...].astype(jnp.float32)
        for ref in refs[1:-1]:
            total = total + ref[...].astype(jnp.float32)
        refs[-1][...] = total.astype(jnp.bfloat16)

    return call(
        kernel,
        "add_pieces",
        [shape(pieces[0].shape, jnp.bfloat16)],
        [VMEM] * len(pieces),
    )(*pieces)[0]


def filter_rows(offsets, taps, x4, other, edges, part, filled=None):
    groups, _, sub, half = x4.shape
    rows = groups * sub
    chunk = 512
    count = half // chunk
    extra = list(edges) + ([] if filled is None else [filled])

    def kernel(off_ref, taps_ref, x_ref, other_ref, *refs):
        edge_refs = refs[: len(edges)]
        out_ref, power_ref, value_buf, sems = refs[len(extra) :]
        tile = lax.axis_index("tm")
        core = tile % 2
        matrix = fir_tile(taps_ref[...])
        first_kept = off_ref[tile // 2]

        def store(index):
            place = out_ref.at[:, pl.ds(part * half + index * chunk, chunk)]
            return pltpu.make_async_copy(value_buf.at[index], place, sems.at[index])

        def run(read, previous):
            power = jnp.zeros((rows, LANE), jnp.float32)
            for index in range(count):
                for j in range(chunk // LANE):
                    first = index * chunk + j * LANE
                    current = read(slice(first, first + LANE)).reshape(rows, LANE)
                    framed = jnp.concatenate([previous, current], axis=1)
                    value = jnp.dot(framed, matrix, preferred_element_type=jnp.float32)
                    power = power + value * value
                    place = lax.broadcasted_iota(jnp.int32, (1, LANE), 1) + part * half + first
                    value = value * jnp.where(place >= first_kept, 1.0, 0.0)
                    value_buf[index, :, j * LANE : (j + 1) * LANE] = value
                    previous = current
                store(index).start()
            power_ref[...] = power

        def own(cols):
            return x_ref[:, core, :, cols]

        def swapped(cols):
            return other_ref[:, :, cols]

        last = slice(half - LANE, half)
        readers = (own, swapped)
        for index in range(2):
            low, high = readers[index], readers[1 - index]

            @pl.when(core == index)
            def _(index=index, low=low, high=high):
                if part == 1:
                    run(high, low(last).reshape(rows, LANE))
                else:
                    run(low, edge_refs[index][:groups].reshape(rows, LANE))

        for index in range(count):
            store(index).wait()

    return call(
        kernel,
        "filter_rows",
        [shape((rows, 2 * half), jnp.float32), shape((rows, LANE), jnp.float32)],
        [SMEM, VMEM, VMEM, VMEM] + [VMEM] * len(edges) + ([] if filled is None else [ANY]),
        [pltpu.VMEM((count, rows, chunk), jnp.float32), pltpu.SemaphoreType.DMA((count,))],
        out_specs=[ANY, VMEM],
        limit=40,
        flops=rows * 2 * half * 512,
        moved=6 * MIB,
        aliases=None if filled is None else {4 + len(edges): 0},
    )(offsets, taps, x4, other, *extra)


def filter_sources(offsets, taps, mine, other, powers, chips):
    length = WIN + 2 * MAXLAG
    count = length // LANE
    half = mine.shape[1] - LEFT

    def kernel(off_ref, taps_ref, mine_ref, other_ref, *refs):
        *power_refs, out_ref, energy_ref = refs
        tile = lax.axis_index("tm")
        core, chip = tile % 2, tile // 2
        mine_rows = mine_ref[...].astype(jnp.float32)
        other_rows = other_ref[...].astype(jnp.float32)
        low = jnp.where(core == 0, mine_rows, other_rows)
        high = jnp.where(core == 0, other_rows, mine_rows)
        raw = [low[:, half:], low[:, :half], high[:, :half], high[:, half : half + LANE]]
        raw = jnp.concatenate(raw, axis=1)
        blocks = [raw[:, j * LANE : (j + 1) * LANE] for j in range(count + 1)]
        before = jnp.concatenate(blocks[:-1], axis=0)
        after = jnp.concatenate(blocks[1:], axis=0)
        framed = jnp.concatenate([before, after], axis=1).astype(jnp.bfloat16)
        value = jnp.dot(framed, fir_tile(taps_ref[...]), preferred_element_type=jnp.float32)
        total = jnp.zeros((NS, LANE), jnp.float32)
        first_kept = [
            off_ref[jnp.maximum(chip - 1, 0)],
            off_ref[chip],
            off_ref[jnp.minimum(chip + 1, chips - 1)],
        ]
        for j in range(count):
            piece = value[j * NS : (j + 1) * NS, :]
            start = j * LANE - MAXLAG
            window = start // WIN
            if window == 0:
                total = total + piece * piece
            place = lax.broadcasted_iota(jnp.int32, (1, LANE), 1) + (start - window * WIN)
            keep = jnp.where(place >= first_kept[window + 1], 1.0, 0.0)
            if window < 0:
                keep = keep * jnp.where(chip > 0, 1.0, 0.0)
            if window > 0:
                keep = keep * jnp.where(chip < chips - 1, 1.0, 0.0)
            out_ref[:, j * LANE : (j + 1) * LANE] = piece * keep
        lines = []
        for r in range(power_refs[0].shape[0] // LANE):
            block = sum(ref[r * LANE : (r + 1) * LANE, :] for ref in power_refs)
            lines.append(jnp.sum(block.T, axis=0, keepdims=True))
        repeated = jnp.concatenate([total] * SHIFTS, axis=0)
        lines.append(jnp.sum(repeated.T, axis=0, keepdims=True))
        lines.append(jnp.zeros((8 - len(lines), LANE), jnp.float32))
        energy = jnp.concatenate(lines, axis=0)
        energy_ref[...] = jnp.broadcast_to(energy[None], energy_ref.shape)

    return call(
        kernel,
        "filter_sources",
        [shape((NS, length), jnp.float32), shape((chips, 8, LANE), jnp.float32)],
        [SMEM, VMEM, VMEM, VMEM] + [VMEM] * len(powers),
        moved=MIB,
    )(offsets, taps, mine, other, *powers)


def lag_block(table_ref, start, depth, pair):
    offset = start + pair * 2 * SHIFTS
    left = table_ref[offset : offset + depth, :]
    right = table_ref[offset + SHIFTS : offset + SHIFTS + depth, :]
    return jnp.concatenate([left, right], axis=1)


def split_line(value, cols, keep_ref, send_ref, half_groups):
    rows, width = value.shape
    own_low = (lax.axis_index("tm") // 2) % 2 == 0
    value = value.reshape(half_groups, 2, rows // half_groups // 2, width)
    low, high = value[:, 0], value[:, 1]
    keep_ref[:, :, cols] = jnp.where(own_low, low, high)
    send_ref[:, :, cols] = jnp.where(own_low, high, low).astype(jnp.bfloat16)


def correlate_first(energies, traces, row_blocks, pairs, half_groups, total_samples):
    block_rows, depth = row_blocks[0].shape
    parts = len(row_blocks)
    channels = block_rows * parts
    length = traces.shape[1]
    chunk = 1024
    loads = depth // chunk

    def kernel(energy_ref, traces_ref, *refs):
        row_refs = refs[:parts]
        keep_ref, send_ref, white, table, buf, total, sems = refs[parts:]
        copies = []
        for i in range(loads):
            for r, rows_ref in enumerate(row_refs):
                source = rows_ref.at[:, pl.ds(i * chunk, chunk)]
                place = buf.at[i, pl.ds(r * block_rows, block_rows)]
                copies.append(pltpu.make_async_copy(source, place, sems.at[i * parts + r]))
        for copy in copies:
            copy.start()
        energy = jnp.sum(energy_ref[...], axis=0)
        scale = lax.rsqrt(energy / total_samples + EPS)
        padded = jnp.concatenate([scale, jnp.zeros((LANE - 8, LANE), jnp.float32)], axis=0)
        turned = padded.T
        blocks = channels // LANE
        gain = jnp.concatenate([turned[:, r : r + 1] for r in range(blocks)], axis=0)
        source_gain = turned[:NS, blocks : blocks + 1]
        lane = lax.broadcasted_iota(jnp.int32, (NS, LANE), 1)

        def traces_block(j):
            if j * LANE >= length:
                return jnp.zeros((NS, LANE), jnp.float32)
            block = traces_ref[:, j * LANE : (j + 1) * LANE] * source_gain
            return block.astype(jnp.bfloat16).astype(jnp.float32)

        def build(low, high):
            for j in range(low // LANE, high // LANE):
                here, after = traces_block(j), traces_block(j + 1)
                lines = [here]
                for b in range(1, SHIFTS):
                    lines.append(pltpu.roll(jnp.where(lane < b, after, here), LANE - b, 1))
                turned_block = jnp.concatenate(lines, axis=0).T
                table[j * LANE : (j + 1) * LANE, :] = turned_block.astype(jnp.bfloat16)

        ahead = chunk + LAGS
        build(0, ahead)
        for i in range(loads):
            for copy in copies[i * parts : (i + 1) * parts]:
                copy.wait()
            span = slice(i * chunk, (i + 1) * chunk)
            white[:, span] = (buf[i] * gain).astype(jnp.bfloat16)
            if i + 1 < loads:
                build(i * chunk + ahead, min((i + 1) * chunk + ahead, length))
            for place, pair in enumerate(pairs):
                value = jnp.dot(
                    white[:, span],
                    lag_block(table, i * chunk, chunk, pair),
                    preferred_element_type=jnp.float32,
                )
                cols = slice(place * 2 * LANE, (place + 1) * 2 * LANE)
                total[:, cols] = value if i == 0 else total[:, cols] + value
        for place in range(len(pairs)):
            cols = slice(place * 2 * LANE, (place + 1) * 2 * LANE)
            split_line(total[:, cols], cols, keep_ref, send_ref, half_groups)

    sub = channels // half_groups // 2
    cols = len(pairs) * 2 * LANE
    return call(
        kernel,
        "correlate_first",
        [
            shape((half_groups, sub, cols), jnp.float32),
            shape((half_groups, sub, cols), jnp.bfloat16),
            shape((channels, depth), jnp.bfloat16),
            shape((length, LANE), jnp.bfloat16),
        ],
        [VMEM, VMEM] + [ANY] * parts,
        [
            pltpu.VMEM((loads, channels, chunk), jnp.float32),
            pltpu.VMEM((channels, len(pairs) * 2 * LANE), jnp.float32),
            pltpu.SemaphoreType.DMA((loads * parts,)),
        ],
        limit=40,
        flops=2 * channels * depth * cols,
        moved=16 * MIB,
    )(energies, traces, *row_blocks)


def correlate_next(white, table, pairs, half_groups):
    channels, depth = white.shape

    def kernel(white_ref, table_ref, keep_ref, send_ref):
        for place, pair in enumerate(pairs):
            lags = lag_block(table_ref, 0, depth, pair)
            value = jnp.dot(white_ref[...], lags, preferred_element_type=jnp.float32)
            cols = slice(place * 2 * LANE, (place + 1) * 2 * LANE)
            split_line(value, cols, keep_ref, send_ref, half_groups)

    sub = channels // half_groups // 2
    cols = len(pairs) * 2 * LANE
    return call(
        kernel,
        "correlate_next",
        [
            shape((half_groups, sub, cols), jnp.float32),
            shape((half_groups, sub, cols), jnp.bfloat16),
        ],
        [VMEM, VMEM],
        flops=2 * channels * depth * cols,
        moved=8 * MIB,
    )(white, table)


def add_line(keeps, arrivals):
    groups, sub, _ = keeps[0].shape
    widths = [keep.shape[2] for keep in keeps]
    count = len(keeps)

    def kernel(*refs):
        start = 0
        for keep_ref, across_ref, width in zip(refs[:count], refs[count : 2 * count], widths):
            value = keep_ref[...] + across_ref[...].astype(jnp.float32)
            refs[-1][:, :, start : start + width] = value.astype(jnp.bfloat16)
            start += width

    return call(
        kernel,
        "add_line",
        [shape((groups, sub, sum(widths)), jnp.bfloat16)],
        [VMEM] * (2 * count),
        moved=MIB,
    )(*keeps, *arrivals)[0]


def finish(parts, factor):
    count, sub, cols = parts.shape

    stack = LANE // sub

    def kernel(parts_ref, out_ref, turned):
        lane = lax.broadcasted_iota(jnp.int32, (sub, LANE), 1)
        value = parts_ref[0].astype(jnp.float32)
        for i in range(1, count):
            value = value + parts_ref[i].astype(jnp.float32)
        value = value * factor
        for g in range(cols // LANE // stack):
            first = g * stack
            blocks = [value[:, (first + k) * LANE : (first + k + 1) * LANE] for k in range(stack)]
            turned[...] = jnp.concatenate(blocks, axis=0).T
            by_source = [turned[pl.ds(m, SHIFTS, stride=NS), :] for m in range(NS)]
            ordered = jnp.concatenate(by_source, axis=0).T
            for m in range(NS):
                line = jnp.zeros((sub, LANE), jnp.float32)
                for k in range(stack):
                    block = ordered[k * sub : (k + 1) * sub, :]
                    moved = pltpu.roll(block, ((k - m) * SHIFTS) % LANE, 1) if k != m else block
                    line = jnp.where(lane // SHIFTS == k, moved, line)
                out_ref[:, m // SB, m % SB, g * LANE : (g + 1) * LANE] = line

    return call(
        kernel,
        "finish",
        [shape((sub, NSRC, SB, LAGS), jnp.float32)],
        [VMEM],
        [pltpu.VMEM((LANE, LANE), jnp.float32)],
        moved=MIB,
    )(parts)[0]


def shards(strain_rate, whiten_taps, source_channels, window_offsets):
    channels, samples = strain_rate.shape
    tiles = lax.axis_size("tm")
    groups_chan = lax.axis_size("chan")
    total_samples = samples * tiles
    chips = tiles // 2
    sub = channels // tiles
    taps = wide_taps(whiten_taps)

    x4 = strain_rate.reshape(chips, 2, sub, samples)
    own, edge, high, away = pick_sources(source_channels, x4)

    swap = [(i, i ^ 1) for i in range(tiles)]
    to_next = [(2 * k - 1, 2 * k) for k in range(1, chips)]
    both_next = to_next + [(b, a) for a, b in to_next]
    edge = lax.ppermute(edge, "tm", both_next)
    other = lax.ppermute(away, "tm", swap)
    high = lax.ppermute(high, "tm", [(2 * k - 1, 2 * k + 1) for k in range(1, chips)])

    piece = extend_sources(own, edge)
    parts = [
        lax.ppermute(piece, "chan", [(i, (i + 2 * d) % groups_chan) for i in range(groups_chan)])
        for d in range(1, groups_chan // 2)
    ]
    filtered, power_a = filter_rows(window_offsets, taps, x4, other, [], 1)
    *parts, power_a = lax.optimization_barrier((*parts, power_a))
    piece = add_pieces(piece, *parts)
    arrived = lax.ppermute(piece, "chan", [(i, i ^ 1) for i in range(groups_chan)])
    filtered, power_b = filter_rows(
        window_offsets, taps, x4, other, [edge, high], 0, filtered
    )
    arrived, power_b = lax.optimization_barrier((arrived, power_b))
    piece = add_pieces(piece, arrived)
    piece_other = lax.ppermute(piece, "tm", swap)
    traces, energy = filter_sources(
        window_offsets, taps, piece, piece_other, [power_a, power_b], chips
    )
    same = [[2 * k + c for k in range(chips)] for c in range(2)]
    energies = lax.all_to_all(energy, "tm", 0, 0, tiled=True, axis_index_groups=same)

    column = tiles // 4
    dots = LAGS // (2 * SHIFTS)
    splits = [range(0, dots // 4), range(dots // 4, dots * 5 // 8), range(dots * 5 // 8, dots)]
    line = [(i, i ^ 2) for i in range(tiles)]
    keep, send, white, table = correlate_first(
        energies, traces, [filtered], splits[0], column, total_samples
    )
    keeps, arrivals = [keep], [lax.ppermute(send, "tm", line)]
    for pairs in splits[1:]:
        if len(keeps) > 1:
            white, arrivals[-2] = lax.optimization_barrier((white, arrivals[-2]))
        keep, send = correlate_next(white, table, pairs, column)
        keeps.append(keep)
        arrivals.append(lax.ppermute(send, "tm", line))
    summed = add_line(keeps, arrivals)
    columns = [[4 * z + r for z in range(column)] for r in range(4)]
    parts = lax.all_to_all(summed, "tm", 0, 0, tiled=True, axis_index_groups=columns)
    return finish(parts, 1.0 / math.sqrt(total_samples))


def solution(mesh):
    return jax.shard_map(
        shards,
        mesh=mesh,
        in_specs=(P("chan", "tm"), P(), P(), P()),
        out_specs=P(("chan", "tm"), None, None, None),
        check_vma=False,
    )
```
